32 devices in a mesh: clus: 16 (over z, y, x), samp: 2 (over core).
Axes of the slice: x: 2, y: 2, z: 4, core: 2. Of those that a mesh axis runs over, the one named last changes fastest.
Arguments:
- child_patterns: float32 [512, 2, 6, 512], P('clus', None, 'samp'), may hold values from -6 to 6
- theta_weights: float32 [6, 9], replicated, may hold values from -0.4 to 0.6
- phi_stencil: int32 [1024, 6], replicated, may hold values from 0 to 511, as said below
- phi_weights: float32 [1024, 6], replicated, may hold values from -0.3 to 0.7
- shift_phase: float32 [8, 12, 1024], P(None, 'samp'), may hold values from -3.140625 to 3.140625
- translation_table: float32 [16, 2, 12, 1024], P(None, None, 'samp', 'clus'), may hold values from -1.25 to 1.25
- far_list: int32 [64, 12], replicated, may hold values from 0 to 63, as said below
- far_vector: int32 [64, 12], replicated, may hold values from 0 to 15
Outputs:
- parent_incoming: float32 [64, 2, 12, 1024], P('clus', None, 'samp')
- child_incoming: float32 [512, 2, 6, 512], P('clus', None, 'samp')
The draws below stay inside these ranges and needn't reach their ends.
Inputs may be any that keep to these rules, and one draw needn't show every extreme that they name: `far_list`: row i names 12 different parent clusters, never i itself. `phi_stencil`: row n names 6 cyclically consecutive child columns starting at n // 2 - 6 // 2 + 1 or one column later.
All inputs are finite; a program needn't handle non-finite values.
Results may differ from the reference program's by a relative error of at most 0.00007.
Values sent between devices are 32-bit elements; how exact they have to be, the bound alone decides.
No kernel may reach another device: no remote copies, remote signals or barrier semaphores. Data moves between devices by JAX's collectives and lax.ppermute only.
A program may use at most 128 MiB of HBM per device.

```python
import jax
import jax.numpy as jnp
from jax import lax

TR_DEV = 6
NPH = 1024
NPC = 512
P_SIZE = 6
L = 12
NV = 16
NCL = 64
NCH = 512
TR = 12
TRC = 6


def draw_far_list(key, part):
    keys = jax.random.split(jax.random.fold_in(key, 11), NCL)

    def single(row_key):
        return jax.random.permutation(row_key, NCL - 1)[:L]
    offsets = jax.vmap(single)(keys).astype(jnp.int32)
    owners = jnp.arange(NCL, dtype=jnp.int32)[:, None]
    return ((owners + 1 + offsets) % NCL).astype(jnp.int32)


def draw_phi_stencil(key, part):
    columns = jnp.arange(NPH, dtype=jnp.int32)
    extra = jax.random.randint(jax.random.fold_in(key, 23), (NPH,), 0, 2).astype(jnp.int32)
    start = columns // 2 - P_SIZE // 2 + 1 + extra
    points = jnp.arange(P_SIZE, dtype=jnp.int32)
    return ((start[:, None] + points[None, :]) % NPC).astype(jnp.int32)


def set_ends(result, own_key, smallest, high):
    dims = result.shape
    place = [jax.random.randint(jax.random.fold_in(own_key, axis), (), 0, dims[axis]) for axis in range(len(dims))]
    result = result.at[tuple(place)].set(smallest)
    longest = dims.index(max(dims))
    place[longest] = (place[longest] + 1) % dims[longest]
    return result.at[tuple(place)].set(high)


def levels(rng, extent, cuts, smallest, top_value):
    loudness, own = 1.0, jax.random.fold_in(rng, 6)
    for position, shards_of in cuts:
        heights = jnp.exp(jax.random.uniform(jax.random.fold_in(own, position), (shards_of,), jnp.float32, smallest / len(cuts), top_value / len(cuts)))
        loudness = loudness * jnp.repeat(heights, extent[position] // shards_of).reshape([-1 if axis == position else 1 for axis in range(len(extent))])
    return loudness


def normal_values(rng, extent, scale, limit, shards=(), kind=jnp.bfloat16):
    gain = levels(rng, extent, shards, -0.22, 0.18) if shards else 1.0
    result = jax.random.normal(rng, extent, jnp.float32) * scale * gain
    return jnp.minimum(jnp.maximum(result, -limit), limit).astype(kind)


def setup_inputs(seed: int = 0) -> dict:
    splits = jax.random.split(jax.random.key(seed), 9)
    return {
        "child_patterns": normal_values(splits[0], (NCH, 2, TRC, NPC), 1.0, 6.0, ((0, 16), (2, 2)), jnp.float32),
        "theta_weights": jnp.clip(jax.random.uniform(splits[1], (TR_DEV, TR_DEV // 2 + P_SIZE), jnp.float32, -0.4, 0.6), -0.4, 0.6),
        "phi_stencil": draw_phi_stencil(jax.random.fold_in(splits[8], 71), 0),
        "phi_weights": jnp.clip(jax.random.uniform(splits[3], (NPH, P_SIZE), jnp.float32, -0.3, 0.7), -0.3, 0.7),
        "shift_phase": jnp.clip(jax.random.uniform(splits[4], (8, TR, NPH), jnp.float32, -3.140625, 3.140625), -3.140625, 3.140625),
        "translation_table": normal_values(splits[5], (NV, 2, TR, NPH), (2 * L) ** -0.5, 1.25, ((2, 2), (3, 16)), jnp.float32),
        "far_list": draw_far_list(jax.random.fold_in(splits[8], 71), 0),
        "far_vector": set_ends(jax.random.randint(splits[7], (NCL, L), 0, NV), jax.random.fold_in(splits[7], 1), 0, NV - 1).astype(jnp.int32),
    }


def phi_table(phi_stencil, phi_weights):
    positions = jnp.arange(NPC, dtype=jnp.int32)
    total = jnp.zeros((NPC, NPH), jnp.float32)
    for point in range(P_SIZE):
        hits = (phi_stencil[None, :, point] == positions[:, None]).astype(jnp.float32)
        total = total + hits * phi_weights[None, :, point]
    return total


def theta_table(theta_weights):
    rows = jnp.arange(TR, dtype=jnp.int32)
    owner = rows // TR_DEV
    local = rows % TR_DEV
    child_rows = jnp.arange(TRC, dtype=jnp.int32)
    total = jnp.zeros((TR, TRC), jnp.float32)
    for point in range(TR_DEV // 2 + P_SIZE):
        target = (owner * (TR_DEV // 2) - P_SIZE // 2 + point) % TRC
        hits = (target[:, None] == child_rows[None, :]).astype(jnp.float32)
        total = total + hits * theta_weights[local, point][:, None]
    return total


def reference(child_patterns, theta_weights, phi_stencil, phi_weights, shift_phase, translation_table, far_list, far_vector):
    highest = lax.Precision.HIGHEST
    phi_matrix = phi_table(phi_stencil, phi_weights)
    theta_matrix = theta_table(theta_weights)
    cosine = jnp.cos(shift_phase)
    sine = jnp.sin(shift_phase)

    def aggregate(family):
        spread = jnp.einsum("cqtp,pn->cqtn", family, phi_matrix, precision=highest)
        refined = jnp.einsum("rt,cqtn->cqrn", theta_matrix, spread, precision=highest)
        real_part = refined[:, 0] * cosine - refined[:, 1] * sine
        imag_part = refined[:, 0] * sine + refined[:, 1] * cosine
        return jnp.stack([jnp.sum(real_part, axis=0), jnp.sum(imag_part, axis=0)], axis=0)

    outgoing = lax.map(aggregate, child_patterns.reshape(NCL, 8, 2, TRC, NPC))

    def translate(entry):
        far_ids, vec_ids = entry
        source = outgoing[far_ids]
        operator = translation_table[vec_ids]
        real_part = operator[:, 0] * source[:, 0] - operator[:, 1] * source[:, 1]
        imag_part = operator[:, 0] * source[:, 1] + operator[:, 1] * source[:, 0]
        return jnp.stack([jnp.sum(real_part, axis=0), jnp.sum(imag_part, axis=0)], axis=0)

    parent_incoming = lax.map(translate, (far_list, far_vector))

    def disaggregate(field):
        low_real = field[None, 0] * cosine + field[None, 1] * sine
        low_imag = field[None, 1] * cosine - field[None, 0] * sine
        lowered = jnp.stack([low_real, low_imag], axis=1)
        coarse = jnp.einsum("rt,cqrn->cqtn", theta_matrix, lowered, precision=highest)
        return jnp.einsum("cqtn,pn->cqtp", coarse, phi_matrix, precision=highest)

    child_incoming = lax.map(disaggregate, parent_incoming).reshape(NCH, 2, TRC, NPC)
    return parent_incoming, child_incoming
```

```python
import jax
import jax.numpy as jnp
from jax import lax
from jax.experimental import pallas as pl
from jax.experimental.pallas import tpu as pltpu
from jax.sharding import PartitionSpec as P

P_SIZE = 6
OCTANTS = 8
TILE = 128
PAIR = 2 * TILE
HALF = TILE // 2
VMEM_BYTES = 24 * 1024 * 1024
F32 = jnp.float32
BF16 = jnp.bfloat16

SIN_TERMS = (-1 / 6, 1 / 120, -1 / 5040, 1 / 362880, -1 / 39916800, 1 / 6227020800)
COS_TERMS = (-1 / 2, 1 / 24, -1 / 720, 1 / 40320, -1 / 3628800, 1 / 479001600, -1 / 87178291200)


def split_two(value):
    high = value.astype(BF16)
    return high, (value - high.astype(F32)).astype(BF16)


def split_three(value):
    high = value.astype(BF16)
    rest = value - high.astype(F32)
    middle = rest.astype(BF16)
    return high, middle, (rest - middle.astype(F32)).astype(BF16)


def product(left, right, left_dim=1, right_dim=0):
    return lax.dot_general(left, right, (((left_dim,), (right_dim,)), ((), ())), preferred_element_type=F32)


def product_exact(left, right, left_dim=1, right_dim=0):
    return lax.dot_general(
        left,
        right,
        (((left_dim,), (right_dim,)), ((), ())),
        preferred_element_type=F32,
        precision=lax.Precision.HIGHEST,
    )


def series(square, terms):
    total = jnp.full_like(square, terms[-1])
    for term in terms[-2::-1]:
        total = total * square + term
    return total


def iota(shape, dim):
    return lax.broadcasted_iota(jnp.int32, shape, dim)


def turned(block):
    return jnp.roll(block, HALF, axis=1)


def folded(theta, sources, own):
    below, middle, above = theta[:, :own], theta[:, own : 2 * own], theta[:, 2 * own :]
    return (middle, below + above) if sources == 2 else (middle, below, above)


def prepare_kernel(groups, sources, own, phase_ref, stencil_ref, weight_ref, theta_ref, cos_ref, sin_ref, wide_ref, up_ref, down_ref, cos_s, sin_s):
    rows = theta_ref.shape[0]
    azimuth = phase_ref.shape[1]
    blocks = wide_ref.shape[0]
    half = 0.5 * phase_ref[...]
    square = half * half
    sine = half + half * square * series(square, SIN_TERMS)
    cosine = 1.0 + square * series(square, COS_TERMS)
    for value, held, target in ((1.0 - 2.0 * sine * sine, cos_s, cos_ref), (2.0 * sine * cosine, sin_s, sin_ref)):
        for tile in range(azimuth // TILE):
            lanes = slice(tile * TILE, (tile + 1) * TILE)
            held[tile] = value[:, lanes]
            for octant in range(OCTANTS):
                part = held[tile, pl.ds(octant, rows, stride=OCTANTS), :]
                for group in range(groups):
                    target[octant, group * rows : (group + 1) * rows, lanes] = part
    for block in range(blocks):
        columns = slice(block * PAIR, (block + 1) * PAIR)
        after, before = (block + 1) % blocks, (block - 1) % blocks
        pieces = (
            (0, TILE, block * TILE),
            (TILE, 16, after * TILE),
            (PAIR - 16, 16, before * TILE + TILE - 16),
        )
        for start, size, first in pieces:
            child = iota((size, PAIR), 0) + first
            total = jnp.zeros((size, PAIR), F32)
            for point in range(P_SIZE):
                hit = stencil_ref[point : point + 1, columns] == child
                total = jnp.where(hit, weight_ref[point : point + 1, columns], total)
            high, low = split_two(total)
            wide_ref[block, start : start + size, :] = high
            wide_ref[block, PAIR + start : PAIR + start + size, :] = low
        empty = jnp.zeros((TILE - 32, PAIR), BF16)
        wide_ref[block, TILE + 16 : PAIR - 16, :] = empty
        wide_ref[block, PAIR + TILE + 16 : 2 * PAIR - 16, :] = empty
    tall, long = OCTANTS * groups * rows, groups * OCTANTS * own
    theta = theta_ref[...]
    for place, weights in enumerate(folded(theta, sources, own)):
        at_row = iota((tall, rows), 0) % rows == iota((tall, rows), 1)
        at_own = iota((own, long), 1) % own == iota((own, long), 0)
        spread = product_exact(product_exact(at_row.astype(F32), weights), at_own.astype(F32))
        tall_id = iota((tall, long), 0)
        octant = tall_id // (groups * rows)
        group = (tall_id // rows) % groups
        same = iota((tall, long), 1) // own == group * OCTANTS + octant
        high, low = split_two(jnp.where(same, spread, 0.0))
        up_ref[0, :, place * long : (place + 1) * long] = high
        up_ref[1, :, place * long : (place + 1) * long] = low
        at_row = iota((rows, tall), 1) % rows == iota((rows, tall), 0)
        at_own = iota((long, own), 0) % own == iota((long, own), 1)
        spread = product_exact(product_exact(at_own.astype(F32), weights, 1, 1), at_row.astype(F32))
        tall_id = iota((long, tall), 1)
        octant = tall_id // (groups * rows)
        group = (tall_id // rows) % groups
        same = iota((long, tall), 0) // own == group * OCTANTS + octant
        high, low = split_two(jnp.where(same, spread, 0.0))
        down_ref[0, place * long : (place + 1) * long, :] = high
        down_ref[1, place * long : (place + 1) * long, :] = low


def packed_pieces(real, imag, columns):
    lane = iota((real.shape[0], TILE), 1)
    found = []
    if columns == HALF:
        for start in range(0, real.shape[1], TILE):
            a, b = real[:, start : start + TILE], imag[:, start : start + TILE]
            found.append(jnp.where(lane < HALF, a, turned(b)))
            found.append(jnp.where(lane < HALF, turned(a), b))
        return found
    for start in range(0, real.shape[1], columns):
        found.append(jnp.concatenate([real[:, start : start + columns], imag[:, start : start + columns]], axis=1))
    return found


def unpacked_pieces(read, devices, columns):
    if columns == HALF:
        real, imag = [], []
        for pair in range(devices // 2):
            a, b = read(2 * pair), read(2 * pair + 1)
            lane = iota(a.shape, 1)
            real.append(jnp.where(lane < HALF, a, turned(b)))
            imag.append(jnp.where(lane < HALF, turned(a), b))
        return jnp.concatenate(real, axis=1), jnp.concatenate(imag, axis=1)
    blocks = [read(device) for device in range(devices)]
    return (
        jnp.concatenate([block[:, :columns] for block in blocks], axis=1),
        jnp.concatenate([block[:, columns:] for block in blocks], axis=1),
    )


def aggregate_kernel(groups, sources, own, devices, relative, *refs):
    fields = refs[:sources]
    cos_ref, sin_ref, wide_ref, up_ref = refs[sources : sources + 4]
    outs = refs[sources + 4 : -1]
    scratch = refs[-1]
    me = lax.axis_index("clus") if relative else 0
    blocks = wide_ref.shape[0]
    rows_all = cos_ref.shape[1]
    azimuth = cos_ref.shape[2]
    columns = azimuth // devices
    long = groups * OCTANTS * own
    stride = 2 * blocks
    refined = []
    for part in range(2):
        stacked = jnp.concatenate(
            [
                jnp.concatenate([field[pl.ds(2 * block + part, long, stride=stride), :] for block in range(blocks)], axis=1)
                for field in fields
            ],
            axis=0,
        )
        high, low = split_two(stacked)
        refined.append(product(up_ref[0], high) + (product(up_ref[1], high) + product(up_ref[0], low)))
    refined = jnp.concatenate(refined, axis=0)
    high, low = split_two(refined)
    lane = iota((refined.shape[0], TILE), 1)
    tall = OCTANTS * rows_all

    def windows(value, block):
        main = value[:, block * TILE : (block + 1) * TILE]
        after, before = (block + 1) % blocks, (block - 1) % blocks
        rim = jnp.where(lane < HALF, value[:, after * TILE : (after + 1) * TILE], value[:, before * TILE : (before + 1) * TILE])
        return [main, rim]

    for block in range(blocks):
        one, two = windows(high, block), windows(low, block)
        left = jnp.concatenate(one + two + one, axis=1)
        right = jnp.concatenate([wide_ref[block, :PAIR], wide_ref[block, :PAIR], wide_ref[block, PAIR:]], axis=0)
        spread = product(left, right)
        real = jnp.zeros((rows_all, PAIR), F32)
        imag = jnp.zeros((rows_all, PAIR), F32)
        for octant in range(OCTANTS):
            cosine = cos_ref[octant, :, block * PAIR : (block + 1) * PAIR]
            sine = sin_ref[octant, :, block * PAIR : (block + 1) * PAIR]
            a = spread[octant * rows_all : (octant + 1) * rows_all]
            b = spread[tall + octant * rows_all : tall + (octant + 1) * rows_all]
            real += a * cosine - b * sine
            imag += a * sine + b * cosine
        first = block * PAIR // columns
        for place, piece in enumerate(packed_pieces(real, imag, columns)):
            scratch[(first + place) ^ me] = piece
    hand_out(scratch, outs)


def hand_out(scratch, outs):
    if len(outs) == 1:
        outs[0][...] = scratch[...]
    else:
        for place, out in enumerate(outs):
            out[...] = scratch[place]


def tables_kernel(listed_ref, vector_ref, even_ref, odd_ref, hot_ref, even_out, odd_out):
    clusters, partners = listed_ref.shape
    vectors = even_ref.shape[0]
    even = jnp.concatenate(split_three(even_ref[...]), axis=0)
    odd = jnp.concatenate(split_three(odd_ref[...]), axis=0)
    for partner in range(partners):
        rows = slice(partner * clusters, (partner + 1) * clusters)
        listed = listed_ref[:, partner : partner + 1]
        hot = (iota((clusters, 3 * clusters), 1) % clusters == listed).astype(F32)
        hot_ref[rows, :] = hot.astype(BF16)
        vector = vector_ref[:, partner : partner + 1]
        chosen = (iota((clusters, 3 * vectors), 1) % vectors == vector).astype(F32).astype(BF16)
        even_out[rows, :] = product(chosen, even)
        odd_out[rows, :] = product(chosen, odd)


def translate_kernel(groups, rows, devices, relative, hot_ref, even_ref, odd_ref, *refs):
    count = devices if relative else 1
    arrived, outs, held, ready = refs[:count], refs[count : 2 * count], refs[-2], refs[-1]
    me = lax.axis_index("clus") if relative else 0
    size = groups * rows
    clusters = groups * devices
    partners = hot_ref.shape[0] // clusters
    width = held.shape[1]
    if relative:
        for place, block in enumerate(arrived):
            held[pl.ds(pl.multiple_of((me ^ place) * size, 8), size), :] = block[...]
    else:
        for device in range(devices):
            held[device * size : (device + 1) * size, :] = arrived[0][device]
    for row in range(rows):
        source = held[pl.ds(row, clusters, stride=rows), :]
        gathered = product(hot_ref[...], jnp.concatenate(split_three(source), axis=0))
        direct = jnp.zeros((clusters, width), F32)
        crossed = jnp.zeros((clusters, width), F32)
        for partner in range(partners):
            part = slice(partner * clusters, (partner + 1) * clusters)
            value = gathered[part]
            direct += value * even_ref[part, row * width : (row + 1) * width]
            crossed += value * odd_ref[part, row * width : (row + 1) * width]
        ready[pl.ds(row, clusters, stride=rows), :] = direct + jnp.roll(crossed, width // 2, axis=1)
    if relative:
        for place, out in enumerate(outs):
            out[...] = ready[pl.ds(pl.multiple_of((me ^ place) * size, 8), size), :]
    else:
        for device in range(devices):
            outs[0][device] = ready[device * size : (device + 1) * size, :]


def lower_kernel(groups, sources, own, devices, relative, *refs):
    count = devices if relative else 1
    arrived = refs[:count]
    cos_ref, sin_ref, wide_ref, down_ref = refs[count : count + 4]
    real_ref, imag_ref = refs[count + 4 : count + 6]
    outs = refs[count + 6 : count + 6 + sources]
    held = refs[-1]
    me = lax.axis_index("clus") if relative else 0
    blocks = wide_ref.shape[0]
    rows_all = cos_ref.shape[1]
    azimuth = cos_ref.shape[2]
    columns = azimuth // devices
    long = groups * OCTANTS * own
    tall = OCTANTS * rows_all
    stride = 2 * blocks
    if relative:
        for place, block in enumerate(arrived):
            held[me ^ place] = block[...]
    else:
        held[...] = arrived[0][...]
    real, imag = unpacked_pieces(lambda device: held[device], devices, columns)
    real_ref[...] = real
    imag_ref[...] = imag
    mains, rims = [], []
    for block in range(blocks):
        part = slice(block * PAIR, (block + 1) * PAIR)
        a, b = real[:, part], imag[:, part]
        low_real, low_imag = [], []
        for octant in range(OCTANTS):
            cosine, sine = cos_ref[octant, :, part], sin_ref[octant, :, part]
            low_real.append(a * cosine + b * sine)
            low_imag.append(b * cosine - a * sine)
        high, low = split_two(jnp.concatenate(low_real + low_imag, axis=0))
        left = jnp.concatenate([high, low, high], axis=1)
        right = jnp.concatenate([wide_ref[block, :PAIR], wide_ref[block, :PAIR], wide_ref[block, PAIR:]], axis=1)
        both = product(left, right, 1, 1)
        mains.append(both[:, :TILE])
        rims.append(both[:, TILE:])
    lane = iota((2 * tall, TILE), 1)
    coarse = jnp.concatenate(
        [
            mains[block] + jnp.where(lane < HALF, rims[(block - 1) % blocks], rims[(block + 1) % blocks])
            for block in range(blocks)
        ],
        axis=1,
    )
    high, low = split_two(coarse)
    for place, out in enumerate(outs):
        up, fine = down_ref[0, place * long : (place + 1) * long, :], down_ref[1, place * long : (place + 1) * long, :]
        for part in range(2):
            rows = slice(part * tall, (part + 1) * tall)
            value = product(up, high[rows]) + (product(fine, high[rows]) + product(up, low[rows]))
            for block in range(blocks):
                out[pl.ds(2 * block + part, long, stride=stride), :] = value[:, block * TILE : (block + 1) * TILE]


def call(kernel, outs, args, flops, scratch=(), name=None):
    held = sum(4 * leaf.size for leaf in outs) + sum(4 * arg.size for arg in args)
    return pl.pallas_call(
        kernel,
        out_shape=outs,
        in_specs=[pl.BlockSpec(memory_space=pltpu.VMEM)] * len(args),
        out_specs=[pl.BlockSpec(memory_space=pltpu.VMEM)] * len(outs),
        scratch_shapes=list(scratch),
        compiler_params=pltpu.CompilerParams(vmem_limit_bytes=VMEM_BYTES),
        cost_estimate=pl.CostEstimate(flops=flops, bytes_accessed=held, transcendentals=0),
        name=name,
    )(*args)


def bind(kernel, *settings):
    return lambda *refs: kernel(*settings, *refs)


def exchange(blocks, devices, relative):
    if not relative:
        return [lax.all_to_all(blocks[0], "clus", split_axis=0, concat_axis=0, tiled=True)]
    moved = [blocks[0]]
    for step in range(1, devices):
        moved.append(lax.ppermute(blocks[step], "clus", [(i, i ^ step) for i in range(devices)]))
    return moved


def per_device(child_patterns, theta_weights, phi_stencil, phi_weights, shift_phase, translation_table, far_list, far_vector):
    devices, halves = lax.axis_size("clus"), lax.axis_size("samp")
    children, _, own, columns = child_patterns.shape
    groups = children // OCTANTS
    rows, azimuth = theta_weights.shape[0], phi_stencil.shape[0]
    clusters, partners = far_list.shape
    vectors, width = translation_table.shape[0], 2 * translation_table.shape[3]
    blocks, rows_all = columns // TILE, groups * rows
    long, tall = children * own, OCTANTS * rows_all
    sources = 2 if halves == 2 else 3
    relative = devices & (devices - 1) == 0 and devices <= 16 and (rows_all % 8 == 0)
    struct = jax.ShapeDtypeStruct

    field = child_patterns.reshape(children, 2, own, blocks, TILE).transpose(0, 2, 3, 1, 4).reshape(long * blocks * 2, TILE)
    from_below = lax.ppermute(field, "samp", [(i, (i + 1) % halves) for i in range(halves)])
    fields = [field, from_below]
    if sources == 3:
        fields.append(lax.ppermute(field, "samp", [((i + 1) % halves, i) for i in range(halves)]))

    phase = shift_phase.transpose(1, 0, 2).reshape(rows * OCTANTS, azimuth)
    cosine, sine, wide, up, down = call(
        bind(prepare_kernel, groups, sources, own),
        [
            struct((OCTANTS, rows_all, azimuth), F32),
            struct((OCTANTS, rows_all, azimuth), F32),
            struct((blocks, 2 * PAIR, PAIR), BF16),
            struct((2, tall, sources * long), BF16),
            struct((2, sources * long, tall), BF16),
        ],
        [phase, phi_stencil.T, phi_weights.T, theta_weights],
        200_000_000,
        [pltpu.VMEM((azimuth // TILE, rows * OCTANTS, TILE), F32)] * 2,
        "prepare",
    )
    size = struct((rows_all, width), F32)
    sent = [size] * devices if relative else [struct((devices, rows_all, width), F32)]
    outgoing = call(
        bind(aggregate_kernel, groups, sources, own, devices, relative),
        sent,
        [*fields, cosine, sine, wide, up],
        1_500_000_000,
        [pltpu.VMEM((devices, rows_all, width), F32)],
        "aggregate",
    )
    arrived = exchange(outgoing, devices, relative)

    real, imag = translation_table[:, 0], translation_table[:, 1]
    even = jnp.concatenate([real, real], axis=-1).reshape(vectors, rows * width)
    odd = jnp.concatenate([imag, -imag], axis=-1).reshape(vectors, rows * width)
    hot, even, odd = call(
        tables_kernel,
        [
            struct((partners * clusters, 3 * clusters), BF16),
            struct((partners * clusters, rows * width), F32),
            struct((partners * clusters, rows * width), F32),
        ],
        [far_list, far_vector, even, odd],
        600_000_000,
        (),
        "tables",
    )
    translated = call(
        bind(translate_kernel, groups, rows, devices, relative),
        sent,
        [hot, even, odd, *arrived],
        600_000_000,
        [pltpu.VMEM((clusters * rows, width), F32)] * 2,
        "translate",
    )
    returned = exchange(translated, devices, relative)
    lowered = call(
        bind(lower_kernel, groups, sources, own, devices, relative),
        [struct((rows_all, azimuth), F32)] * 2 + [struct((long * blocks * 2, TILE), F32)] * sources,
        [*returned, cosine, sine, wide, down],
        1_500_000_000,
        [pltpu.VMEM((devices, rows_all, width), F32)],
        "lower",
    )
    total = lowered[2] + lax.ppermute(lowered[3], "samp", [((i + 1) % halves, i) for i in range(halves)])
    if sources == 3:
        total = total + lax.ppermute(lowered[4], "samp", [(i, (i + 1) % halves) for i in range(halves)])
    child_incoming = total.reshape(children, own, blocks, 2, TILE).transpose(0, 3, 1, 2, 4).reshape(children, 2, own, columns)
    parent_incoming = jnp.stack([part.reshape(groups, rows, azimuth) for part in lowered[:2]], axis=1)
    return (parent_incoming, child_incoming)


def solution(mesh):
    placed = (
        P("clus", None, "samp", None),
        P(),
        P(),
        P(),
        P(None, "samp", None),
        P(None, None, "samp", "clus"),
        P(),
        P(),
    )
    return jax.shard_map(
        per_device,
        mesh=mesh,
        in_specs=placed,
        out_specs=(P("clus", None, "samp", None), P("clus", None, "samp", None)),
        check_vma=False,
    )
```

```python
import jax
import jax.numpy as jnp
from jax import lax
from jax.experimental import pallas as pl
from jax.experimental.pallas import tpu as pltpu
from jax.sharding import PartitionSpec as P

P_SIZE = 6
OCTANTS = 8
TILE = 128
PAIR = 2 * TILE
HALF = TILE // 2
VMEM_BYTES = 24 * 1024 * 1024
F32 = jnp.float32
BF16 = jnp.bfloat16

SIN_TERMS = (-1 / 6, 1 / 120, -1 / 5040, 1 / 362880, -1 / 39916800, 1 / 6227020800)
COS_TERMS = (-1 / 2, 1 / 24, -1 / 720, 1 / 40320, -1 / 3628800, 1 / 479001600, -1 / 87178291200)


def split_two(value):
    high = value.astype(BF16)
    return high, (value - high.astype(F32)).astype(BF16)


def split_three(value):
    high = value.astype(BF16)
    rest = value - high.astype(F32)
    middle = rest.astype(BF16)
    return high, middle, (rest - middle.astype(F32)).astype(BF16)


def product(left, right, left_dim=1, right_dim=0):
    return lax.dot_general(left, right, (((left_dim,), (right_dim,)), ((), ())), preferred_element_type=F32)


def product_exact(left, right, left_dim=1, right_dim=0):
    return lax.dot_general(
        left,
        right,
        (((left_dim,), (right_dim,)), ((), ())),
        preferred_element_type=F32,
        precision=lax.Precision.HIGHEST,
    )


def series(square, terms):
    total = jnp.full_like(square, terms[-1])
    for term in terms[-2::-1]:
        total = total * square + term
    return total


def iota(shape, dim):
    return lax.broadcasted_iota(jnp.int32, shape, dim)


def turned(block):
    return jnp.roll(block, HALF, axis=1)


def folded(theta, sources, own):
    below, middle, above = theta[:, :own], theta[:, own : 2 * own], theta[:, 2 * own :]
    return (middle, below + above) if sources == 2 else (middle, below, above)


def prepare_kernel(groups, sources, own, phase_ref, stencil_ref, weight_ref, theta_ref, cos_ref, sin_ref, wide_ref, up_ref, down_ref, cos_s, sin_s):
    rows = theta_ref.shape[0]
    azimuth = phase_ref.shape[1]
    blocks = wide_ref.shape[0]
    half = 0.5 * phase_ref[...]
    square = half * half
    sine = half + half * square * series(square, SIN_TERMS)
    cosine = 1.0 + square * series(square, COS_TERMS)
    for value, held, target in ((1.0 - 2.0 * sine * sine, cos_s, cos_ref), (2.0 * sine * cosine, sin_s, sin_ref)):
        for tile in range(azimuth // TILE):
            lanes = slice(tile * TILE, (tile + 1) * TILE)
            held[tile] = value[:, lanes]
            for octant in range(OCTANTS):
                part = held[tile, pl.ds(octant, rows, stride=OCTANTS), :]
                for group in range(groups):
                    target[octant, group * rows : (group + 1) * rows, lanes] = part
    for block in range(blocks):
        columns = slice(block * PAIR, (block + 1) * PAIR)
        after, before = (block + 1) % blocks, (block - 1) % blocks
        pieces = (
            (0, TILE, block * TILE),
            (TILE, 16, after * TILE),
            (PAIR - 16, 16, before * TILE + TILE - 16),
        )
        for start, size, first in pieces:
            child = iota((size, PAIR), 0) + first
            total = jnp.zeros((size, PAIR), F32)
            for point in range(P_SIZE):
                hit = stencil_ref[point : point + 1, columns] == child
                total = jnp.where(hit, weight_ref[point : point + 1, columns], total)
            high, low = split_two(total)
            wide_ref[block, start : start + size, :] = high
            wide_ref[block, PAIR + start : PAIR + start + size, :] = low
        empty = jnp.zeros((TILE - 32, PAIR), BF16)
        wide_ref[block, TILE + 16 : PAIR - 16, :] = empty
        wide_ref[block, PAIR + TILE + 16 : 2 * PAIR - 16, :] = empty
    tall, long = OCTANTS * groups * rows, groups * OCTANTS * own
    theta = theta_ref[...]
    for place, weights in enumerate(folded(theta, sources, own)):
        at_row = iota((tall, rows), 0) % rows == iota((tall, rows), 1)
        at_own = iota((own, long), 1) % own == iota((own, long), 0)
        spread = product_exact(product_exact(at_row.astype(F32), weights), at_own.astype(F32))
        tall_id = iota((tall, long), 0)
        octant = tall_id // (groups * rows)
        group = (tall_id // rows) % groups
        same = iota((tall, long), 1) // own == group * OCTANTS + octant
        high, low = split_two(jnp.where(same, spread, 0.0))
        up_ref[0, :, place * long : (place + 1) * long] = high
        up_ref[1, :, place * long : (place + 1) * long] = low
        at_row = iota((rows, tall), 1) % rows == iota((rows, tall), 0)
        at_own = iota((long, own), 0) % own == iota((long, own), 1)
        spread = product_exact(product_exact(at_own.astype(F32), weights, 1, 1), at_row.astype(F32))
        tall_id = iota((long, tall), 1)
        octant = tall_id // (groups * rows)
        group = (tall_id // rows) % groups
        same = iota((long, tall), 0) // own == group * OCTANTS + octant
        high, low = split_two(jnp.where(same, spread, 0.0))
        down_ref[0, place * long : (place + 1) * long, :] = high
        down_ref[1, place * long : (place + 1) * long, :] = low


def packed_pieces(real, imag, columns):
    lane = iota((real.shape[0], TILE), 1)
    found = []
    if columns == HALF:
        for start in range(0, real.shape[1], TILE):
            a, b = real[:, start : start + TILE], imag[:, start : start + TILE]
            found.append(jnp.where(lane < HALF, a, turned(b)))
            found.append(jnp.where(lane < HALF, turned(a), b))
        return found
    for start in range(0, real.shape[1], columns):
        found.append(jnp.concatenate([real[:, start : start + columns], imag[:, start : start + columns]], axis=1))
    return found


def unpacked_pieces(read, devices, columns):
    if columns == HALF:
        real, imag = [], []
        for pair in range(devices // 2):
            a, b = read(2 * pair), read(2 * pair + 1)
            lane = iota(a.shape, 1)
            real.append(jnp.where(lane < HALF, a, turned(b)))
            imag.append(jnp.where(lane < HALF, turned(a), b))
        return jnp.concatenate(real, axis=1), jnp.concatenate(imag, axis=1)
    blocks = [read(device) for device in range(devices)]
    return (
        jnp.concatenate([block[:, :columns] for block in blocks], axis=1),
        jnp.concatenate([block[:, columns:] for block in blocks], axis=1),
    )


def aggregate_kernel(groups, sources, own, devices, relative, *refs):
    fields = refs[:sources]
    cos_ref, sin_ref, wide_ref, up_ref = refs[sources : sources + 4]
    outs = refs[sources + 4 : -1]
    scratch = refs[-1]
    me = lax.axis_index("clus") if relative else 0
    blocks = wide_ref.shape[0]
    rows_all = cos_ref.shape[1]
    azimuth = cos_ref.shape[2]
    columns = azimuth // devices
    long = groups * OCTANTS * own
    stride = 2 * blocks
    refined = []
    for part in range(2):
        stacked = jnp.concatenate(
            [
                jnp.concatenate([field[pl.ds(2 * block + part, long, stride=stride), :] for block in range(blocks)], axis=1)
                for field in fields
            ],
            axis=0,
        )
        high, low = split_two(stacked)
        refined.append(product(up_ref[0], high) + (product(up_ref[1], high) + product(up_ref[0], low)))
    refined = jnp.concatenate(refined, axis=0)
    high, low = split_two(refined)
    lane = iota((refined.shape[0], TILE), 1)
    tall = OCTANTS * rows_all

    def windows(value, block):
        main = value[:, block * TILE : (block + 1) * TILE]
        after, before = (block + 1) % blocks, (block - 1) % blocks
        rim = jnp.where(lane < HALF, value[:, after * TILE : (after + 1) * TILE], value[:, before * TILE : (before + 1) * TILE])
        return [main, rim]

    for block in range(blocks):
        one, two = windows(high, block), windows(low, block)
        left = jnp.concatenate(one + two + one, axis=1)
        right = jnp.concatenate([wide_ref[block, :PAIR], wide_ref[block, :PAIR], wide_ref[block, PAIR:]], axis=0)
        spread = product(left, right)
        real = jnp.zeros((rows_all, PAIR), F32)
        imag = jnp.zeros((rows_all, PAIR), F32)
        for octant in range(OCTANTS):
            cosine = cos_ref[octant, :, block * PAIR : (block + 1) * PAIR]
            sine = sin_ref[octant, :, block * PAIR : (block + 1) * PAIR]
            a = spread[octant * rows_all : (octant + 1) * rows_all]
            b = spread[tall + octant * rows_all : tall + (octant + 1) * rows_all]
            real += a * cosine - b * sine
            imag += a * sine + b * cosine
        first = block * PAIR // columns
        for place, piece in enumerate(packed_pieces(real, imag, columns)):
            scratch[(first + place) ^ me] = piece
    hand_out(scratch, outs)


def hand_out(scratch, outs):
    if len(outs) == 1:
        outs[0][...] = scratch[...]
    else:
        for place, out in enumerate(outs):
            out[...] = scratch[place]


def tables_kernel(listed_ref, vector_ref, even_ref, odd_ref, hot_ref, even_out, odd_out):
    clusters, partners = listed_ref.shape
    vectors = even_ref.shape[0]
    even = jnp.concatenate(split_three(even_ref[...]), axis=0)
    odd = jnp.concatenate(split_three(odd_ref[...]), axis=0)
    for partner in range(partners):
        rows = slice(partner * clusters, (partner + 1) * clusters)
        listed = listed_ref[:, partner : partner + 1]
        hot = (iota((clusters, 3 * clusters), 1) % clusters == listed).astype(F32)
        hot_ref[rows, :] = hot.astype(BF16)
        vector = vector_ref[:, partner : partner + 1]
        chosen = (iota((clusters, 3 * vectors), 1) % vectors == vector).astype(F32).astype(BF16)
        even_out[rows, :] = product(chosen, even)
        odd_out[rows, :] = product(chosen, odd)


def translate_kernel(groups, rows, devices, relative, hot_ref, even_ref, odd_ref, *refs):
    count = devices if relative else 1
    arrived, outs, held, ready = refs[:count], refs[count : 2 * count], refs[-2], refs[-1]
    me = lax.axis_index("clus") if relative else 0
    size = groups * rows
    clusters = groups * devices
    partners = hot_ref.shape[0] // clusters
    width = held.shape[1]
    if relative:
        for place, block in enumerate(arrived):
            held[pl.ds(pl.multiple_of((me ^ place) * size, 8), size), :] = block[...]
    else:
        for device in range(devices):
            held[device * size : (device + 1) * size, :] = arrived[0][device]
    for row in range(rows):
        source = held[pl.ds(row, clusters, stride=rows), :]
        gathered = product(hot_ref[...], jnp.concatenate(split_three(source), axis=0))
        direct = jnp.zeros((clusters, width), F32)
        crossed = jnp.zeros((clusters, width), F32)
        for partner in range(partners):
            part = slice(partner * clusters, (partner + 1) * clusters)
            value = gathered[part]
            direct += value * even_ref[part, row * width : (row + 1) * width]
            crossed += value * odd_ref[part, row * width : (row + 1) * width]
        ready[pl.ds(row, clusters, stride=rows), :] = direct + jnp.roll(crossed, width // 2, axis=1)
    if relative:
        for place, out in enumerate(outs):
            out[...] = ready[pl.ds(pl.multiple_of((me ^ place) * size, 8), size), :]
    else:
        for device in range(devices):
            outs[0][device] = ready[device * size : (device + 1) * size, :]


def lower_kernel(groups, sources, own, devices, relative, *refs):
    count = devices if relative else 1
    arrived = refs[:count]
    cos_ref, sin_ref, wide_ref, down_ref = refs[count : count + 4]
    real_ref, imag_ref = refs[count + 4 : count + 6]
    outs = refs[count + 6 : count + 6 + sources]
    held = refs[-1]
    me = lax.axis_index("clus") if relative else 0
    blocks = wide_ref.shape[0]
    rows_all = cos_ref.shape[1]
    azimuth = cos_ref.shape[2]
    columns = azimuth // devices
    long = groups * OCTANTS * own
    tall = OCTANTS * rows_all
    stride = 2 * blocks
    if relative:
        for place, block in enumerate(arrived):
            held[me ^ place] = block[...]
    else:
        held[...] = arrived[0][...]
    real, imag = unpacked_pieces(lambda device: held[device], devices, columns)
    real_ref[...] = real
    imag_ref[...] = imag
    mains, rims = [], []
    for block in range(blocks):
        part = slice(block * PAIR, (block + 1) * PAIR)
        a, b = real[:, part], imag[:, part]
        low_real, low_imag = [], []
        for octant in range(OCTANTS):
            cosine, sine = cos_ref[octant, :, part], sin_ref[octant, :, part]
            low_real.append(a * cosine + b * sine)
            low_imag.append(b * cosine - a * sine)
        high, low = split_two(jnp.concatenate(low_real + low_imag, axis=0))
        left = jnp.concatenate([high, low, high], axis=1)
        right = jnp.concatenate([wide_ref[block, :PAIR], wide_ref[block, :PAIR], wide_ref[block, PAIR:]], axis=1)
        both = product(left, right, 1, 1)
        mains.append(both[:, :TILE])
        rims.append(both[:, TILE:])
    lane = iota((2 * tall, TILE), 1)
    coarse = jnp.concatenate(
        [
            mains[block] + jnp.where(lane < HALF, rims[(block - 1) % blocks], rims[(block + 1) % blocks])
            for block in range(blocks)
        ],
        axis=1,
    )
    high, low = split_two(coarse)
    for place, out in enumerate(outs):
        up, fine = down_ref[0, place * long : (place + 1) * long, :], down_ref[1, place * long : (place + 1) * long, :]
        for part in range(2):
            rows = slice(part * tall, (part + 1) * tall)
            value = product(up, high[rows]) + (product(fine, high[rows]) + product(up, low[rows]))
            for block in range(blocks):
                out[pl.ds(2 * block + part, long, stride=stride), :] = value[:, block * TILE : (block + 1) * TILE]


def call(kernel, outs, args, flops, scratch=(), name=None):
    held = sum(4 * leaf.size for leaf in outs) + sum(4 * arg.size for arg in args)
    return pl.pallas_call(
        kernel,
        out_shape=outs,
        in_specs=[pl.BlockSpec(memory_space=pltpu.VMEM)] * len(args),
        out_specs=[pl.BlockSpec(memory_space=pltpu.VMEM)] * len(outs),
        scratch_shapes=list(scratch),
        compiler_params=pltpu.CompilerParams(vmem_limit_bytes=VMEM_BYTES),
        cost_estimate=pl.CostEstimate(flops=flops, bytes_accessed=held, transcendentals=0),
        name=name,
    )(*args)


def bind(kernel, *settings):
    return lambda *refs: kernel(*settings, *refs)


def exchange(blocks, devices, relative):
    if not relative:
        return [lax.all_to_all(blocks[0], "clus", split_axis=0, concat_axis=0, tiled=True)]
    moved = [blocks[0]]
    for step in range(1, devices):
        moved.append(lax.ppermute(blocks[step], "clus", [(i, i ^ step) for i in range(devices)]))
    return moved


def per_device(child_patterns, theta_weights, phi_stencil, phi_weights, shift_phase, translation_table, far_list, far_vector):
    devices, halves = lax.axis_size("clus"), lax.axis_size("samp")
    children, _, own, columns = child_patterns.shape
    groups = children // OCTANTS
    rows, azimuth = theta_weights.shape[0], phi_stencil.shape[0]
    clusters, partners = far_list.shape
    vectors, width = translation_table.shape[0], 2 * translation_table.shape[3]
    blocks, rows_all = columns // TILE, groups * rows
    long, tall = children * own, OCTANTS * rows_all
    sources = 2 if halves == 2 else 3
    relative = False
    struct = jax.ShapeDtypeStruct

    field = child_patterns.reshape(children, 2, own, blocks, TILE).transpose(0, 2, 3, 1, 4).reshape(long * blocks * 2, TILE)
    from_below = lax.ppermute(field, "samp", [(i, (i + 1) % halves) for i in range(halves)])
    fields = [field, from_below]
    if sources == 3:
        fields.append(lax.ppermute(field, "samp", [((i + 1) % halves, i) for i in range(halves)]))

    phase = shift_phase.transpose(1, 0, 2).reshape(rows * OCTANTS, azimuth)
    cosine, sine, wide, up, down = call(
        bind(prepare_kernel, groups, sources, own),
        [
            struct((OCTANTS, rows_all, azimuth), F32),
            struct((OCTANTS, rows_all, azimuth), F32),
            struct((blocks, 2 * PAIR, PAIR), BF16),
            struct((2, tall, sources * long), BF16),
            struct((2, sources * long, tall), BF16),
        ],
        [phase, phi_stencil.T, phi_weights.T, theta_weights],
        200_000_000,
        [pltpu.VMEM((azimuth // TILE, rows * OCTANTS, TILE), F32)] * 2,
        "prepare",
    )
    size = struct((rows_all, width), F32)
    sent = [size] * devices if relative else [struct((devices, rows_all, width), F32)]
    outgoing = call(
        bind(aggregate_kernel, groups, sources, own, devices, relative),
        sent,
        [*fields, cosine, sine, wide, up],
        1_500_000_000,
        [pltpu.VMEM((devices, rows_all, width), F32)],
        "aggregate",
    )
    arrived = exchange(outgoing, devices, relative)

    real, imag = translation_table[:, 0], translation_table[:, 1]
    even = jnp.concatenate([real, real], axis=-1).reshape(vectors, rows * width)
    odd = jnp.concatenate([imag, -imag], axis=-1).reshape(vectors, rows * width)
    hot, even, odd = call(
        tables_kernel,
        [
            struct((partners * clusters, 3 * clusters), BF16),
            struct((partners * clusters, rows * width), F32),
            struct((partners * clusters, rows * width), F32),
        ],
        [far_list, far_vector, even, odd],
        600_000_000,
        (),
        "tables",
    )
    translated = call(
        bind(translate_kernel, groups, rows, devices, relative),
        sent,
        [hot, even, odd, *arrived],
        600_000_000,
        [pltpu.VMEM((clusters * rows, width), F32)] * 2,
        "translate",
    )
    returned = exchange(translated, devices, relative)
    lowered = call(
        bind(lower_kernel, groups, sources, own, devices, relative),
        [struct((rows_all, azimuth), F32)] * 2 + [struct((long * blocks * 2, TILE), F32)] * sources,
        [*returned, cosine, sine, wide, down],
        1_500_000_000,
        [pltpu.VMEM((devices, rows_all, width), F32)],
        "lower",
    )
    total = lowered[2] + lax.ppermute(lowered[3], "samp", [((i + 1) % halves, i) for i in range(halves)])
    if sources == 3:
        total = total + lax.ppermute(lowered[4], "samp", [(i, (i + 1) % halves) for i in range(halves)])
    child_incoming = total.reshape(children, own, blocks, 2, TILE).transpose(0, 3, 1, 2, 4).reshape(children, 2, own, columns)
    parent_incoming = jnp.stack([part.reshape(groups, rows, azimuth) for part in lowered[:2]], axis=1)
    return (parent_incoming, child_incoming)


def solution(mesh):
    placed = (
        P("clus", None, "samp", None),
        P(),
        P(),
        P(),
        P(None, "samp", None),
        P(None, None, "samp", "clus"),
        P(),
        P(),
    )
    return jax.shard_map(
        per_device,
        mesh=mesh,
        in_specs=placed,
        out_specs=(P("clus", None, "samp", None), P("clus", None, "samp", None)),
        check_vma=False,
    )
```

```python
import jax
import jax.numpy as jnp
from jax import lax
from jax.experimental import pallas as pl
from jax.experimental.pallas import tpu as pltpu
from jax.sharding import PartitionSpec as P

P_SIZE = 6
OCTANTS = 8
TILE = 128
PAIR = 2 * TILE
HALF = TILE // 2
VMEM_BYTES = 24 * 1024 * 1024
F32 = jnp.float32
BF16 = jnp.bfloat16

SIN_TERMS = (-1 / 6, 1 / 120, -1 / 5040, 1 / 362880, -1 / 39916800, 1 / 6227020800)
COS_TERMS = (-1 / 2, 1 / 24, -1 / 720, 1 / 40320, -1 / 3628800, 1 / 479001600, -1 / 87178291200)


def split_two(value):
    high = value.astype(BF16)
    return high, (value - high.astype(F32)).astype(BF16)


def split_three(value):
    high = value.astype(BF16)
    rest = value - high.astype(F32)
    middle = rest.astype(BF16)
    return high, middle, (rest - middle.astype(F32)).astype(BF16)


def product(left, right, left_dim=1, right_dim=0):
    return lax.dot_general(left, right, (((left_dim,), (right_dim,)), ((), ())), preferred_element_type=F32)


def product_exact(left, right, left_dim=1, right_dim=0):
    return lax.dot_general(
        left,
        right,
        (((left_dim,), (right_dim,)), ((), ())),
        preferred_element_type=F32,
        precision=lax.Precision.HIGHEST,
    )


def series(square, terms):
    total = jnp.full_like(square, terms[-1])
    for term in terms[-2::-1]:
        total = total * square + term
    return total


def iota(shape, dim):
    return lax.broadcasted_iota(jnp.int32, shape, dim)


def turned(block):
    return jnp.roll(block, HALF, axis=1)


def folded(theta, sources, own):
    below, middle, above = theta[:, :own], theta[:, own : 2 * own], theta[:, 2 * own :]
    return (middle, below + above) if sources == 2 else (middle, below, above)


def prepare_kernel(groups, sources, own, *refs):
    names = 8
    remote, outs, rest = refs[:names], refs[names : names + 8], refs[names + 8 :]
    local, cos_s, sin_s, sems = rest[:names], rest[names], rest[names + 1], rest[names + 2]
    copies = [pltpu.make_async_copy(source, target, sems.at[place]) for place, (source, target) in enumerate(zip(remote, local))]
    for copy in copies:
        copy.start()
    theta_ref, phase_ref, stencil_ref, weight_ref, listed_ref, vector_ref, table_ref, field_ref = local
    cos_ref, sin_ref, wide_ref, up_ref, down_ref, hot_ref, table_out, partial_ref = outs
    rows = theta_ref.shape[0]
    azimuth = phase_ref.shape[1]
    blocks = wide_ref.shape[0]
    tall, long = OCTANTS * groups * rows, groups * OCTANTS * own

    copies[0].wait()
    theta = theta_ref[...]
    for place, weights in enumerate(folded(theta, sources, own)):
        at_row = iota((tall, rows), 0) % rows == iota((tall, rows), 1)
        at_own = iota((own, long), 1) % own == iota((own, long), 0)
        spread = product_exact(product_exact(at_row.astype(F32), weights), at_own.astype(F32))
        tall_id = iota((tall, long), 0)
        same = iota((tall, long), 1) // own == (tall_id // rows) % groups * OCTANTS + tall_id // (groups * rows)
        high, low = split_two(jnp.where(same, spread, 0.0))
        up_ref[place, 0] = high
        up_ref[place, 1] = low
        at_row = iota((rows, tall), 1) % rows == iota((rows, tall), 0)
        at_own = iota((long, own), 0) % own == iota((long, own), 1)
        spread = product_exact(product_exact(at_own.astype(F32), weights, 1, 1), at_row.astype(F32))
        tall_id = iota((long, tall), 1)
        same = iota((long, tall), 0) // own == (tall_id // rows) % groups * OCTANTS + tall_id // (groups * rows)
        high, low = split_two(jnp.where(same, spread, 0.0))
        down_ref[place, 0] = high
        down_ref[place, 1] = low

    copies[1].wait()
    half = 0.5 * phase_ref[...]
    square = half * half
    sine = half + half * square * series(square, SIN_TERMS)
    cosine = 1.0 + square * series(square, COS_TERMS)
    for value, held, target in ((1.0 - 2.0 * sine * sine, cos_s, cos_ref), (2.0 * sine * cosine, sin_s, sin_ref)):
        for tile in range(azimuth // TILE):
            lanes = slice(tile * TILE, (tile + 1) * TILE)
            held[tile] = value[:, lanes]
            for octant in range(OCTANTS):
                part = held[tile, pl.ds(octant, rows, stride=OCTANTS), :]
                for group in range(groups):
                    target[octant, group * rows : (group + 1) * rows, lanes] = part

    copies[2].wait()
    copies[3].wait()
    for block in range(blocks):
        columns = slice(block * PAIR, (block + 1) * PAIR)
        after, before = (block + 1) % blocks, (block - 1) % blocks
        pieces = (
            (0, TILE, block * TILE),
            (TILE, 16, after * TILE),
            (PAIR - 16, 16, before * TILE + TILE - 16),
        )
        for start, size, first in pieces:
            child = iota((size, PAIR), 0) + first
            total = jnp.zeros((size, PAIR), F32)
            for point in range(P_SIZE):
                hit = stencil_ref[point : point + 1, columns] == child
                total = jnp.where(hit, weight_ref[point : point + 1, columns], total)
            high, low = split_two(total)
            wide_ref[block, start : start + size, :] = high
            wide_ref[block, PAIR + start : PAIR + start + size, :] = low
        empty = jnp.zeros((TILE - 32, PAIR), BF16)
        wide_ref[block, TILE + 16 : PAIR - 16, :] = empty
        wide_ref[block, PAIR + TILE + 16 : 2 * PAIR - 16, :] = empty

    copies[4].wait()
    copies[5].wait()
    partners, clusters = listed_ref.shape
    vectors = table_out.shape[1] // 3
    unit = (iota((clusters, clusters), 0) == iota((clusters, clusters), 1)).astype(F32)
    listed = product_exact(unit, listed_ref[...].astype(F32), 1, 1)
    chosen = product_exact(unit, vector_ref[...].astype(F32), 1, 1)
    cluster = (iota((clusters, 3 * clusters), 1) % clusters).astype(F32)
    vector = (iota((clusters, 3 * vectors), 1) % vectors).astype(F32)
    for partner in range(partners):
        part = slice(partner * clusters, (partner + 1) * clusters)
        hot_ref[part, : 3 * clusters] = (cluster == listed[:, partner : partner + 1]).astype(F32).astype(BF16)
        hot_ref[part, 3 * clusters :] = (vector == chosen[:, partner : partner + 1]).astype(F32).astype(BF16)

    copies[6].wait()
    raw = table_ref[...]
    width = raw.shape[1]
    many = raw.shape[0]
    at = iota((many, many), 1)
    row = iota((many, many), 0)
    order = at == row % vectors * (2 * rows) + row // (2 * vectors) * 2 + row // vectors % 2
    sorted_rows = product_exact(order.astype(F32), raw)
    lane = iota((width, 2 * width), 1)
    twice = (lane % width == iota((width, 2 * width), 0)).astype(F32)
    signed = jnp.where(lane < width, twice, -twice)
    even = product_exact(sorted_rows, twice)
    odd = product_exact(sorted_rows, signed)
    for row in range(rows):
        start = 2 * row * vectors
        for place, piece in enumerate(split_three(even[start : start + vectors])):
            table_out[row, place * vectors : (place + 1) * vectors, : 2 * width] = piece
        for place, piece in enumerate(split_three(odd[start + vectors : start + 2 * vectors])):
            table_out[row, place * vectors : (place + 1) * vectors, 2 * width :] = piece

    copies[7].wait()
    for part in range(2):
        partial_ref[part * tall : (part + 1) * tall, :] = polar(up_ref[0, 0], up_ref[0, 1], field_rows(field_ref, part, blocks, long))


def field_rows(field, part, blocks, long):
    return jnp.concatenate([field[pl.ds(2 * block + part, long, stride=2 * blocks), :] for block in range(blocks)], axis=1)


def polar(high_weights, low_weights, value):
    high, low = split_two(value)
    return product(high_weights, high) + (product(low_weights, high) + product(high_weights, low))


def packed_pieces(real, imag, columns):
    lane = iota((real.shape[0], TILE), 1)
    found = []
    if columns == HALF:
        for start in range(0, real.shape[1], TILE):
            a, b = real[:, start : start + TILE], imag[:, start : start + TILE]
            found.append(jnp.where(lane < HALF, a, turned(b)))
            found.append(jnp.where(lane < HALF, turned(a), b))
        return found
    for start in range(0, real.shape[1], columns):
        found.append(jnp.concatenate([real[:, start : start + columns], imag[:, start : start + columns]], axis=1))
    return found


def unpacked_pieces(read, devices, columns):
    if columns == HALF:
        real, imag = [], []
        for pair in range(devices // 2):
            a, b = read(2 * pair), read(2 * pair + 1)
            lane = iota(a.shape, 1)
            real.append(jnp.where(lane < HALF, a, turned(b)))
            imag.append(jnp.where(lane < HALF, turned(a), b))
        return jnp.concatenate(real, axis=1), jnp.concatenate(imag, axis=1)
    blocks = [read(device) for device in range(devices)]
    return (
        jnp.concatenate([block[:, :columns] for block in blocks], axis=1),
        jnp.concatenate([block[:, columns:] for block in blocks], axis=1),
    )


def aggregate_kernel(groups, sources, own, devices, *refs):
    fields = refs[: sources - 1]
    partial_ref, cos_ref, sin_ref, wide_ref, up_ref, out = refs[sources - 1 :]
    blocks = wide_ref.shape[0]
    rows_all = cos_ref.shape[1]
    columns = cos_ref.shape[2] // devices
    long, tall = groups * OCTANTS * own, OCTANTS * rows_all
    refined = []
    for part in range(2):
        value = partial_ref[part * tall : (part + 1) * tall, :]
        for place, field in enumerate(fields):
            value += polar(up_ref[place + 1, 0], up_ref[place + 1, 1], field_rows(field, part, blocks, long))
        refined.append(value)
    high, low = split_two(jnp.concatenate(refined, axis=0))
    lane = iota((2 * tall, TILE), 1)

    def windows(value, block):
        main = value[:, block * TILE : (block + 1) * TILE]
        after, before = (block + 1) % blocks, (block - 1) % blocks
        rim = jnp.where(lane < HALF, value[:, after * TILE : (after + 1) * TILE], value[:, before * TILE : (before + 1) * TILE])
        return [main, rim]

    for block in range(blocks):
        one, two = windows(high, block), windows(low, block)
        left = jnp.concatenate(one + two + one, axis=1)
        right = jnp.concatenate([wide_ref[block, :PAIR], wide_ref[block, :PAIR], wide_ref[block, PAIR:]], axis=0)
        spread = product(left, right)
        real = jnp.zeros((rows_all, PAIR), F32)
        imag = jnp.zeros((rows_all, PAIR), F32)
        for octant in range(OCTANTS):
            cosine = cos_ref[octant, :, block * PAIR : (block + 1) * PAIR]
            sine = sin_ref[octant, :, block * PAIR : (block + 1) * PAIR]
            a = spread[octant * rows_all : (octant + 1) * rows_all]
            b = spread[tall + octant * rows_all : tall + (octant + 1) * rows_all]
            real += a * cosine - b * sine
            imag += a * sine + b * cosine
        first = block * PAIR // columns
        for place, piece in enumerate(packed_pieces(real, imag, columns)):
            out[first + place] = piece


def translate_kernel(rows, hot_ref, table_ref, arrived_ref, out):
    width = arrived_ref.shape[1]
    clusters = arrived_ref.shape[0] // rows
    partners = hot_ref.shape[0] // clusters
    hot_cluster = hot_ref[:, : 3 * clusters]
    hot_vector = hot_ref[:, 3 * clusters :]
    step = 2 if rows % 2 == 0 else 1
    for first in range(0, rows, step):
        source = jnp.concatenate(
            [arrived_ref[pl.ds(row, clusters, stride=rows), :] for row in range(first, first + step)], axis=1
        )
        gathered = product(hot_cluster, jnp.concatenate(split_three(source), axis=0))
        for row in range(first, first + step):
            factors = product(hot_vector, table_ref[row])
            direct = jnp.zeros((clusters, width), F32)
            crossed = jnp.zeros((clusters, width), F32)
            for partner in range(partners):
                part = slice(partner * clusters, (partner + 1) * clusters)
                value = gathered[part, (row - first) * width : (row - first + 1) * width]
                direct += value * factors[part, :width]
                crossed += value * factors[part, width:]
            out[pl.ds(row, clusters, stride=rows), :] = direct + jnp.roll(crossed, width // 2, axis=1)


def lower_kernel(groups, sources, own, devices, arrived_ref, cos_ref, sin_ref, wide_ref, down_ref, parent_ref, *outs):
    blocks = wide_ref.shape[0]
    rows_all = cos_ref.shape[1]
    azimuth = cos_ref.shape[2]
    columns = azimuth // devices
    long, tall = groups * OCTANTS * own, OCTANTS * rows_all
    real, imag = unpacked_pieces(lambda device: arrived_ref[device], devices, columns)
    tiles = azimuth // TILE
    for tile in range(tiles):
        for part, value in enumerate((real, imag)):
            parent_ref[pl.ds(2 * tile + part, rows_all, stride=2 * tiles), :] = value[:, tile * TILE : (tile + 1) * TILE]
    mains, rims = [], []
    for block in range(blocks):
        part = slice(block * PAIR, (block + 1) * PAIR)
        a, b = real[:, part], imag[:, part]
        low_real, low_imag = [], []
        for octant in range(OCTANTS):
            cosine, sine = cos_ref[octant, :, part], sin_ref[octant, :, part]
            low_real.append(a * cosine + b * sine)
            low_imag.append(b * cosine - a * sine)
        high, low = split_two(jnp.concatenate(low_real + low_imag, axis=0))
        left = jnp.concatenate([high, low, high], axis=1)
        right = jnp.concatenate([wide_ref[block, :PAIR], wide_ref[block, :PAIR], wide_ref[block, PAIR:]], axis=1)
        both = product(left, right, 1, 1)
        mains.append(both[:, :TILE])
        rims.append(both[:, TILE:])
    lane = iota((2 * tall, TILE), 1)
    coarse = jnp.concatenate(
        [
            mains[block] + jnp.where(lane < HALF, rims[(block - 1) % blocks], rims[(block + 1) % blocks])
            for block in range(blocks)
        ],
        axis=1,
    )
    high, low = split_two(coarse)
    for place, out in enumerate(outs):
        up, fine = down_ref[place, 0], down_ref[place, 1]
        for part in range(2):
            rows = slice(part * tall, (part + 1) * tall)
            value = product(up, high[rows]) + (product(fine, high[rows]) + product(up, low[rows]))
            for block in range(blocks):
                out[pl.ds(2 * block + part, long, stride=2 * blocks), :] = value[:, block * TILE : (block + 1) * TILE]


def call(kernel, outs, args, flops, scratch=(), name=None, space=pltpu.VMEM):
    held = sum(4 * leaf.size for leaf in outs) + sum(4 * arg.size for arg in args)
    return pl.pallas_call(
        kernel,
        out_shape=outs,
        in_specs=[pl.BlockSpec(memory_space=space)] * len(args),
        out_specs=[pl.BlockSpec(memory_space=pltpu.VMEM)] * len(outs),
        scratch_shapes=list(scratch),
        compiler_params=pltpu.CompilerParams(vmem_limit_bytes=VMEM_BYTES),
        cost_estimate=pl.CostEstimate(flops=flops, bytes_accessed=held, transcendentals=0),
        name=name,
    )(*args)


def bind(kernel, *settings):
    return lambda *refs: kernel(*settings, *refs)


def exchange(blocks):
    return lax.all_to_all(blocks, "clus", split_axis=0, concat_axis=0, tiled=True)


def per_device(child_patterns, theta_weights, phi_stencil, phi_weights, shift_phase, translation_table, far_list, far_vector):
    devices, halves = lax.axis_size("clus"), lax.axis_size("samp")
    children, _, own, columns = child_patterns.shape
    groups = children // OCTANTS
    rows, azimuth = theta_weights.shape[0], phi_stencil.shape[0]
    clusters, partners = far_list.shape
    vectors, width = translation_table.shape[0], 2 * translation_table.shape[3]
    blocks, rows_all = columns // TILE, groups * rows
    long, tall = children * own, OCTANTS * rows_all
    sources = 2 if halves == 2 else 3
    struct = jax.ShapeDtypeStruct
    forward = [(i, (i + 1) % halves) for i in range(halves)]
    backward = [((i + 1) % halves, i) for i in range(halves)]

    field = child_patterns.reshape(children, 2, own, blocks, TILE).transpose(0, 2, 3, 1, 4).reshape(long * blocks * 2, TILE)
    neighbours = [lax.ppermute(field, "samp", forward)]
    if sources == 3:
        neighbours.append(lax.ppermute(field, "samp", backward))

    phase = shift_phase.transpose(1, 0, 2).reshape(rows * OCTANTS, azimuth)
    table = translation_table.transpose(0, 2, 1, 3).reshape(vectors * rows * 2, width // 2)
    given = [theta_weights, phase, phi_stencil.T, phi_weights.T, far_list.T, far_vector.T, table, field]
    given = [pltpu.with_memory_space_constraint(arg, pltpu.HBM) for arg in given]
    spread = pltpu.VMEM((azimuth // TILE, rows * OCTANTS, TILE), F32)
    cosine, sine, wide, up, down, hot, factors, partial = call(
        bind(prepare_kernel, groups, sources, own),
        [
            struct((OCTANTS, rows_all, azimuth), F32),
            struct((OCTANTS, rows_all, azimuth), F32),
            struct((blocks, 2 * PAIR, PAIR), BF16),
            struct((sources, 2, tall, long), BF16),
            struct((sources, 2, long, tall), BF16),
            struct((partners * clusters, 3 * clusters + 3 * vectors), BF16),
            struct((rows, 3 * vectors, 2 * width), BF16),
            struct((2 * tall, columns), F32),
        ],
        given,
        400_000_000,
        [pltpu.VMEM(arg.shape, arg.dtype) for arg in given] + [spread, spread, pltpu.SemaphoreType.DMA((len(given),))],
        "prepare",
        pltpu.HBM,
    )
    (outgoing,) = call(
        bind(aggregate_kernel, groups, sources, own, devices),
        [struct((devices, rows_all, width), F32)],
        [*neighbours, partial, cosine, sine, wide, up],
        1_500_000_000,
        (),
        "aggregate",
    )
    arrived = exchange(outgoing)
    (translated,) = call(
        bind(translate_kernel, rows),
        [struct((clusters * rows, width), F32)],
        [hot, factors, arrived.reshape(clusters * rows, width)],
        600_000_000,
        (),
        "translate",
    )
    returned = exchange(translated.reshape(devices, rows_all, width))
    parent, *children_parts = call(
        bind(lower_kernel, groups, sources, own, devices),
        [struct((rows_all * 2 * azimuth // TILE, TILE), F32)] + [struct((long * blocks * 2, TILE), F32)] * sources,
        [returned, cosine, sine, wide, down],
        1_500_000_000,
        (),
        "lower",
    )
    total = children_parts[0] + lax.ppermute(children_parts[1], "samp", backward)
    if sources == 3:
        total = total + lax.ppermute(children_parts[2], "samp", forward)
    child_incoming = total.reshape(children, own, blocks, 2, TILE).transpose(0, 3, 1, 2, 4).reshape(children, 2, own, columns)
    parent_incoming = (
        parent.reshape(groups, rows, azimuth // TILE, 2, TILE).transpose(0, 3, 1, 2, 4).reshape(groups, 2, rows, azimuth)
    )
    return (parent_incoming, child_incoming)


def solution(mesh):
    placed = (
        P("clus", None, "samp", None),
        P(),
        P(),
        P(),
        P(None, "samp", None),
        P(None, None, "samp", "clus"),
        P(),
        P(),
    )
    return jax.shard_map(
        per_device,
        mesh=mesh,
        in_specs=placed,
        out_specs=(P("clus", None, "samp", None), P("clus", None, "samp", None)),
        check_vma=False,
    )
```

```python
import jax
import jax.numpy as jnp
from jax import lax
from jax.experimental import pallas as pl
from jax.experimental.pallas import tpu as pltpu
from jax.sharding import PartitionSpec as P

P_SIZE = 6
OCTANTS = 8
TILE = 128
PAIR = 2 * TILE
HALF = TILE // 2
VMEM_BYTES = 24 * 1024 * 1024
F32 = jnp.float32
BF16 = jnp.bfloat16

SIN_TERMS = (-1 / 6, 1 / 120, -1 / 5040, 1 / 362880, -1 / 39916800, 1 / 6227020800)
COS_TERMS = (-1 / 2, 1 / 24, -1 / 720, 1 / 40320, -1 / 3628800, 1 / 479001600, -1 / 87178291200)


def split_two(value):
    high = value.astype(BF16)
    return high, (value - high.astype(F32)).astype(BF16)


def split_three(value):
    high = value.astype(BF16)
    rest = value - high.astype(F32)
    middle = rest.astype(BF16)
    return high, middle, (rest - middle.astype(F32)).astype(BF16)


def product(left, right, left_dim=1, right_dim=0):
    return lax.dot_general(left, right, (((left_dim,), (right_dim,)), ((), ())), preferred_element_type=F32)


def product_exact(left, right, left_dim=1, right_dim=0):
    return lax.dot_general(
        left,
        right,
        (((left_dim,), (right_dim,)), ((), ())),
        preferred_element_type=F32,
        precision=lax.Precision.HIGHEST,
    )


def series(square, terms):
    total = jnp.full_like(square, terms[-1])
    for term in terms[-2::-1]:
        total = total * square + term
    return total


def iota(shape, dim):
    return lax.broadcasted_iota(jnp.int32, shape, dim)


def turned(block):
    return jnp.roll(block, HALF, axis=1)


def folded(theta, sources, own):
    below, middle, above = theta[:, :own], theta[:, own : 2 * own], theta[:, 2 * own :]
    return (middle, below + above) if sources == 2 else (middle, below, above)


def started(remote, local, sems):
    copies = [pltpu.make_async_copy(source, target, sems.at[place]) for place, (source, target) in enumerate(zip(remote, local))]
    for copy in copies:
        copy.start()
    return copies


def one_hot(flags):
    return flags.astype(F32).astype(BF16)


def halves_of(theta, sources, own):
    high, low = split_two(jnp.concatenate(folded(theta, sources, own), axis=1))
    return jnp.concatenate([high, low], axis=1)


def prepare_kernel(groups, sources, own, *refs):
    count = 5
    remote, outs, rest = refs[:count], refs[count : count + 5], refs[count + 5 :]
    local, sems = rest[:count], rest[count]
    theta_ref, phase_ref, stencil_ref, weight_ref, field_ref = local
    cos_ref, sin_ref, wide_ref, up_ref, partial_ref = outs
    copies = started(remote, local, sems)
    rows = theta_ref.shape[0]
    blocks = wide_ref.shape[0]
    tall, long = OCTANTS * groups * rows, groups * OCTANTS * own

    lengths = 2 * sources * long
    at_row = one_hot(iota((tall, rows), 0) % rows == iota((tall, rows), 1))
    column = iota((2 * sources * own, lengths), 1)
    at_own = one_hot(column // long * own + column % own == iota((2 * sources * own, lengths), 0))
    tall_id = iota((tall, long), 0)
    same = iota((tall, long), 1) // own == (tall_id // rows) % groups * OCTANTS + tall_id // (groups * rows)
    shape = (tall, 3 * OCTANTS * rows)
    place, phase_id = iota(shape, 0), iota(shape, 1) % (OCTANTS * rows)
    repeat = one_hot(place % rows * OCTANTS + place // (groups * rows) == phase_id)

    copies[0].wait()
    tall_theta = product(at_row, halves_of(theta_ref[...], sources, own)).astype(BF16)
    spread = product(tall_theta, at_own)
    for place in range(2 * sources):
        up_ref[place % sources, place // sources] = jnp.where(same, spread[:, place * long : (place + 1) * long], 0.0).astype(BF16)

    copies[1].wait()
    half = 0.5 * phase_ref[...]
    square = half * half
    sine = half + half * square * series(square, SIN_TERMS)
    cosine = 1.0 + square * series(square, COS_TERMS)
    cos_ref[...] = product(repeat, jnp.concatenate(split_three(1.0 - 2.0 * sine * sine), axis=0))
    sin_ref[...] = product(repeat, jnp.concatenate(split_three(2.0 * sine * cosine), axis=0))

    copies[2].wait()
    copies[3].wait()
    for block in range(blocks):
        columns = slice(block * PAIR, (block + 1) * PAIR)
        after, before = (block + 1) % blocks, (block - 1) % blocks
        pieces = (
            (0, TILE, block * TILE),
            (TILE, 16, after * TILE),
            (PAIR - 16, 16, before * TILE + TILE - 16),
        )
        for start, size, first in pieces:
            child = iota((size, PAIR), 0) + first
            total = jnp.zeros((size, PAIR), F32)
            for point in range(P_SIZE):
                hit = stencil_ref[point : point + 1, columns] == child
                total = jnp.where(hit, weight_ref[point : point + 1, columns], total)
            high, low = split_two(total)
            wide_ref[block, start : start + size, :] = high
            wide_ref[block, PAIR + start : PAIR + start + size, :] = low
        empty = jnp.zeros((TILE - 32, PAIR), BF16)
        wide_ref[block, TILE + 16 : PAIR - 16, :] = empty
        wide_ref[block, PAIR + TILE + 16 : 2 * PAIR - 16, :] = empty

    copies[4].wait()
    for part in range(2):
        partial_ref[part * tall : (part + 1) * tall, :] = polar(up_ref[0, 0], up_ref[0, 1], field_rows(field_ref, part, blocks, long))


def tables_kernel(groups, sources, own, *refs):
    count = 4
    remote, outs, rest = refs[:count], refs[count + 1 : count + 5], refs[count + 5 :]
    local, sems = rest[:count], rest[count]
    theta_ref, listed_ref, vector_ref, table_ref = local
    down_ref, hot_ref, even_ref, odd_ref = outs
    copies = started(remote, local, sems)
    rows = theta_ref.shape[0]
    tall, long = OCTANTS * groups * rows, groups * OCTANTS * own

    copies[0].wait()
    lengths = 2 * sources * long
    at_row = one_hot(iota((rows, tall), 1) % rows == iota((rows, tall), 0))
    column = iota((lengths, 2 * sources * own), 0)
    at_own = one_hot(column // long * own + column % own == iota((lengths, 2 * sources * own), 1))
    tall_id = iota((long, tall), 1)
    same = iota((long, tall), 0) // own == (tall_id // rows) % groups * OCTANTS + tall_id // (groups * rows)
    own_theta = product(at_own, halves_of(theta_ref[...], sources, own), 1, 1).astype(BF16)
    spread = product(own_theta, at_row)
    for place in range(2 * sources):
        down_ref[place % sources, place // sources] = jnp.where(same, spread[place * long : (place + 1) * long], 0.0).astype(BF16)

    copies[3].wait()
    raw = table_ref[...]
    many, width = raw.shape
    vectors = many // (2 * rows)
    at, row = iota((many, many), 1), iota((many, many), 0)
    order = at == row % vectors * (2 * rows) + row // (2 * vectors) * 2 + row // vectors % 2
    sorted_rows = product_exact(order.astype(F32), raw)
    lane = iota((width, 2 * width), 1)
    twice = (lane % width == iota((width, 2 * width), 0)).astype(F32)
    signed = jnp.where(lane < width, twice, -twice)
    even = product_exact(sorted_rows, twice)
    odd = product_exact(sorted_rows, signed)

    copies[1].wait()
    copies[2].wait()
    partners, clusters = listed_ref.shape
    unit = (iota((clusters, clusters), 0) == iota((clusters, clusters), 1)).astype(F32)
    listed = product_exact(unit, listed_ref[...].astype(F32), 1, 1)
    chosen = product_exact(unit, vector_ref[...].astype(F32), 1, 1)
    cluster = (iota((clusters, 3 * clusters), 1) % clusters).astype(F32)
    vector = (iota((clusters, 3 * vectors), 1) % vectors).astype(F32)
    hot_vector = []
    for partner in range(partners):
        hot_ref[partner * clusters : (partner + 1) * clusters, :] = one_hot(cluster == listed[:, partner : partner + 1])
        hot_vector.append(one_hot(vector == chosen[:, partner : partner + 1]))
    hot_vector = jnp.concatenate(hot_vector, axis=0)
    for row in range(rows):
        start = 2 * row * vectors
        columns = slice(row * 2 * width, (row + 1) * 2 * width)
        even_ref[:, columns] = product(hot_vector, jnp.concatenate(split_three(even[start : start + vectors]), axis=0))
        odd_ref[:, columns] = product(hot_vector, jnp.concatenate(split_three(odd[start + vectors : start + 2 * vectors]), axis=0))


def field_rows(field, part, blocks, long):
    return jnp.concatenate([field[pl.ds(2 * block + part, long, stride=2 * blocks), :] for block in range(blocks)], axis=1)


def polar(high_weights, low_weights, value):
    high, low = split_two(value)
    return product(high_weights, high) + (product(low_weights, high) + product(high_weights, low))


def packed_pieces(real, imag, columns):
    lane = iota((real.shape[0], TILE), 1)
    found = []
    if columns == HALF:
        for start in range(0, real.shape[1], TILE):
            a, b = real[:, start : start + TILE], imag[:, start : start + TILE]
            found.append(jnp.where(lane < HALF, a, turned(b)))
            found.append(jnp.where(lane < HALF, turned(a), b))
        return found
    for start in range(0, real.shape[1], columns):
        found.append(jnp.concatenate([real[:, start : start + columns], imag[:, start : start + columns]], axis=1))
    return found


def unpacked_pieces(read, devices, columns):
    if columns == HALF:
        real, imag = [], []
        for pair in range(devices // 2):
            a, b = read(2 * pair), read(2 * pair + 1)
            lane = iota(a.shape, 1)
            real.append(jnp.where(lane < HALF, a, turned(b)))
            imag.append(jnp.where(lane < HALF, turned(a), b))
        return jnp.concatenate(real, axis=1), jnp.concatenate(imag, axis=1)
    blocks = [read(device) for device in range(devices)]
    return (
        jnp.concatenate([block[:, :columns] for block in blocks], axis=1),
        jnp.concatenate([block[:, columns:] for block in blocks], axis=1),
    )


def aggregate_kernel(groups, sources, own, devices, *refs):
    fields = refs[: sources - 1]
    partial_ref, cos_ref, sin_ref, wide_ref, up_ref, out = refs[sources - 1 :]
    blocks = wide_ref.shape[0]
    rows_all = cos_ref.shape[0] // OCTANTS
    columns = cos_ref.shape[1] // devices
    long, tall = groups * OCTANTS * own, OCTANTS * rows_all
    refined = []
    for part in range(2):
        value = partial_ref[part * tall : (part + 1) * tall, :]
        for place, field in enumerate(fields):
            value += polar(up_ref[place + 1, 0], up_ref[place + 1, 1], field_rows(field, part, blocks, long))
        refined.append(value)
    high, low = split_two(jnp.concatenate(refined, axis=0))
    lane = iota((2 * tall, TILE), 1)

    def windows(value, block):
        main = value[:, block * TILE : (block + 1) * TILE]
        after, before = (block + 1) % blocks, (block - 1) % blocks
        rim = jnp.where(lane < HALF, value[:, after * TILE : (after + 1) * TILE], value[:, before * TILE : (before + 1) * TILE])
        return [main, rim]

    for block in range(blocks):
        one, two = windows(high, block), windows(low, block)
        left = jnp.concatenate(one + two + one, axis=1)
        right = jnp.concatenate([wide_ref[block, :PAIR], wide_ref[block, :PAIR], wide_ref[block, PAIR:]], axis=0)
        spread = product(left, right)
        real = jnp.zeros((rows_all, PAIR), F32)
        imag = jnp.zeros((rows_all, PAIR), F32)
        for octant in range(OCTANTS):
            rows = slice(octant * rows_all, (octant + 1) * rows_all)
            cosine = cos_ref[rows, block * PAIR : (block + 1) * PAIR]
            sine = sin_ref[rows, block * PAIR : (block + 1) * PAIR]
            a = spread[rows]
            b = spread[tall + octant * rows_all : tall + (octant + 1) * rows_all]
            real += a * cosine - b * sine
            imag += a * sine + b * cosine
        first = block * PAIR // columns
        for place, piece in enumerate(packed_pieces(real, imag, columns)):
            out[first + place] = piece


def translate_kernel(rows, hot_ref, even_ref, odd_ref, arrived_ref, out):
    width = arrived_ref.shape[1]
    clusters = arrived_ref.shape[0] // rows
    partners = hot_ref.shape[0] // clusters
    step = 2 if rows % 2 == 0 else 1
    for first in range(0, rows, step):
        source = jnp.concatenate(
            [arrived_ref[pl.ds(row, clusters, stride=rows), :] for row in range(first, first + step)], axis=1
        )
        gathered = product(hot_ref[...], jnp.concatenate(split_three(source), axis=0))
        columns = slice(first * width, (first + step) * width)
        direct = jnp.zeros((clusters, step * width), F32)
        crossed = jnp.zeros((clusters, step * width), F32)
        for partner in range(partners):
            part = slice(partner * clusters, (partner + 1) * clusters)
            direct += gathered[part] * even_ref[part, columns]
            crossed += gathered[part] * odd_ref[part, columns]
        for row in range(step):
            own = slice(row * width, (row + 1) * width)
            out[pl.ds(first + row, clusters, stride=rows), :] = direct[:, own] + jnp.roll(crossed[:, own], width // 2, axis=1)


def lower_kernel(groups, sources, own, devices, arrived_ref, cos_ref, sin_ref, wide_ref, down_ref, parent_ref, *outs):
    blocks = wide_ref.shape[0]
    rows_all = cos_ref.shape[0] // OCTANTS
    azimuth = cos_ref.shape[1]
    columns = azimuth // devices
    long, tall = groups * OCTANTS * own, OCTANTS * rows_all
    real, imag = unpacked_pieces(lambda device: arrived_ref[device], devices, columns)
    tiles = azimuth // TILE
    for tile in range(tiles):
        for part, value in enumerate((real, imag)):
            parent_ref[pl.ds(2 * tile + part, rows_all, stride=2 * tiles), :] = value[:, tile * TILE : (tile + 1) * TILE]
    mains, rims = [], []
    for block in range(blocks):
        part = slice(block * PAIR, (block + 1) * PAIR)
        a, b = real[:, part], imag[:, part]
        low_real, low_imag = [], []
        for octant in range(OCTANTS):
            rows = slice(octant * rows_all, (octant + 1) * rows_all)
            cosine, sine = cos_ref[rows, part], sin_ref[rows, part]
            low_real.append(a * cosine + b * sine)
            low_imag.append(b * cosine - a * sine)
        high, low = split_two(jnp.concatenate(low_real + low_imag, axis=0))
        left = jnp.concatenate([high, low, high], axis=1)
        right = jnp.concatenate([wide_ref[block, :PAIR], wide_ref[block, :PAIR], wide_ref[block, PAIR:]], axis=1)
        both = product(left, right, 1, 1)
        mains.append(both[:, :TILE])
        rims.append(both[:, TILE:])
    lane = iota((2 * tall, TILE), 1)
    coarse = jnp.concatenate(
        [
            mains[block] + jnp.where(lane < HALF, rims[(block - 1) % blocks], rims[(block + 1) % blocks])
            for block in range(blocks)
        ],
        axis=1,
    )
    high, low = split_two(coarse)
    for place, out in enumerate(outs):
        up, fine = down_ref[place, 0], down_ref[place, 1]
        for part in range(2):
            rows = slice(part * tall, (part + 1) * tall)
            value = product(up, high[rows]) + (product(fine, high[rows]) + product(up, low[rows]))
            for block in range(blocks):
                out[pl.ds(2 * block + part, long, stride=2 * blocks), :] = value[:, block * TILE : (block + 1) * TILE]


def call(kernel, outs, args, flops, name, remote=()):
    held = sum(4 * leaf.size for leaf in outs) + sum(4 * arg.size for arg in (*remote, *args))
    remote = [pltpu.with_memory_space_constraint(arg, pltpu.HBM) for arg in remote]
    scratch = [pltpu.VMEM(arg.shape, arg.dtype) for arg in remote]
    if remote:
        scratch.append(pltpu.SemaphoreType.DMA((len(remote),)))
    return pl.pallas_call(
        kernel,
        out_shape=outs,
        in_specs=[pl.BlockSpec(memory_space=pltpu.HBM)] * len(remote) + [pl.BlockSpec(memory_space=pltpu.VMEM)] * len(args),
        out_specs=[pl.BlockSpec(memory_space=pltpu.VMEM)] * len(outs),
        scratch_shapes=scratch,
        compiler_params=pltpu.CompilerParams(vmem_limit_bytes=VMEM_BYTES),
        cost_estimate=pl.CostEstimate(flops=flops, bytes_accessed=held, transcendentals=0),
        name=name,
    )(*remote, *args)


def bind(kernel, *settings):
    return lambda *refs: kernel(*settings, *refs)


def exchange(blocks):
    return lax.all_to_all(blocks, "clus", split_axis=0, concat_axis=0, tiled=True)


def per_device(child_patterns, theta_weights, phi_stencil, phi_weights, shift_phase, translation_table, far_list, far_vector):
    devices, halves = lax.axis_size("clus"), lax.axis_size("samp")
    children, _, own, columns = child_patterns.shape
    groups = children // OCTANTS
    rows, azimuth = theta_weights.shape[0], phi_stencil.shape[0]
    clusters, partners = far_list.shape
    vectors, width = translation_table.shape[0], 2 * translation_table.shape[3]
    blocks, rows_all = columns // TILE, groups * rows
    long, tall = children * own, OCTANTS * rows_all
    sources = 2 if halves == 2 else 3
    struct = jax.ShapeDtypeStruct
    forward = [(i, (i + 1) % halves) for i in range(halves)]
    backward = [((i + 1) % halves, i) for i in range(halves)]

    field = child_patterns.reshape(children, 2, own, blocks, TILE).transpose(0, 2, 3, 1, 4).reshape(long * blocks * 2, TILE)
    neighbours = [lax.ppermute(field, "samp", forward)]
    if sources == 3:
        neighbours.append(lax.ppermute(field, "samp", backward))

    phase = shift_phase.transpose(1, 0, 2).reshape(rows * OCTANTS, azimuth)
    table = translation_table.transpose(0, 2, 1, 3).reshape(vectors * rows * 2, width // 2)
    cosine, sine, wide, up, partial = call(
        bind(prepare_kernel, groups, sources, own),
        [
            struct((tall, azimuth), F32),
            struct((tall, azimuth), F32),
            struct((blocks, 2 * PAIR, PAIR), BF16),
            struct((sources, 2, tall, long), BF16),
            struct((2 * tall, columns), F32),
        ],
        [],
        400_000_000,
        "prepare",
        [theta_weights, phase, phi_stencil.T, phi_weights.T, field],
    )
    (outgoing,) = call(
        bind(aggregate_kernel, groups, sources, own, devices),
        [struct((devices, rows_all, width), F32)],
        [*neighbours, partial, cosine, sine, wide, up],
        1_500_000_000,
        "aggregate",
    )
    arrived = exchange(outgoing)
    down, hot, even, odd = call(
        bind(tables_kernel, groups, sources, own),
        [
            struct((sources, 2, long, tall), BF16),
            struct((partners * clusters, 3 * clusters), BF16),
            struct((partners * clusters, rows * width), F32),
            struct((partners * clusters, rows * width), F32),
        ],
        [outgoing],
        600_000_000,
        "tables",
        [theta_weights, far_list.T, far_vector.T, table],
    )
    (translated,) = call(
        bind(translate_kernel, rows),
        [struct((clusters * rows, width), F32)],
        [hot, even, odd, arrived.reshape(clusters * rows, width)],
        600_000_000,
        "translate",
    )
    returned = exchange(translated.reshape(devices, rows_all, width))
    parent, *children_parts = call(
        bind(lower_kernel, groups, sources, own, devices),
        [struct((rows_all * 2 * azimuth // TILE, TILE), F32)] + [struct((long * blocks * 2, TILE), F32)] * sources,
        [returned, cosine, sine, wide, down],
        1_500_000_000,
        "lower",
    )
    total = children_parts[0] + lax.ppermute(children_parts[1], "samp", backward)
    if sources == 3:
        total = total + lax.ppermute(children_parts[2], "samp", forward)
    child_incoming = total.reshape(children, own, blocks, 2, TILE).transpose(0, 3, 1, 2, 4).reshape(children, 2, own, columns)
    parent_incoming = (
        parent.reshape(groups, rows, azimuth // TILE, 2, TILE).transpose(0, 3, 1, 2, 4).reshape(groups, 2, rows, azimuth)
    )
    return (parent_incoming, child_incoming)


def solution(mesh):
    placed = (
        P("clus", None, "samp", None),
        P(),
        P(),
        P(),
        P(None, "samp", None),
        P(None, None, "samp", "clus"),
        P(),
        P(),
    )
    return jax.shard_map(
        per_device,
        mesh=mesh,
        in_specs=placed,
        out_specs=(P("clus", None, "samp", None), P("clus", None, "samp", None)),
        check_vma=False,
    )
```

```python
import jax
import jax.numpy as jnp
from jax import lax
from jax.experimental import pallas as pl
from jax.experimental.pallas import tpu as pltpu
from jax.sharding import PartitionSpec as P

P_SIZE = 6
OCTANTS = 8
TILE = 128
PAIR = 2 * TILE
HALF = TILE // 2
VMEM_BYTES = 8 * 1024 * 1024
F32 = jnp.float32
BF16 = jnp.bfloat16

SIN_TERMS = (-1 / 6, 1 / 120, -1 / 5040, 1 / 362880, -1 / 39916800, 1 / 6227020800)
COS_TERMS = (-1 / 2, 1 / 24, -1 / 720, 1 / 40320, -1 / 3628800, 1 / 479001600, -1 / 87178291200)


def split_two(value):
    high = value.astype(BF16)
    return high, (value - high.astype(F32)).astype(BF16)


def split_three(value):
    high = value.astype(BF16)
    rest = value - high.astype(F32)
    middle = rest.astype(BF16)
    return high, middle, (rest - middle.astype(F32)).astype(BF16)


def product(left, right, left_dim=1, right_dim=0):
    return lax.dot_general(left, right, (((left_dim,), (right_dim,)), ((), ())), preferred_element_type=F32)


def series(square, terms):
    total = jnp.full_like(square, terms[-1])
    for term in terms[-2::-1]:
        total = total * square + term
    return total


def iota(shape, dim):
    return lax.broadcasted_iota(jnp.int32, shape, dim)


def turned(block):
    return jnp.roll(block, HALF, axis=1)


def folded(theta, sources, own):
    below, middle, above = theta[:, :own], theta[:, own : 2 * own], theta[:, 2 * own :]
    return (middle, below + above) if sources == 2 else (middle, below, above)


def started(remote, local, sems):
    copies = [pltpu.make_async_copy(source, target, sems.at[place]) for place, (source, target) in enumerate(zip(remote, local))]
    for copy in copies:
        copy.start()
    return copies


def one_hot(flags):
    return flags.astype(F32).astype(BF16)


def halves_of(theta, sources, own):
    high, low = split_two(jnp.concatenate(folded(theta, sources, own), axis=1))
    return jnp.concatenate([high, low], axis=1)


def prepare_kernel(groups, sources, own, *refs):
    count = 5
    remote, outs, rest = refs[:count], refs[count : count + 5], refs[count + 5 :]
    local, sems = rest[:count], rest[count]
    theta_ref, phase_ref, stencil_ref, weight_ref, field_ref = local
    cos_ref, sin_ref, wide_ref, up_ref, partial_ref = outs
    copies = started(remote, local, sems)
    rows = theta_ref.shape[0]
    blocks = wide_ref.shape[0]
    tall, long = OCTANTS * groups * rows, groups * OCTANTS * own

    lengths = 2 * sources * long
    at_row = one_hot(iota((tall, rows), 0) % rows == iota((tall, rows), 1))
    column = iota((2 * sources * own, lengths), 1)
    at_own = one_hot(column // long * own + column % own == iota((2 * sources * own, lengths), 0))
    tall_id = iota((tall, long), 0)
    same = iota((tall, long), 1) // own == (tall_id // rows) % groups * OCTANTS + tall_id // (groups * rows)
    shape = (tall, 3 * OCTANTS * rows)
    place, phase_id = iota(shape, 0), iota(shape, 1) % (OCTANTS * rows)
    repeat = one_hot(place % rows * OCTANTS + place // (groups * rows) == phase_id)

    copies[0].wait()
    tall_theta = product(at_row, halves_of(theta_ref[...], sources, own)).astype(BF16)
    spread = product(tall_theta, at_own)
    for place in range(2 * sources):
        up_ref[place % sources, place // sources] = jnp.where(same, spread[:, place * long : (place + 1) * long], 0.0).astype(BF16)

    copies[1].wait()
    half = 0.5 * phase_ref[...]
    square = half * half
    sine = half + half * square * series(square, SIN_TERMS)
    cosine = 1.0 + square * series(square, COS_TERMS)
    cos_ref[...] = product(repeat, jnp.concatenate(split_three(1.0 - 2.0 * sine * sine), axis=0))
    sin_ref[...] = product(repeat, jnp.concatenate(split_three(2.0 * sine * cosine), axis=0))

    copies[2].wait()
    copies[3].wait()
    for block in range(blocks):
        columns = slice(block * PAIR, (block + 1) * PAIR)
        after, before = (block + 1) % blocks, (block - 1) % blocks
        pieces = (
            (0, TILE, block * TILE),
            (TILE, 16, after * TILE),
            (PAIR - 16, 16, before * TILE + TILE - 16),
        )
        for start, size, first in pieces:
            child = iota((size, PAIR), 0) + first
            total = jnp.zeros((size, PAIR), F32)
            for point in range(P_SIZE):
                hit = stencil_ref[point : point + 1, columns] == child
                total = jnp.where(hit, weight_ref[point : point + 1, columns], total)
            high, low = split_two(total)
            wide_ref[block, start : start + size, :] = high
            wide_ref[block, PAIR + start : PAIR + start + size, :] = low
        empty = jnp.zeros((TILE - 32, PAIR), BF16)
        wide_ref[block, TILE + 16 : PAIR - 16, :] = empty
        wide_ref[block, PAIR + TILE + 16 : 2 * PAIR - 16, :] = empty

    copies[4].wait()
    for part in range(2):
        partial_ref[part * tall : (part + 1) * tall, :] = polar(up_ref[0, 0], up_ref[0, 1], field_rows(field_ref, part, blocks, long))


def tables_kernel(groups, sources, own, *refs):
    count = 4
    remote, outs, rest = refs[:count], refs[count + 1 : count + 4], refs[count + 4 :]
    local, sems = rest[:count], rest[count]
    theta_ref, listed_ref, vector_ref, table_ref = local
    down_ref, hot_ref, table_out = outs
    copies = started(remote, local, sems)
    rows = theta_ref.shape[0]
    tall, long = OCTANTS * groups * rows, groups * OCTANTS * own

    copies[0].wait()
    lengths = 2 * sources * long
    at_row = one_hot(iota((rows, tall), 1) % rows == iota((rows, tall), 0))
    column = iota((lengths, 2 * sources * own), 0)
    at_own = one_hot(column // long * own + column % own == iota((lengths, 2 * sources * own), 1))
    tall_id = iota((long, tall), 1)
    same = iota((long, tall), 0) // own == (tall_id // rows) % groups * OCTANTS + tall_id // (groups * rows)
    own_theta = product(at_own, halves_of(theta_ref[...], sources, own), 1, 1).astype(BF16)
    spread = product(own_theta, at_row)
    for place in range(2 * sources):
        down_ref[place % sources, place // sources] = jnp.where(same, spread[place * long : (place + 1) * long], 0.0).astype(BF16)

    copies[3].wait()
    raw = table_ref[...]
    many, width = raw.shape
    vectors = many // (2 * rows)
    at, place = iota((many, many), 1), iota((many, many), 0)
    order = one_hot(at == place % vectors * (2 * rows) + place // (2 * vectors) * 2 + place // vectors % 2)
    lane, source = iota((width, 4 * width), 1), iota((width, 4 * width), 0)
    twice = jnp.where(lane % width == source, jnp.where(lane < 3 * width, 1.0, -1.0), 0.0).astype(BF16)
    for piece, part in enumerate(split_three(raw)):
        wide = product(product(order, part).astype(BF16), twice).astype(BF16)
        for row in range(rows):
            start = 2 * row * vectors
            target = slice(piece * vectors, (piece + 1) * vectors)
            table_out[row, target, : 2 * width] = wide[start : start + vectors, : 2 * width]
            table_out[row, target, 2 * width :] = wide[start + vectors : start + 2 * vectors, 2 * width :]

    copies[1].wait()
    copies[2].wait()
    partners, clusters = listed_ref.shape
    unit = one_hot(iota((clusters, clusters), 0) == iota((clusters, clusters), 1))
    listed = sum(product(unit, half, 1, 1) for half in split_two(listed_ref[...].astype(F32)))
    chosen = sum(product(unit, half, 1, 1) for half in split_two(vector_ref[...].astype(F32)))
    cluster = (iota((clusters, 3 * clusters), 1) % clusters).astype(F32)
    vector = (iota((clusters, 3 * vectors), 1) % vectors).astype(F32)
    for partner in range(partners):
        part = slice(partner * clusters, (partner + 1) * clusters)
        hot_ref[part, : 3 * clusters] = one_hot(cluster == listed[:, partner : partner + 1])
        hot_ref[part, 3 * clusters :] = one_hot(vector == chosen[:, partner : partner + 1])


def field_rows(field, part, blocks, long):
    return jnp.concatenate([field[pl.ds(2 * block + part, long, stride=2 * blocks), :] for block in range(blocks)], axis=1)


def polar(high_weights, low_weights, value):
    high, low = split_two(value)
    return product(high_weights, high) + (product(low_weights, high) + product(high_weights, low))


def packed_pieces(real, imag, columns):
    lane = iota((real.shape[0], TILE), 1)
    found = []
    if columns == HALF:
        for start in range(0, real.shape[1], TILE):
            a, b = real[:, start : start + TILE], imag[:, start : start + TILE]
            found.append(jnp.where(lane < HALF, a, turned(b)))
            found.append(jnp.where(lane < HALF, turned(a), b))
        return found
    for start in range(0, real.shape[1], columns):
        found.append(jnp.concatenate([real[:, start : start + columns], imag[:, start : start + columns]], axis=1))
    return found


def unpacked_pieces(read, devices, columns):
    if columns == HALF:
        real, imag = [], []
        for pair in range(devices // 2):
            a, b = read(2 * pair), read(2 * pair + 1)
            lane = iota(a.shape, 1)
            real.append(jnp.where(lane < HALF, a, turned(b)))
            imag.append(jnp.where(lane < HALF, turned(a), b))
        return jnp.concatenate(real, axis=1), jnp.concatenate(imag, axis=1)
    blocks = [read(device) for device in range(devices)]
    return (
        jnp.concatenate([block[:, :columns] for block in blocks], axis=1),
        jnp.concatenate([block[:, columns:] for block in blocks], axis=1),
    )


def aggregate_kernel(groups, sources, own, devices, *refs):
    fields = refs[: sources - 1]
    partial_ref, cos_ref, sin_ref, wide_ref, up_ref, out = refs[sources - 1 :]
    blocks = wide_ref.shape[0]
    rows_all = cos_ref.shape[0] // OCTANTS
    columns = cos_ref.shape[1] // devices
    long, tall = groups * OCTANTS * own, OCTANTS * rows_all
    refined = []
    for part in range(2):
        value = partial_ref[part * tall : (part + 1) * tall, :]
        for place, field in enumerate(fields):
            value += polar(up_ref[place + 1, 0], up_ref[place + 1, 1], field_rows(field, part, blocks, long))
        refined.append(value)
    high, low = split_two(jnp.concatenate(refined, axis=0))
    lane = iota((2 * tall, TILE), 1)

    def windows(value, block):
        main = value[:, block * TILE : (block + 1) * TILE]
        after, before = (block + 1) % blocks, (block - 1) % blocks
        rim = jnp.where(lane < HALF, value[:, after * TILE : (after + 1) * TILE], value[:, before * TILE : (before + 1) * TILE])
        return [main, rim]

    for block in range(blocks):
        one, two = windows(high, block), windows(low, block)
        left = jnp.concatenate(one + two + one, axis=1)
        right = jnp.concatenate([wide_ref[block, :PAIR], wide_ref[block, :PAIR], wide_ref[block, PAIR:]], axis=0)
        spread = product(left, right)
        real = jnp.zeros((rows_all, PAIR), F32)
        imag = jnp.zeros((rows_all, PAIR), F32)
        for octant in range(OCTANTS):
            rows = slice(octant * rows_all, (octant + 1) * rows_all)
            cosine = cos_ref[rows, block * PAIR : (block + 1) * PAIR]
            sine = sin_ref[rows, block * PAIR : (block + 1) * PAIR]
            a = spread[rows]
            b = spread[tall + octant * rows_all : tall + (octant + 1) * rows_all]
            real += a * cosine - b * sine
            imag += a * sine + b * cosine
        first = block * PAIR // columns
        for place, piece in enumerate(packed_pieces(real, imag, columns)):
            out[first + place] = piece


def translate_kernel(rows, hot_ref, table_ref, arrived_ref, out):
    width = arrived_ref.shape[1]
    clusters = arrived_ref.shape[0] // rows
    partners = hot_ref.shape[0] // clusters
    hot_cluster = hot_ref[:, : 3 * clusters]
    hot_vector = hot_ref[:, 3 * clusters :]
    step = 2 if rows % 2 == 0 else 1
    for first in range(0, rows, step):
        source = jnp.concatenate(
            [arrived_ref[pl.ds(row, clusters, stride=rows), :] for row in range(first, first + step)], axis=1
        )
        gathered = product(hot_cluster, jnp.concatenate(split_three(source), axis=0))
        for row in range(first, first + step):
            factors = product(hot_vector, table_ref[row])
            direct = jnp.zeros((clusters, width), F32)
            crossed = jnp.zeros((clusters, width), F32)
            for partner in range(partners):
                part = slice(partner * clusters, (partner + 1) * clusters)
                value = gathered[part, (row - first) * width : (row - first + 1) * width]
                direct += value * factors[part, :width]
                crossed += value * factors[part, width:]
            out[pl.ds(row, clusters, stride=rows), :] = direct + jnp.roll(crossed, width // 2, axis=1)


def lower_kernel(groups, sources, own, devices, arrived_ref, cos_ref, sin_ref, wide_ref, down_ref, parent_ref, *outs):
    blocks = wide_ref.shape[0]
    rows_all = cos_ref.shape[0] // OCTANTS
    azimuth = cos_ref.shape[1]
    columns = azimuth // devices
    long, tall = groups * OCTANTS * own, OCTANTS * rows_all
    real, imag = unpacked_pieces(lambda device: arrived_ref[device], devices, columns)
    tiles = azimuth // TILE
    for tile in range(tiles):
        for part, value in enumerate((real, imag)):
            parent_ref[pl.ds(2 * tile + part, rows_all, stride=2 * tiles), :] = value[:, tile * TILE : (tile + 1) * TILE]
    mains, rims = [], []
    for block in range(blocks):
        part = slice(block * PAIR, (block + 1) * PAIR)
        a, b = real[:, part], imag[:, part]
        low_real, low_imag = [], []
        for octant in range(OCTANTS):
            rows = slice(octant * rows_all, (octant + 1) * rows_all)
            cosine, sine = cos_ref[rows, part], sin_ref[rows, part]
            low_real.append(a * cosine + b * sine)
            low_imag.append(b * cosine - a * sine)
        high, low = split_two(jnp.concatenate(low_real + low_imag, axis=0))
        left = jnp.concatenate([high, low, high], axis=1)
        right = jnp.concatenate([wide_ref[block, :PAIR], wide_ref[block, :PAIR], wide_ref[block, PAIR:]], axis=1)
        both = product(left, right, 1, 1)
        mains.append(both[:, :TILE])
        rims.append(both[:, TILE:])
    lane = iota((2 * tall, TILE), 1)
    coarse = jnp.concatenate(
        [
            mains[block] + jnp.where(lane < HALF, rims[(block - 1) % blocks], rims[(block + 1) % blocks])
            for block in range(blocks)
        ],
        axis=1,
    )
    high, low = split_two(coarse)
    for place, out in enumerate(outs):
        up, fine = down_ref[place, 0], down_ref[place, 1]
        for part in range(2):
            rows = slice(part * tall, (part + 1) * tall)
            value = product(up, high[rows]) + (product(fine, high[rows]) + product(up, low[rows]))
            for block in range(blocks):
                out[pl.ds(2 * block + part, long, stride=2 * blocks), :] = value[:, block * TILE : (block + 1) * TILE]


def call(kernel, outs, args, flops, name, remote=()):
    held = sum(4 * leaf.size for leaf in outs) + sum(4 * arg.size for arg in (*remote, *args))
    remote = [pltpu.with_memory_space_constraint(arg, pltpu.HBM) for arg in remote]
    scratch = [pltpu.VMEM(arg.shape, arg.dtype) for arg in remote]
    if remote:
        scratch.append(pltpu.SemaphoreType.DMA((len(remote),)))
    return pl.pallas_call(
        kernel,
        out_shape=outs,
        in_specs=[pl.BlockSpec(memory_space=pltpu.HBM)] * len(remote) + [pl.BlockSpec(memory_space=pltpu.VMEM)] * len(args),
        out_specs=[pl.BlockSpec(memory_space=pltpu.VMEM)] * len(outs),
        scratch_shapes=scratch,
        compiler_params=pltpu.CompilerParams(vmem_limit_bytes=max(VMEM_BYTES, 8 * max(arg.size for arg in (*remote, *args)))),
        cost_estimate=pl.CostEstimate(flops=flops, bytes_accessed=held, transcendentals=0),
        name=name,
    )(*remote, *args)


def bind(kernel, *settings):
    return lambda *refs: kernel(*settings, *refs)


def exchange(blocks):
    return lax.all_to_all(blocks, "clus", split_axis=0, concat_axis=0, tiled=True)


def per_device(child_patterns, theta_weights, phi_stencil, phi_weights, shift_phase, translation_table, far_list, far_vector):
    devices, halves = lax.axis_size("clus"), lax.axis_size("samp")
    children, _, own, columns = child_patterns.shape
    groups = children // OCTANTS
    rows, azimuth = theta_weights.shape[0], phi_stencil.shape[0]
    clusters, partners = far_list.shape
    vectors, width = translation_table.shape[0], 2 * translation_table.shape[3]
    blocks, rows_all = columns // TILE, groups * rows
    long, tall = children * own, OCTANTS * rows_all
    sources = 2 if halves == 2 else 3
    struct = jax.ShapeDtypeStruct
    forward = [(i, (i + 1) % halves) for i in range(halves)]
    backward = [((i + 1) % halves, i) for i in range(halves)]

    field = child_patterns.reshape(children, 2, own, blocks, TILE).transpose(0, 2, 3, 1, 4).reshape(long * blocks * 2, TILE)
    neighbours = [lax.ppermute(field, "samp", forward)]
    if sources == 3:
        neighbours.append(lax.ppermute(field, "samp", backward))

    phase = shift_phase.transpose(1, 0, 2).reshape(rows * OCTANTS, azimuth)
    table = translation_table.transpose(0, 2, 1, 3).reshape(vectors * rows * 2, width // 2)
    cosine, sine, wide, up, partial = call(
        bind(prepare_kernel, groups, sources, own),
        [
            struct((tall, azimuth), F32),
            struct((tall, azimuth), F32),
            struct((blocks, 2 * PAIR, PAIR), BF16),
            struct((sources, 2, tall, long), BF16),
            struct((2 * tall, columns), F32),
        ],
        [],
        400_000_000,
        "prepare",
        [theta_weights, phase, phi_stencil.T, phi_weights.T, field],
    )
    (outgoing,) = call(
        bind(aggregate_kernel, groups, sources, own, devices),
        [struct((devices, rows_all, width), F32)],
        [*neighbours, partial, cosine, sine, wide, up],
        1_500_000_000,
        "aggregate",
    )
    arrived = exchange(outgoing)
    down, hot, factors = call(
        bind(tables_kernel, groups, sources, own),
        [
            struct((sources, 2, long, tall), BF16),
            struct((partners * clusters, 3 * clusters + 3 * vectors), BF16),
            struct((rows, 3 * vectors, 2 * width), BF16),
        ],
        [outgoing],
        600_000_000,
        "tables",
        [theta_weights, far_list.T, far_vector.T, table],
    )
    (translated,) = call(
        bind(translate_kernel, rows),
        [struct((clusters * rows, width), F32)],
        [hot, factors, arrived.reshape(clusters * rows, width)],
        600_000_000,
        "translate",
    )
    returned = exchange(translated.reshape(devices, rows_all, width))
    parent, *children_parts = call(
        bind(lower_kernel, groups, sources, own, devices),
        [struct((rows_all * 2 * azimuth // TILE, TILE), F32)] + [struct((long * blocks * 2, TILE), F32)] * sources,
        [returned, cosine, sine, wide, down],
        1_500_000_000,
        "lower",
    )
    total = children_parts[0] + lax.ppermute(children_parts[1], "samp", backward)
    if sources == 3:
        total = total + lax.ppermute(children_parts[2], "samp", forward)
    child_incoming = total.reshape(children, own, blocks, 2, TILE).transpose(0, 3, 1, 2, 4).reshape(children, 2, own, columns)
    parent_incoming = (
        parent.reshape(groups, rows, azimuth // TILE, 2, TILE).transpose(0, 3, 1, 2, 4).reshape(groups, 2, rows, azimuth)
    )
    return (parent_incoming, child_incoming)


def solution(mesh):
    placed = (
        P("clus", None, "samp", None),
        P(),
        P(),
        P(),
        P(None, "samp", None),
        P(None, None, "samp", "clus"),
        P(),
        P(),
    )
    return jax.shard_map(
        per_device,
        mesh=mesh,
        in_specs=placed,
        out_specs=(P("clus", None, "samp", None), P("clus", None, "samp", None)),
        check_vma=False,
    )
```

```python
import jax
import jax.numpy as jnp
from jax import lax
from jax.experimental import pallas as pl
from jax.experimental.pallas import tpu as pltpu
from jax.sharding import PartitionSpec as P

P_SIZE = 6
OCTANTS = 8
TILE = 128
PAIR = 2 * TILE
HALF = TILE // 2
VMEM_BYTES = 8 * 1024 * 1024
F32 = jnp.float32
BF16 = jnp.bfloat16

SIN_TERMS = (-1 / 6, 1 / 120, -1 / 5040, 1 / 362880, -1 / 39916800, 1 / 6227020800)
COS_TERMS = (-1 / 2, 1 / 24, -1 / 720, 1 / 40320, -1 / 3628800, 1 / 479001600, -1 / 87178291200)


def split_two(value):
    high = value.astype(BF16)
    return high, (value - high.astype(F32)).astype(BF16)


def split_three(value):
    high = value.astype(BF16)
    rest = value - high.astype(F32)
    middle = rest.astype(BF16)
    return high, middle, (rest - middle.astype(F32)).astype(BF16)


def product(left, right, left_dim=1, right_dim=0):
    return lax.dot_general(left, right, (((left_dim,), (right_dim,)), ((), ())), preferred_element_type=F32)


def series(square, terms):
    total = jnp.full_like(square, terms[-1])
    for term in terms[-2::-1]:
        total = total * square + term
    return total


def iota(shape, dim):
    return lax.broadcasted_iota(jnp.int32, shape, dim)


def turned(block):
    return jnp.roll(block, HALF, axis=1)


def folded(theta, sources, own):
    below, middle, above = theta[:, :own], theta[:, own : 2 * own], theta[:, 2 * own :]
    return (middle, below + above) if sources == 2 else (middle, below, above)


def started(remote, local, sems):
    copies = [pltpu.make_async_copy(source, target, sems.at[place]) for place, (source, target) in enumerate(zip(remote, local))]
    for copy in copies:
        copy.start()
    return copies


def one_hot(flags):
    return flags.astype(F32).astype(BF16)


def halves_of(theta, sources, own):
    high, low = split_two(jnp.concatenate(folded(theta, sources, own), axis=1))
    return jnp.concatenate([high, low], axis=1)


def turns(phase, groups, rows):
    tall = OCTANTS * groups * rows
    shape = (tall, 3 * OCTANTS * rows)
    place, phase_id = iota(shape, 0), iota(shape, 1) % (OCTANTS * rows)
    repeat = one_hot(place % rows * OCTANTS + place // (groups * rows) == phase_id)
    half = 0.5 * phase
    square = half * half
    sine = half + half * square * series(square, SIN_TERMS)
    cosine = 1.0 + square * series(square, COS_TERMS)
    return [
        product(repeat, jnp.concatenate(split_three(value), axis=0)) for value in (1.0 - 2.0 * sine * sine, 2.0 * sine * cosine)
    ]


def prepare_kernel(groups, sources, own, *refs):
    count = 5
    remote, outs, rest = refs[:count], refs[count : count + 5], refs[count + 5 :]
    local, sems = rest[:count], rest[count]
    theta_ref, phase_ref, stencil_ref, weight_ref, field_ref = local
    cos_ref, sin_ref, wide_ref, up_ref, partial_ref = outs
    copies = started(remote, local, sems)
    rows = theta_ref.shape[0]
    blocks = wide_ref.shape[0]
    tall, long = OCTANTS * groups * rows, groups * OCTANTS * own

    lengths = 2 * sources * long
    at_row = one_hot(iota((tall, rows), 0) % rows == iota((tall, rows), 1))
    column = iota((2 * sources * own, lengths), 1)
    at_own = one_hot(column // long * own + column % own == iota((2 * sources * own, lengths), 0))
    tall_id = iota((tall, long), 0)
    same = iota((tall, long), 1) // own == (tall_id // rows) % groups * OCTANTS + tall_id // (groups * rows)

    copies[0].wait()
    tall_theta = product(at_row, halves_of(theta_ref[...], sources, own)).astype(BF16)
    spread = product(tall_theta, at_own)
    for place in range(2 * sources):
        up_ref[place % sources, place // sources] = jnp.where(same, spread[:, place * long : (place + 1) * long], 0.0).astype(BF16)

    copies[1].wait()
    cos_ref[...], sin_ref[...] = turns(phase_ref[...], groups, rows)

    copies[2].wait()
    copies[3].wait()
    for block in range(blocks):
        columns = slice(block * PAIR, (block + 1) * PAIR)
        after, before = (block + 1) % blocks, (block - 1) % blocks
        pieces = (
            (0, TILE, block * TILE),
            (TILE, 16, after * TILE),
            (PAIR - 16, 16, before * TILE + TILE - 16),
        )
        for start, size, first in pieces:
            child = iota((size, PAIR), 0) + first
            total = jnp.zeros((size, PAIR), F32)
            for point in range(P_SIZE):
                hit = stencil_ref[point : point + 1, columns] == child
                total = jnp.where(hit, weight_ref[point : point + 1, columns], total)
            high, low = split_two(total)
            wide_ref[block, start : start + size, :] = high
            wide_ref[block, PAIR + start : PAIR + start + size, :] = low
        empty = jnp.zeros((TILE - 32, PAIR), BF16)
        wide_ref[block, TILE + 16 : PAIR - 16, :] = empty
        wide_ref[block, PAIR + TILE + 16 : 2 * PAIR - 16, :] = empty

    copies[4].wait()
    for part in range(2):
        partial_ref[part * tall : (part + 1) * tall, :] = polar(up_ref[0, 0], up_ref[0, 1], field_rows(field_ref, part, blocks, long))


def tables_kernel(groups, sources, own, *refs):
    count = 4
    remote, phases = refs[:count], refs[count : count + sources - 1]
    outs = refs[count + sources : -count - 1]
    local, sems = refs[-count - 1 : -1], refs[-1]
    theta_ref, listed_ref, vector_ref, table_ref = local
    down_ref, hot_ref, table_out, *turned_refs = outs
    copies = started(remote, local, sems)
    rows = theta_ref.shape[0]
    tall, long = OCTANTS * groups * rows, groups * OCTANTS * own

    copies[0].wait()
    lengths = 2 * sources * long
    at_row = one_hot(iota((rows, tall), 1) % rows == iota((rows, tall), 0))
    column = iota((lengths, 2 * sources * own), 0)
    at_own = one_hot(column // long * own + column % own == iota((lengths, 2 * sources * own), 1))
    tall_id = iota((long, tall), 1)
    same = iota((long, tall), 0) // own == (tall_id // rows) % groups * OCTANTS + tall_id // (groups * rows)
    own_theta = product(at_own, halves_of(theta_ref[...], sources, own), 1, 1).astype(BF16)
    spread = product(own_theta, at_row)
    for place in range(2 * sources):
        down_ref[place % sources, place // sources] = jnp.where(same, spread[place * long : (place + 1) * long], 0.0).astype(BF16)

    copies[3].wait()
    raw = table_ref[...]
    many, width = raw.shape
    vectors = many // (2 * rows)
    at, place = iota((many, many), 1), iota((many, many), 0)
    order = one_hot(at == place % vectors * (2 * rows) + place // (2 * vectors) * 2 + place // vectors % 2)
    lane, source = iota((width, 4 * width), 1), iota((width, 4 * width), 0)
    twice = jnp.where(lane % width == source, jnp.where(lane < 3 * width, 1.0, -1.0), 0.0).astype(BF16)
    for piece, part in enumerate(split_three(raw)):
        wide = product(product(order, part).astype(BF16), twice).astype(BF16)
        for row in range(rows):
            start = 2 * row * vectors
            target = slice(piece * vectors, (piece + 1) * vectors)
            table_out[row, target, : 2 * width] = wide[start : start + vectors, : 2 * width]
            table_out[row, target, 2 * width :] = wide[start + vectors : start + 2 * vectors, 2 * width :]

    copies[1].wait()
    copies[2].wait()
    partners, clusters = listed_ref.shape
    unit = one_hot(iota((clusters, clusters), 0) == iota((clusters, clusters), 1))
    listed = sum(product(unit, half, 1, 1) for half in split_two(listed_ref[...].astype(F32)))
    chosen = sum(product(unit, half, 1, 1) for half in split_two(vector_ref[...].astype(F32)))
    cluster = (iota((clusters, 3 * clusters), 1) % clusters).astype(F32)
    vector = (iota((clusters, 3 * vectors), 1) % vectors).astype(F32)
    for partner in range(partners):
        part = slice(partner * clusters, (partner + 1) * clusters)
        hot_ref[part, : 3 * clusters] = one_hot(cluster == listed[:, partner : partner + 1])
        hot_ref[part, 3 * clusters :] = one_hot(vector == chosen[:, partner : partner + 1])

    for place, phase in enumerate(phases):
        turned_refs[2 * place][...], turned_refs[2 * place + 1][...] = turns(phase[...], groups, rows)


def field_rows(field, part, blocks, long):
    return jnp.concatenate([field[pl.ds(2 * block + part, long, stride=2 * blocks), :] for block in range(blocks)], axis=1)


def polar(high_weights, low_weights, value):
    high, low = split_two(value)
    return product(high_weights, high) + (product(low_weights, high) + product(high_weights, low))


def packed_pieces(real, imag, columns):
    lane = iota((real.shape[0], TILE), 1)
    found = []
    if columns == HALF:
        for start in range(0, real.shape[1], TILE):
            a, b = real[:, start : start + TILE], imag[:, start : start + TILE]
            found.append(jnp.where(lane < HALF, a, turned(b)))
            found.append(jnp.where(lane < HALF, turned(a), b))
        return found
    for start in range(0, real.shape[1], columns):
        found.append(jnp.concatenate([real[:, start : start + columns], imag[:, start : start + columns]], axis=1))
    return found


def unpacked_pieces(read, devices, columns):
    if columns == HALF:
        real, imag = [], []
        for pair in range(devices // 2):
            a, b = read(2 * pair), read(2 * pair + 1)
            lane = iota(a.shape, 1)
            real.append(jnp.where(lane < HALF, a, turned(b)))
            imag.append(jnp.where(lane < HALF, turned(a), b))
        return jnp.concatenate(real, axis=1), jnp.concatenate(imag, axis=1)
    blocks = [read(device) for device in range(devices)]
    return (
        jnp.concatenate([block[:, :columns] for block in blocks], axis=1),
        jnp.concatenate([block[:, columns:] for block in blocks], axis=1),
    )


def aggregate_kernel(groups, sources, own, devices, *refs):
    fields = refs[: sources - 1]
    partial_ref, cos_ref, sin_ref, wide_ref, up_ref, out, ready, sems = refs[sources - 1 :]
    blocks = wide_ref.shape[0]
    rows_all = cos_ref.shape[0] // OCTANTS
    columns = cos_ref.shape[1] // devices
    long, tall = groups * OCTANTS * own, OCTANTS * rows_all
    refined = []
    for part in range(2):
        value = partial_ref[part * tall : (part + 1) * tall, :]
        for place, field in enumerate(fields):
            value += polar(up_ref[place + 1, 0], up_ref[place + 1, 1], field_rows(field, part, blocks, long))
        refined.append(value)
    high, low = split_two(jnp.concatenate(refined, axis=0))
    lane = iota((2 * tall, TILE), 1)

    def windows(value, block):
        main = value[:, block * TILE : (block + 1) * TILE]
        after, before = (block + 1) % blocks, (block - 1) % blocks
        rim = jnp.where(lane < HALF, value[:, after * TILE : (after + 1) * TILE], value[:, before * TILE : (before + 1) * TILE])
        return [main, rim]

    copies = []
    for block in range(blocks):
        one, two = windows(high, block), windows(low, block)
        left = jnp.concatenate(one + two + one, axis=1)
        right = jnp.concatenate([wide_ref[block, :PAIR], wide_ref[block, :PAIR], wide_ref[block, PAIR:]], axis=0)
        spread = product(left, right)
        real = jnp.zeros((rows_all, PAIR), F32)
        imag = jnp.zeros((rows_all, PAIR), F32)
        for octant in range(OCTANTS):
            rows = slice(octant * rows_all, (octant + 1) * rows_all)
            cosine = cos_ref[rows, block * PAIR : (block + 1) * PAIR]
            sine = sin_ref[rows, block * PAIR : (block + 1) * PAIR]
            a = spread[rows]
            b = spread[tall + octant * rows_all : tall + (octant + 1) * rows_all]
            real += a * cosine - b * sine
            imag += a * sine + b * cosine
        first, many = block * PAIR // columns, PAIR // columns
        for place, piece in enumerate(packed_pieces(real, imag, columns)):
            ready[first + place] = piece
        copies.append(pltpu.make_async_copy(ready.at[first : first + many], out.at[first : first + many], sems.at[block]))
        copies[-1].start()
    for copy in copies:
        copy.wait()


def translate_kernel(rows, hot_ref, table_ref, arrived_ref, out):
    width = arrived_ref.shape[1]
    clusters = arrived_ref.shape[0] // rows
    partners = hot_ref.shape[0] // clusters
    hot_cluster = hot_ref[:, : 3 * clusters]
    hot_vector = hot_ref[:, 3 * clusters :]
    step = 2 if rows % 2 == 0 else 1
    for first in range(0, rows, step):
        source = jnp.concatenate(
            [arrived_ref[pl.ds(row, clusters, stride=rows), :] for row in range(first, first + step)], axis=1
        )
        gathered = product(hot_cluster, jnp.concatenate(split_three(source), axis=0))
        for row in range(first, first + step):
            factors = product(hot_vector, table_ref[row])
            direct = jnp.zeros((clusters, width), F32)
            crossed = jnp.zeros((clusters, width), F32)
            for partner in range(partners):
                part = slice(partner * clusters, (partner + 1) * clusters)
                value = gathered[part, (row - first) * width : (row - first + 1) * width]
                direct += value * factors[part, :width]
                crossed += value * factors[part, width:]
            out[pl.ds(row, clusters, stride=rows), :] = direct + jnp.roll(crossed, width // 2, axis=1)


def coarse_columns(real, imag, cos_ref, sin_ref, wide_ref):
    blocks = wide_ref.shape[0]
    rows_all = cos_ref.shape[0] // OCTANTS
    mains, rims = [], []
    for block in range(blocks):
        part = slice(block * PAIR, (block + 1) * PAIR)
        a, b = real[:, part], imag[:, part]
        low_real, low_imag = [], []
        for octant in range(OCTANTS):
            rows = slice(octant * rows_all, (octant + 1) * rows_all)
            cosine, sine = cos_ref[rows, part], sin_ref[rows, part]
            low_real.append(a * cosine + b * sine)
            low_imag.append(b * cosine - a * sine)
        high, low = split_two(jnp.concatenate(low_real + low_imag, axis=0))
        left = jnp.concatenate([high, low, high], axis=1)
        right = jnp.concatenate([wide_ref[block, :PAIR], wide_ref[block, :PAIR], wide_ref[block, PAIR:]], axis=1)
        both = product(left, right, 1, 1)
        mains.append(both[:, :TILE])
        rims.append(both[:, TILE:])
    lane = iota((2 * OCTANTS * rows_all, TILE), 1)
    return jnp.concatenate(
        [
            mains[block] + jnp.where(lane < HALF, rims[(block - 1) % blocks], rims[(block + 1) % blocks])
            for block in range(blocks)
        ],
        axis=1,
    )


def lower_kernel(devices, arrived_ref, cos_ref, sin_ref, wide_ref, down_ref, parent_out, partial_ref, parent_ref, sem):
    rows_all = cos_ref.shape[0] // OCTANTS
    azimuth = cos_ref.shape[1]
    long, tall = down_ref.shape[2:]
    real, imag = unpacked_pieces(lambda device: arrived_ref[device], devices, azimuth // devices)
    tiles = azimuth // TILE
    for tile in range(tiles):
        for part, value in enumerate((real, imag)):
            parent_ref[pl.ds(2 * tile + part, rows_all, stride=2 * tiles), :] = value[:, tile * TILE : (tile + 1) * TILE]
    copy = pltpu.make_async_copy(parent_ref, parent_out, sem)
    copy.start()
    coarse = coarse_columns(real, imag, cos_ref, sin_ref, wide_ref)
    for part in range(2):
        partial_ref[part * long : (part + 1) * long, :] = polar(down_ref[0, 0], down_ref[0, 1], coarse[part * tall : (part + 1) * tall])
    copy.wait()


def finish_kernel(devices, sources, *refs):
    arrived = refs[: sources - 1]
    turned_refs = refs[sources - 1 : 3 * (sources - 1)]
    wide_ref, down_ref, partial_ref, out, ready, sems = refs[3 * (sources - 1) :]
    blocks = wide_ref.shape[0]
    azimuth = turned_refs[0].shape[1]
    long, tall = down_ref.shape[2:]
    coarse = []
    for place, field in enumerate(arrived):
        real, imag = unpacked_pieces(lambda device: field[device], devices, azimuth // devices)
        coarse.append(split_two(coarse_columns(real, imag, turned_refs[2 * place], turned_refs[2 * place + 1], wide_ref)))
    copies = []
    size = long // 2
    for first in range(0, long, size):
        rows = slice(first, first + size)
        for part in range(2):
            value = partial_ref[part * long + first : part * long + first + size, :]
            for place, (high, low) in enumerate(coarse):
                source = slice(part * tall, (part + 1) * tall)
                up, fine = down_ref[place + 1, 0, rows], down_ref[place + 1, 1, rows]
                value += product(up, high[source]) + (product(fine, high[source]) + product(up, low[source]))
            for block in range(blocks):
                start = 2 * blocks * first + 2 * block + part
                ready[pl.ds(start, size, stride=2 * blocks), :] = value[:, block * TILE : (block + 1) * TILE]
        whole = slice(2 * blocks * first, 2 * blocks * (first + size))
        copies.append(pltpu.make_async_copy(ready.at[whole], out.at[whole], sems.at[len(copies)]))
        copies[-1].start()
    for copy in copies:
        copy.wait()


def call(kernel, outs, args, flops, name, remote=(), after=(), far=(), scratch=()):
    held = sum(4 * leaf.size for leaf in outs) + sum(4 * arg.size for arg in (*remote, *args))
    remote = [pltpu.with_memory_space_constraint(arg, pltpu.HBM) for arg in remote]
    scratch = [*scratch, *(pltpu.VMEM(arg.shape, arg.dtype) for arg in remote)]
    if remote:
        scratch.append(pltpu.SemaphoreType.DMA((len(remote),)))
    near, away, free = (pl.BlockSpec(memory_space=space) for space in (pltpu.VMEM, pltpu.HBM, pl.ANY))
    return pl.pallas_call(
        kernel,
        out_shape=outs,
        in_specs=[away] * len(remote) + [near] * len(args) + [free] * len(after),
        out_specs=[free if place in far else near for place in range(len(outs))],
        scratch_shapes=scratch,
        compiler_params=pltpu.CompilerParams(vmem_limit_bytes=max(VMEM_BYTES, 8 * max(arg.size for arg in (*remote, *args)))),
        cost_estimate=pl.CostEstimate(flops=flops, bytes_accessed=held, transcendentals=0),
        name=name,
    )(*remote, *args, *after)


def bind(kernel, *settings):
    return lambda *refs: kernel(*settings, *refs)


def exchange(blocks):
    return lax.all_to_all(blocks, "clus", split_axis=0, concat_axis=0, tiled=True)


def per_device(child_patterns, theta_weights, phi_stencil, phi_weights, shift_phase, translation_table, far_list, far_vector):
    devices, halves = lax.axis_size("clus"), lax.axis_size("samp")
    children, _, own, columns = child_patterns.shape
    groups = children // OCTANTS
    rows, azimuth = theta_weights.shape[0], phi_stencil.shape[0]
    clusters, partners = far_list.shape
    vectors, width = translation_table.shape[0], 2 * translation_table.shape[3]
    blocks, rows_all = columns // TILE, groups * rows
    long, tall = children * own, OCTANTS * rows_all
    sources = 2 if halves == 2 else 3
    struct = jax.ShapeDtypeStruct
    forward = [(i, (i + 1) % halves) for i in range(halves)]
    backward = [((i + 1) % halves, i) for i in range(halves)]

    field = child_patterns.reshape(children, 2, own, blocks, TILE).transpose(0, 2, 3, 1, 4).reshape(long * blocks * 2, TILE)
    neighbours = [lax.ppermute(field, "samp", forward)]
    if sources == 3:
        neighbours.append(lax.ppermute(field, "samp", backward))

    phase = shift_phase.transpose(1, 0, 2).reshape(rows * OCTANTS, azimuth)
    ways = [backward] if sources == 2 else [backward, forward]
    phases = [lax.ppermute(phase, "samp", way) for way in ways]
    table = translation_table.transpose(0, 2, 1, 3).reshape(vectors * rows * 2, width // 2)
    cosine, sine, wide, up, partial = call(
        bind(prepare_kernel, groups, sources, own),
        [
            struct((tall, azimuth), F32),
            struct((tall, azimuth), F32),
            struct((blocks, 2 * PAIR, PAIR), BF16),
            struct((sources, 2, tall, long), BF16),
            struct((2 * tall, columns), F32),
        ],
        [],
        400_000_000,
        "prepare",
        [theta_weights, phase, phi_stencil.T, phi_weights.T, field],
    )
    (outgoing,) = call(
        bind(aggregate_kernel, groups, sources, own, devices),
        [struct((devices, rows_all, width), F32)],
        [*neighbours, partial, cosine, sine, wide, up],
        1_500_000_000,
        "aggregate",
        far=(0,),
        scratch=[pltpu.VMEM((devices, rows_all, width), F32), pltpu.SemaphoreType.DMA((blocks,))],
    )
    arrived = exchange(outgoing)
    down, hot, factors, *turned_parts = call(
        bind(tables_kernel, groups, sources, own),
        [
            struct((sources, 2, long, tall), BF16),
            struct((partners * clusters, 3 * clusters + 3 * vectors), BF16),
            struct((rows, 3 * vectors, 2 * width), BF16),
        ]
        + [struct((tall, azimuth), F32)] * (2 * sources - 2),
        phases,
        600_000_000,
        "tables",
        [theta_weights, far_list.T, far_vector.T, table],
        [outgoing],
    )
    (translated,) = call(
        bind(translate_kernel, rows),
        [struct((clusters * rows, width), F32)],
        [hot, factors, arrived.reshape(clusters * rows, width)],
        600_000_000,
        "translate",
    )
    returned = exchange(translated.reshape(devices, rows_all, width))
    size = rows_all * 2 * azimuth // TILE
    parent, partial = call(
        bind(lower_kernel, devices),
        [struct((size, TILE), F32), struct((2 * long, columns), F32)],
        [returned, cosine, sine, wide, down],
        1_500_000_000,
        "lower",
        far=(0,),
        scratch=[pltpu.VMEM((size, TILE), F32), pltpu.SemaphoreType.DMA],
    )
    returned_parts = [lax.ppermute(returned, "samp", way) for way in ways]
    (total,) = call(
        bind(finish_kernel, devices, sources),
        [struct((long * blocks * 2, TILE), F32)],
        [*returned_parts, *turned_parts, wide, down, partial],
        1_500_000_000,
        "finish",
        far=(0,),
        scratch=[pltpu.VMEM((long * blocks * 2, TILE), F32), pltpu.SemaphoreType.DMA((2,))],
    )
    child_incoming = total.reshape(children, own, blocks, 2, TILE).transpose(0, 3, 1, 2, 4).reshape(children, 2, own, columns)
    parent_incoming = (
        parent.reshape(groups, rows, azimuth // TILE, 2, TILE).transpose(0, 3, 1, 2, 4).reshape(groups, 2, rows, azimuth)
    )
    return (parent_incoming, child_incoming)


def solution(mesh):
    placed = (
        P("clus", None, "samp", None),
        P(),
        P(),
        P(),
        P(None, "samp", None),
        P(None, None, "samp", "clus"),
        P(),
        P(),
    )
    return jax.shard_map(
        per_device,
        mesh=mesh,
        in_specs=placed,
        out_specs=(P("clus", None, "samp", None), P("clus", None, "samp", None)),
        check_vma=False,
    )
```

```python
import jax
import jax.numpy as jnp
from jax import lax
from jax.experimental import pallas as pl
from jax.experimental.pallas import tpu as pltpu
from jax.sharding import PartitionSpec as P

P_SIZE = 6
OCTANTS = 8
TILE = 128
PAIR = 2 * TILE
HALF = TILE // 2
VMEM_BYTES = 8 * 1024 * 1024
F32 = jnp.float32
BF16 = jnp.bfloat16

SIN_TERMS = (-1 / 6, 1 / 120, -1 / 5040, 1 / 362880, -1 / 39916800, 1 / 6227020800)
COS_TERMS = (-1 / 2, 1 / 24, -1 / 720, 1 / 40320, -1 / 3628800, 1 / 479001600, -1 / 87178291200)


def split_two(value):
    high = value.astype(BF16)
    return high, (value - high.astype(F32)).astype(BF16)


def split_three(value):
    high = value.astype(BF16)
    rest = value - high.astype(F32)
    middle = rest.astype(BF16)
    return high, middle, (rest - middle.astype(F32)).astype(BF16)


def product(left, right, left_dim=1, right_dim=0):
    return lax.dot_general(left, right, (((left_dim,), (right_dim,)), ((), ())), preferred_element_type=F32)


def series(square, terms):
    total = jnp.full_like(square, terms[-1])
    for term in terms[-2::-1]:
        total = total * square + term
    return total


def iota(shape, dim):
    return lax.broadcasted_iota(jnp.int32, shape, dim)


def turned(block):
    return jnp.roll(block, HALF, axis=1)


def folded(theta, sources, own):
    below, middle, above = theta[:, :own], theta[:, own : 2 * own], theta[:, 2 * own :]
    return (middle, below + above) if sources == 2 else (middle, below, above)


def started(remote, local, sems):
    copies = [pltpu.make_async_copy(source, target, sems.at[place]) for place, (source, target) in enumerate(zip(remote, local))]
    for copy in copies:
        copy.start()
    return copies


def one_hot(flags):
    return flags.astype(F32).astype(BF16)


def halves_of(theta, sources, own):
    high, low = split_two(jnp.concatenate(folded(theta, sources, own), axis=1))
    return jnp.concatenate([high, low], axis=1)


def turns(phase, groups, rows):
    tall = OCTANTS * groups * rows
    shape = (tall, 3 * OCTANTS * rows)
    place, phase_id = iota(shape, 0), iota(shape, 1) % (OCTANTS * rows)
    repeat = one_hot(place % rows * OCTANTS + place // (groups * rows) == phase_id)
    half = 0.5 * phase
    square = half * half
    sine = half + half * square * series(square, SIN_TERMS)
    cosine = 1.0 + square * series(square, COS_TERMS)
    return [
        product(repeat, jnp.concatenate(split_three(value), axis=0)) for value in (1.0 - 2.0 * sine * sine, 2.0 * sine * cosine)
    ]


def prepare_kernel(groups, sources, own, *refs):
    count = 5
    remote, outs, rest = refs[:count], refs[count : count + 5], refs[count + 5 :]
    local, sems = rest[:count], rest[count]
    theta_ref, phase_ref, stencil_ref, weight_ref, field_ref = local
    cos_ref, sin_ref, wide_ref, up_ref, partial_ref = outs
    copies = started(remote, local, sems)
    rows = theta_ref.shape[0]
    blocks = wide_ref.shape[0]
    tall, long = OCTANTS * groups * rows, groups * OCTANTS * own

    lengths = 2 * sources * long
    at_row = one_hot(iota((tall, rows), 0) % rows == iota((tall, rows), 1))
    column = iota((2 * sources * own, lengths), 1)
    at_own = one_hot(column // long * own + column % own == iota((2 * sources * own, lengths), 0))
    tall_id = iota((tall, long), 0)
    same = iota((tall, long), 1) // own == (tall_id // rows) % groups * OCTANTS + tall_id // (groups * rows)

    copies[0].wait()
    tall_theta = product(at_row, halves_of(theta_ref[...], sources, own)).astype(BF16)
    spread = product(tall_theta, at_own)
    for place in range(2 * sources):
        up_ref[place % sources, place // sources] = jnp.where(same, spread[:, place * long : (place + 1) * long], 0.0).astype(BF16)

    copies[1].wait()
    cos_ref[...], sin_ref[...] = turns(phase_ref[...], groups, rows)

    copies[2].wait()
    copies[3].wait()
    for block in range(blocks):
        columns = slice(block * PAIR, (block + 1) * PAIR)
        after, before = (block + 1) % blocks, (block - 1) % blocks
        pieces = (
            (0, TILE, block * TILE),
            (TILE, 16, after * TILE),
            (PAIR - 16, 16, before * TILE + TILE - 16),
        )
        for start, size, first in pieces:
            child = iota((size, PAIR), 0) + first
            total = jnp.zeros((size, PAIR), F32)
            for point in range(P_SIZE):
                hit = stencil_ref[point : point + 1, columns] == child
                total = jnp.where(hit, weight_ref[point : point + 1, columns], total)
            high, low = split_two(total)
            wide_ref[block, start : start + size, :] = high
            wide_ref[block, PAIR + start : PAIR + start + size, :] = low
        empty = jnp.zeros((TILE - 32, PAIR), BF16)
        wide_ref[block, TILE + 16 : PAIR - 16, :] = empty
        wide_ref[block, PAIR + TILE + 16 : 2 * PAIR - 16, :] = empty

    copies[4].wait()
    for part in range(2):
        partial_ref[part * tall : (part + 1) * tall, :] = polar(up_ref[0, 0], up_ref[0, 1], field_rows(field_ref, part, blocks, long))


def tables_kernel(groups, sources, own, *refs):
    count = 4
    remote, phases = refs[:count], refs[count : count + sources - 1]
    outs = refs[count + sources : -count - 1]
    local, sems = refs[-count - 1 : -1], refs[-1]
    theta_ref, listed_ref, vector_ref, table_ref = local
    down_ref, hot_ref, even_ref, odd_ref, *turned_refs = outs
    copies = started(remote, local, sems)
    rows = theta_ref.shape[0]
    tall, long = OCTANTS * groups * rows, groups * OCTANTS * own

    copies[0].wait()
    lengths = 2 * sources * long
    at_row = one_hot(iota((rows, tall), 1) % rows == iota((rows, tall), 0))
    column = iota((lengths, 2 * sources * own), 0)
    at_own = one_hot(column // long * own + column % own == iota((lengths, 2 * sources * own), 1))
    tall_id = iota((long, tall), 1)
    same = iota((long, tall), 0) // own == (tall_id // rows) % groups * OCTANTS + tall_id // (groups * rows)
    own_theta = product(at_own, halves_of(theta_ref[...], sources, own), 1, 1).astype(BF16)
    spread = product(own_theta, at_row)
    for place in range(2 * sources):
        down_ref[place % sources, place // sources] = jnp.where(same, spread[place * long : (place + 1) * long], 0.0).astype(BF16)

    copies[3].wait()
    raw = table_ref[...]
    many, width = raw.shape
    vectors = many // (2 * rows)
    at, place = iota((many, many), 1), iota((many, many), 0)
    order = one_hot(at == place % vectors * (2 * rows) + place // (2 * vectors) * 2 + place // vectors % 2)
    lane, source = iota((width, 4 * width), 1), iota((width, 4 * width), 0)
    twice = jnp.where(lane % width == source, jnp.where(lane < 3 * width, 1.0, -1.0), 0.0).astype(BF16)
    pieces = [product(product(order, part).astype(BF16), twice).astype(BF16) for part in split_three(raw)]

    copies[1].wait()
    copies[2].wait()
    partners, clusters = listed_ref.shape
    unit = one_hot(iota((clusters, clusters), 0) == iota((clusters, clusters), 1))
    listed = sum(product(unit, half, 1, 1) for half in split_two(listed_ref[...].astype(F32)))
    chosen = sum(product(unit, half, 1, 1) for half in split_two(vector_ref[...].astype(F32)))
    cluster = (iota((clusters, 3 * clusters), 1) % clusters).astype(F32)
    vector = (iota((clusters, 3 * vectors), 1) % vectors).astype(F32)
    hot_vector = []
    for partner in range(partners):
        hot_ref[partner * clusters : (partner + 1) * clusters, :] = one_hot(cluster == listed[:, partner : partner + 1])
        hot_vector.append(one_hot(vector == chosen[:, partner : partner + 1]))
    hot_vector = jnp.concatenate(hot_vector, axis=0)
    for row in range(rows):
        real, imag = 2 * row * vectors, (2 * row + 1) * vectors
        columns = slice(row * 2 * width, (row + 1) * 2 * width)
        even = jnp.concatenate([piece[real : real + vectors, : 2 * width] for piece in pieces], axis=0)
        odd = jnp.concatenate([piece[imag : imag + vectors, 2 * width :] for piece in pieces], axis=0)
        both = product(hot_vector, jnp.concatenate([even, odd], axis=1))
        even_ref[:, columns] = both[:, : 2 * width]
        odd_ref[:, columns] = both[:, 2 * width :]

    for place, phase in enumerate(phases):
        turned_refs[2 * place][...], turned_refs[2 * place + 1][...] = turns(phase[...], groups, rows)


def field_rows(field, part, blocks, long):
    return jnp.concatenate([field[pl.ds(2 * block + part, long, stride=2 * blocks), :] for block in range(blocks)], axis=1)


def polar(high_weights, low_weights, value):
    high, low = split_two(value)
    return product(high_weights, high) + (product(low_weights, high) + product(high_weights, low))


def packed_pieces(real, imag, columns):
    lane = iota((real.shape[0], TILE), 1)
    found = []
    if columns == HALF:
        for start in range(0, real.shape[1], TILE):
            a, b = real[:, start : start + TILE], imag[:, start : start + TILE]
            found.append(jnp.where(lane < HALF, a, turned(b)))
            found.append(jnp.where(lane < HALF, turned(a), b))
        return found
    for start in range(0, real.shape[1], columns):
        found.append(jnp.concatenate([real[:, start : start + columns], imag[:, start : start + columns]], axis=1))
    return found


def unpacked_pieces(read, devices, columns):
    if columns == HALF:
        real, imag = [], []
        for pair in range(devices // 2):
            a, b = read(2 * pair), read(2 * pair + 1)
            lane = iota(a.shape, 1)
            real.append(jnp.where(lane < HALF, a, turned(b)))
            imag.append(jnp.where(lane < HALF, turned(a), b))
        return jnp.concatenate(real, axis=1), jnp.concatenate(imag, axis=1)
    blocks = [read(device) for device in range(devices)]
    return (
        jnp.concatenate([block[:, :columns] for block in blocks], axis=1),
        jnp.concatenate([block[:, columns:] for block in blocks], axis=1),
    )


def aggregate_kernel(groups, sources, own, devices, *refs):
    fields = refs[: sources - 1]
    partial_ref, cos_ref, sin_ref, wide_ref, up_ref = refs[sources - 1 : sources + 4]
    out = refs[-1]
    blocks = wide_ref.shape[0]
    rows_all = cos_ref.shape[0] // OCTANTS
    columns = cos_ref.shape[1] // devices
    long, tall = groups * OCTANTS * own, OCTANTS * rows_all
    refined = []
    for part in range(2):
        value = partial_ref[part * tall : (part + 1) * tall, :]
        for place, field in enumerate(fields):
            value += polar(up_ref[place + 1, 0], up_ref[place + 1, 1], field_rows(field, part, blocks, long))
        refined.append(value)
    high, low = split_two(jnp.concatenate(refined, axis=0))
    lane = iota((2 * tall, TILE), 1)

    def windows(value, block):
        main = value[:, block * TILE : (block + 1) * TILE]
        after, before = (block + 1) % blocks, (block - 1) % blocks
        rim = jnp.where(lane < HALF, value[:, after * TILE : (after + 1) * TILE], value[:, before * TILE : (before + 1) * TILE])
        return [main, rim]

    for block in range(blocks):
        one, two = windows(high, block), windows(low, block)
        left = jnp.concatenate(one + two + one, axis=1)
        right = jnp.concatenate([wide_ref[block, :PAIR], wide_ref[block, :PAIR], wide_ref[block, PAIR:]], axis=0)
        spread = product(left, right)
        real = jnp.zeros((rows_all, PAIR), F32)
        imag = jnp.zeros((rows_all, PAIR), F32)
        for octant in range(OCTANTS):
            rows = slice(octant * rows_all, (octant + 1) * rows_all)
            cosine = cos_ref[rows, block * PAIR : (block + 1) * PAIR]
            sine = sin_ref[rows, block * PAIR : (block + 1) * PAIR]
            a = spread[rows]
            b = spread[tall + octant * rows_all : tall + (octant + 1) * rows_all]
            real += a * cosine - b * sine
            imag += a * sine + b * cosine
        first = block * PAIR // columns
        for place, piece in enumerate(packed_pieces(real, imag, columns)):
            out[first + place] = piece


def translate_kernel(rows, hot_ref, even_ref, odd_ref, arrived_ref, out):
    width = arrived_ref.shape[1]
    clusters = arrived_ref.shape[0] // rows
    partners = hot_ref.shape[0] // clusters
    step = 2 if rows % 2 == 0 else 1
    for first in range(0, rows, step):
        source = jnp.concatenate(
            [arrived_ref[pl.ds(row, clusters, stride=rows), :] for row in range(first, first + step)], axis=1
        )
        gathered = product(hot_ref[...], jnp.concatenate(split_three(source), axis=0))
        columns = slice(first * width, (first + step) * width)
        direct = jnp.zeros((clusters, step * width), F32)
        crossed = jnp.zeros((clusters, step * width), F32)
        for partner in range(partners):
            part = slice(partner * clusters, (partner + 1) * clusters)
            direct += gathered[part] * even_ref[part, columns]
            crossed += gathered[part] * odd_ref[part, columns]
        for row in range(step):
            own = slice(row * width, (row + 1) * width)
            out[pl.ds(first + row, clusters, stride=rows), :] = direct[:, own] + jnp.roll(crossed[:, own], width // 2, axis=1)


def coarse_columns(real, imag, cos_ref, sin_ref, wide_ref):
    blocks = wide_ref.shape[0]
    rows_all = cos_ref.shape[0] // OCTANTS
    mains, rims = [], []
    for block in range(blocks):
        part = slice(block * PAIR, (block + 1) * PAIR)
        a, b = real[:, part], imag[:, part]
        low_real, low_imag = [], []
        for octant in range(OCTANTS):
            rows = slice(octant * rows_all, (octant + 1) * rows_all)
            cosine, sine = cos_ref[rows, part], sin_ref[rows, part]
            low_real.append(a * cosine + b * sine)
            low_imag.append(b * cosine - a * sine)
        high, low = split_two(jnp.concatenate(low_real + low_imag, axis=0))
        left = jnp.concatenate([high, low, high], axis=1)
        right = jnp.concatenate([wide_ref[block, :PAIR], wide_ref[block, :PAIR], wide_ref[block, PAIR:]], axis=1)
        both = product(left, right, 1, 1)
        mains.append(both[:, :TILE])
        rims.append(both[:, TILE:])
    lane = iota((2 * OCTANTS * rows_all, TILE), 1)
    return jnp.concatenate(
        [
            mains[block] + jnp.where(lane < HALF, rims[(block - 1) % blocks], rims[(block + 1) % blocks])
            for block in range(blocks)
        ],
        axis=1,
    )


def lower_kernel(devices, arrived_ref, cos_ref, sin_ref, wide_ref, down_ref, parent_out, partial_ref, parent_ref, sem):
    rows_all = cos_ref.shape[0] // OCTANTS
    azimuth = cos_ref.shape[1]
    long, tall = down_ref.shape[2:]
    real, imag = unpacked_pieces(lambda device: arrived_ref[device], devices, azimuth // devices)
    tiles = azimuth // TILE
    for tile in range(tiles):
        for part, value in enumerate((real, imag)):
            parent_ref[pl.ds(2 * tile + part, rows_all, stride=2 * tiles), :] = value[:, tile * TILE : (tile + 1) * TILE]
    copy = pltpu.make_async_copy(parent_ref, parent_out, sem)
    copy.start()
    coarse = coarse_columns(real, imag, cos_ref, sin_ref, wide_ref)
    for part in range(2):
        partial_ref[part * long : (part + 1) * long, :] = polar(down_ref[0, 0], down_ref[0, 1], coarse[part * tall : (part + 1) * tall])
    copy.wait()


def finish_kernel(devices, sources, *refs):
    arrived = refs[: sources - 1]
    turned_refs = refs[sources - 1 : 3 * (sources - 1)]
    wide_ref, down_ref, partial_ref, out, ready, sems = refs[3 * (sources - 1) :]
    blocks = wide_ref.shape[0]
    azimuth = turned_refs[0].shape[1]
    long, tall = down_ref.shape[2:]
    coarse = []
    for place, field in enumerate(arrived):
        real, imag = unpacked_pieces(lambda device: field[device], devices, azimuth // devices)
        coarse.append(split_two(coarse_columns(real, imag, turned_refs[2 * place], turned_refs[2 * place + 1], wide_ref)))
    copies = []
    size = long // 2
    for first in range(0, long, size):
        rows = slice(first, first + size)
        for part in range(2):
            value = partial_ref[part * long + first : part * long + first + size, :]
            for place, (high, low) in enumerate(coarse):
                source = slice(part * tall, (part + 1) * tall)
                up, fine = down_ref[place + 1, 0, rows], down_ref[place + 1, 1, rows]
                value += product(up, high[source]) + (product(fine, high[source]) + product(up, low[source]))
            for block in range(blocks):
                start = 2 * blocks * first + 2 * block + part
                ready[pl.ds(start, size, stride=2 * blocks), :] = value[:, block * TILE : (block + 1) * TILE]
        whole = slice(2 * blocks * first, 2 * blocks * (first + size))
        copies.append(pltpu.make_async_copy(ready.at[whole], out.at[whole], sems.at[len(copies)]))
        copies[-1].start()
    for copy in copies:
        copy.wait()


def call(kernel, outs, args, flops, name, remote=(), after=(), far=(), scratch=()):
    held = sum(4 * leaf.size for leaf in outs) + sum(4 * arg.size for arg in (*remote, *args))
    remote = [pltpu.with_memory_space_constraint(arg, pltpu.HBM) for arg in remote]
    scratch = [*scratch, *(pltpu.VMEM(arg.shape, arg.dtype) for arg in remote)]
    if remote:
        scratch.append(pltpu.SemaphoreType.DMA((len(remote),)))
    near, away, free = (pl.BlockSpec(memory_space=space) for space in (pltpu.VMEM, pltpu.HBM, pl.ANY))
    return pl.pallas_call(
        kernel,
        out_shape=[leaf if place in far else pltpu.VMEM(leaf.shape, leaf.dtype) for place, leaf in enumerate(outs)],
        in_specs=[away] * len(remote) + [near] * len(args) + [free] * len(after),
        out_specs=[free if place in far else near for place in range(len(outs))],
        scratch_shapes=scratch,
        compiler_params=pltpu.CompilerParams(vmem_limit_bytes=max(VMEM_BYTES, 8 * max(arg.size for arg in (*remote, *args)))),
        cost_estimate=pl.CostEstimate(flops=flops, bytes_accessed=held, transcendentals=0),
        name=name,
    )(*remote, *args, *after)


def bind(kernel, *settings):
    return lambda *refs: kernel(*settings, *refs)


def exchange(blocks):
    return lax.all_to_all(blocks, "clus", split_axis=0, concat_axis=0, tiled=True)


def per_device(child_patterns, theta_weights, phi_stencil, phi_weights, shift_phase, translation_table, far_list, far_vector):
    devices, halves = lax.axis_size("clus"), lax.axis_size("samp")
    children, _, own, columns = child_patterns.shape
    groups = children // OCTANTS
    rows, azimuth = theta_weights.shape[0], phi_stencil.shape[0]
    clusters, partners = far_list.shape
    vectors, width = translation_table.shape[0], 2 * translation_table.shape[3]
    blocks, rows_all = columns // TILE, groups * rows
    long, tall = children * own, OCTANTS * rows_all
    sources = 2 if halves == 2 else 3
    struct = jax.ShapeDtypeStruct
    forward = [(i, (i + 1) % halves) for i in range(halves)]
    backward = [((i + 1) % halves, i) for i in range(halves)]

    field = child_patterns.reshape(children, 2, own, blocks, TILE).transpose(0, 2, 3, 1, 4).reshape(long * blocks * 2, TILE)
    neighbours = [lax.ppermute(field, "samp", forward)]
    if sources == 3:
        neighbours.append(lax.ppermute(field, "samp", backward))

    phase = shift_phase.transpose(1, 0, 2).reshape(rows * OCTANTS, azimuth)
    ways = [backward] if sources == 2 else [backward, forward]
    phases = [lax.ppermute(phase, "samp", way) for way in ways]
    table = translation_table.transpose(0, 2, 1, 3).reshape(vectors * rows * 2, width // 2)
    cosine, sine, wide, up, partial = call(
        bind(prepare_kernel, groups, sources, own),
        [
            struct((tall, azimuth), F32),
            struct((tall, azimuth), F32),
            struct((blocks, 2 * PAIR, PAIR), BF16),
            struct((sources, 2, tall, long), BF16),
            struct((2 * tall, columns), F32),
        ],
        [],
        400_000_000,
        "prepare",
        [theta_weights, phase, phi_stencil.T, phi_weights.T, field],
    )
    (outgoing,) = call(
        bind(aggregate_kernel, groups, sources, own, devices),
        [struct((devices, rows_all, width), F32)],
        [*neighbours, partial, cosine, sine, wide, up],
        1_500_000_000,
        "aggregate",
        after=phases,
    )
    arrived = exchange(outgoing)
    down, hot, even, odd, *turned_parts = call(
        bind(tables_kernel, groups, sources, own),
        [
            struct((sources, 2, long, tall), BF16),
            struct((partners * clusters, 3 * clusters), BF16),
            struct((partners * clusters, rows * width), F32),
            struct((partners * clusters, rows * width), F32),
        ]
        + [struct((tall, azimuth), F32)] * (2 * sources - 2),
        phases,
        600_000_000,
        "tables",
        [theta_weights, far_list.T, far_vector.T, table],
        [outgoing],
    )
    (translated,) = call(
        bind(translate_kernel, rows),
        [struct((clusters * rows, width), F32)],
        [hot, even, odd, arrived.reshape(clusters * rows, width)],
        600_000_000,
        "translate",
    )
    returned = exchange(translated.reshape(devices, rows_all, width))
    size = rows_all * 2 * azimuth // TILE
    parent, partial = call(
        bind(lower_kernel, devices),
        [struct((size, TILE), F32), struct((2 * long, columns), F32)],
        [returned, cosine, sine, wide, down],
        1_500_000_000,
        "lower",
        far=(0,),
        scratch=[pltpu.VMEM((size, TILE), F32), pltpu.SemaphoreType.DMA],
    )
    returned_parts = [lax.ppermute(returned, "samp", way) for way in ways]
    (total,) = call(
        bind(finish_kernel, devices, sources),
        [struct((long * blocks * 2, TILE), F32)],
        [*returned_parts, *turned_parts, wide, down, partial],
        1_500_000_000,
        "finish",
        far=(0,),
        scratch=[pltpu.VMEM((long * blocks * 2, TILE), F32), pltpu.SemaphoreType.DMA((2,))],
    )
    child_incoming = total.reshape(children, own, blocks, 2, TILE).transpose(0, 3, 1, 2, 4).reshape(children, 2, own, columns)
    parent_incoming = (
        parent.reshape(groups, rows, azimuth // TILE, 2, TILE).transpose(0, 3, 1, 2, 4).reshape(groups, 2, rows, azimuth)
    )
    return (parent_incoming, child_incoming)


def solution(mesh):
    placed = (
        P("clus", None, "samp", None),
        P(),
        P(),
        P(),
        P(None, "samp", None),
        P(None, None, "samp", "clus"),
        P(),
        P(),
    )
    return jax.shard_map(
        per_device,
        mesh=mesh,
        in_specs=placed,
        out_specs=(P("clus", None, "samp", None), P("clus", None, "samp", None)),
        check_vma=False,
    )
```

```python
import jax
import jax.numpy as jnp
from jax import lax
from jax.experimental import pallas as pl
from jax.experimental.pallas import tpu as pltpu
from jax.sharding import PartitionSpec as P

P_SIZE = 6
OCTANTS = 8
TILE = 128
PAIR = 2 * TILE
HALF = TILE // 2
VMEM_BYTES = 8 * 1024 * 1024
F32 = jnp.float32
BF16 = jnp.bfloat16

SIN_TERMS = (-1 / 6, 1 / 120, -1 / 5040, 1 / 362880, -1 / 39916800, 1 / 6227020800)
COS_TERMS = (-1 / 2, 1 / 24, -1 / 720, 1 / 40320, -1 / 3628800, 1 / 479001600, -1 / 87178291200)


def split_two(value):
    high = value.astype(BF16)
    return high, (value - high.astype(F32)).astype(BF16)


def split_three(value):
    high = value.astype(BF16)
    rest = value - high.astype(F32)
    middle = rest.astype(BF16)
    return high, middle, (rest - middle.astype(F32)).astype(BF16)


def product(left, right, left_dim=1, right_dim=0):
    return lax.dot_general(left, right, (((left_dim,), (right_dim,)), ((), ())), preferred_element_type=F32)


def series(square, terms):
    total = jnp.full_like(square, terms[-1])
    for term in terms[-2::-1]:
        total = total * square + term
    return total


def iota(shape, dim):
    return lax.broadcasted_iota(jnp.int32, shape, dim)


def one_hot(flags):
    return flags.astype(F32).astype(BF16)


def turned(block):
    return jnp.roll(block, HALF, axis=1)


def folded(theta, sources, own):
    below, middle, above = theta[:, :own], theta[:, own : 2 * own], theta[:, 2 * own :]
    return jnp.concatenate((middle, below + above) if sources == 2 else (middle, below, above), axis=1)


def turns(phase):
    half = 0.5 * phase
    square = half * half
    sine = half + half * square * series(square, SIN_TERMS)
    cosine = 1.0 + square * series(square, COS_TERMS)
    return 1.0 - 2.0 * sine * sine, 2.0 * sine * cosine


def started(remote, local, sems):
    copies = [pltpu.make_async_copy(source, target, sems.at[place]) for place, (source, target) in enumerate(zip(remote, local))]
    for copy in copies:
        copy.start()
    return copies


def prepare_kernel(sources, own, *refs):
    count = 5
    remote, outs, rest = refs[:count], refs[count : count + 5], refs[count + 5 :]
    cos_ref, sin_ref, wide_ref, polar_ref, field_out = outs
    theta_ref, phase_ref, stencil_ref, weight_ref, sems = rest
    copies = started(remote, [theta_ref, phase_ref, stencil_ref, weight_ref, field_out], sems)
    rows = theta_ref.shape[0]
    blocks = wide_ref.shape[0]

    wide = sources * own
    at_row = one_hot(iota((rows * wide, rows), 0) // wide == iota((rows * wide, rows), 1))
    keep = iota((rows * wide, wide), 0) % wide == iota((rows * wide, wide), 1)
    ones = jnp.ones((wide, TILE), BF16)
    copies[0].wait()
    parts = [
        product(jnp.where(keep, product(at_row, part), 0.0).astype(BF16), ones)
        for part in split_three(folded(theta_ref[...], sources, own))
    ]
    polar_ref[...] = parts[0] + (parts[1] + parts[2])

    copies[1].wait()
    cos_ref[...], sin_ref[...] = turns(phase_ref[...])

    copies[2].wait()
    copies[3].wait()
    for block in range(blocks):
        columns = slice(block * PAIR, (block + 1) * PAIR)
        after, before = (block + 1) % blocks, (block - 1) % blocks
        pieces = (
            (0, TILE, block * TILE),
            (TILE, 16, after * TILE),
            (PAIR - 16, 16, before * TILE + TILE - 16),
        )
        for start, size, first in pieces:
            child = iota((size, PAIR), 0) + first
            total = jnp.zeros((size, PAIR), F32)
            for point in range(P_SIZE):
                hit = stencil_ref[point : point + 1, columns] == child
                total = jnp.where(hit, weight_ref[point : point + 1, columns], total)
            high, low = split_two(total)
            wide_ref[block, start : start + size, :] = high
            wide_ref[block, PAIR + start : PAIR + start + size, :] = low
        empty = jnp.zeros((TILE - 32, PAIR), BF16)
        wide_ref[block, TILE + 16 : PAIR - 16, :] = empty
        wide_ref[block, PAIR + TILE + 16 : 2 * PAIR - 16, :] = empty
    copies[4].wait()


def polar_splat(polar_ref, row, width):
    return jnp.concatenate([polar_ref[row : row + 1, :]] * (width // TILE), axis=1)


def aggregate_kernel(groups, sources, own, devices, *refs):
    fields = refs[:sources]
    cos_ref, sin_ref, wide_ref, polar_ref = refs[sources : sources + 4]
    out, high_s, low_s = refs[-3:]
    blocks = wide_ref.shape[0]
    rows = cos_ref.shape[0] // OCTANTS
    columns = cos_ref.shape[1] // devices
    size = 2 * groups
    wide = sources * own
    row_stride = 2 * blocks
    child_stride = OCTANTS * own * row_stride

    for octant in range(OCTANTS):
        given = []
        for field in fields:
            for row in range(own):
                start = (octant * own + row) * row_stride
                given.append(
                    jnp.concatenate(
                        [
                            jnp.concatenate(
                                [field[pl.ds(start + 2 * block + part, groups, stride=child_stride), :] for part in range(2)],
                                axis=0,
                            )
                            for block in range(blocks)
                        ],
                        axis=1,
                    )
                )
        for first in range(0, rows, 2):
            pair = []
            for row in (first, first + 1):
                total = given[0] * polar_splat(polar_ref, row * wide, blocks * TILE)
                for place in range(1, wide):
                    total += given[place] * polar_splat(polar_ref, row * wide + place, blocks * TILE)
                pair.append(total)
            high, low = split_two(jnp.concatenate(pair, axis=0))
            target = slice((octant * rows + first) * size, (octant * rows + first + 2) * size)
            high_s[target, :] = high
            low_s[target, :] = low

    lane = iota((OCTANTS * rows * size, TILE), 1)

    def windows(value, block):
        main = value[:, block * TILE : (block + 1) * TILE]
        after, before = (block + 1) % blocks, (block - 1) % blocks
        rim = jnp.where(lane < HALF, value[:, after * TILE : (after + 1) * TILE], value[:, before * TILE : (before + 1) * TILE])
        return [main, rim]

    for block in range(blocks):
        one, two = windows(high_s, block), windows(low_s, block)
        left = jnp.concatenate(one + two + one, axis=1)
        right = jnp.concatenate([wide_ref[block, :PAIR], wide_ref[block, :PAIR], wide_ref[block, PAIR:]], axis=0)
        spread = product(left, right)
        part = slice(block * PAIR, (block + 1) * PAIR)
        summed = []
        for row in range(rows):
            direct = jnp.zeros((size, PAIR), F32)
            crossed = jnp.zeros((size, PAIR), F32)
            for octant in range(OCTANTS):
                start = (octant * rows + row) * size
                turn = slice(row * OCTANTS + octant, row * OCTANTS + octant + 1)
                direct += spread[start : start + size] * cos_ref[turn, part]
                crossed += spread[start : start + size] * sin_ref[turn, part]
            summed.append(direct + jnp.concatenate([-crossed[groups:], crossed[:groups]], axis=0))
        for first in range(0, rows, 2):
            target = slice(first // 2 * size, (first // 2 + 1) * size)
            for place, piece in enumerate(packed_pieces(summed[first], summed[first + 1], columns)):
                out[block * PAIR // columns + place, target, :] = piece


def packed_pieces(one, two, columns):
    found = []
    if columns == HALF:
        lane = iota((one.shape[0], TILE), 1)
        for start in range(0, one.shape[1], TILE):
            a, b = one[:, start : start + TILE], two[:, start : start + TILE]
            found.append(jnp.where(lane < HALF, a, turned(b)))
            found.append(jnp.where(lane < HALF, turned(a), b))
        return found
    for start in range(0, one.shape[1], columns):
        found.append(jnp.concatenate([one[:, start : start + columns], two[:, start : start + columns]], axis=1))
    return found


def unpacked_pieces(blocks, columns):
    if columns == HALF:
        one, two = [], []
        for a, b in zip(blocks[::2], blocks[1::2]):
            lane = iota(a.shape, 1)
            one.append(jnp.where(lane < HALF, a, turned(b)))
            two.append(jnp.where(lane < HALF, turned(a), b))
        return [jnp.concatenate(one, axis=1), jnp.concatenate(two, axis=1)]
    return [
        jnp.concatenate([block[:, :columns] for block in blocks], axis=1),
        jnp.concatenate([block[:, columns:] for block in blocks], axis=1),
    ]


def tables_kernel(groups, sources, rows, *refs):
    count = 3
    remote, phases = refs[:count], refs[count : count + sources - 1]
    outs = refs[count + sources : -count - 1]
    local, sems = refs[-count - 1 : -1], refs[-1]
    listed_ref, vector_ref, table_ref = local
    hot_ref, chosen_ref, table_out, *turned_refs = outs
    copies = started(remote, local, sems)
    for place, phase in enumerate(phases):
        turned_refs[2 * place][...], turned_refs[2 * place + 1][...] = turns(phase[...])

    copies[2].wait()
    raw = table_ref[...]
    many, width = raw.shape
    vectors = many // (2 * rows)
    at, place = iota((many, many), 1), iota((many, many), 0)
    order = one_hot(at == place % vectors * (2 * rows) + place // (2 * vectors) * 2 + place // vectors % 2)
    twice = one_hot(iota((width, 2 * width), 1) % width == iota((width, 2 * width), 0))
    lane = iota((vectors, 2 * width), 1)
    for piece, part in enumerate(split_three(raw)):
        double = product(product(order, part).astype(BF16), twice)
        target = slice(piece * vectors, (piece + 1) * vectors)
        for kind in range(2):
            for first in range(0, rows, 2):
                one, two = (double[(2 * row + kind) * vectors : (2 * row + kind + 1) * vectors] for row in (first, first + 1))
                start = (kind * rows + first) * width
                table_out[target, start : start + 2 * width] = jnp.where(lane < width, one, two).astype(BF16)

    copies[0].wait()
    copies[1].wait()
    partners, clusters = listed_ref.shape
    unit = one_hot(iota((clusters, clusters), 0) == iota((clusters, clusters), 1))
    listed = listed_ref[...]
    at = (listed // groups * (2 * groups) + listed % groups).astype(F32)
    at = sum(product(unit, half, 1, 1) for half in split_two(at))
    chosen = sum(product(unit, half, 1, 1) for half in split_two(vector_ref[...].astype(F32)))
    arrived = (iota((clusters, 4 * clusters), 1) % (2 * clusters)).astype(F32)
    vector = (iota((clusters, 3 * vectors), 1) % vectors).astype(F32)
    for partner in range(partners):
        for part in range(2):
            start = (part * partners + partner) * clusters
            hot_ref[start : start + clusters, :] = one_hot(arrived == at[:, partner : partner + 1] + float(part * groups))
        start = partner * clusters
        chosen_ref[start : start + clusters, :] = one_hot(vector == chosen[:, partner : partner + 1])


def translate_kernel(groups, hot_ref, chosen_ref, table_ref, arrived_ref, out):
    devices, tall, width = arrived_ref.shape
    clusters = devices * groups
    partners = chosen_ref.shape[0] // clusters
    size = 2 * groups
    steps = tall // size
    count = partners * clusters
    source = jnp.concatenate(
        [arrived_ref[:, step * size : (step + 1) * size, :].reshape(devices * size, width) for step in range(steps)], axis=1
    )
    gathered = product(hot_ref[...], jnp.concatenate(split_two(source), axis=0))
    factors = product(chosen_ref[...], table_ref[...])
    for step in range(steps):
        lanes = slice(step * width, (step + 1) * width)
        other = slice((steps + step) * width, (steps + step + 1) * width)
        real = jnp.zeros((clusters, width), F32)
        imag = jnp.zeros((clusters, width), F32)
        for partner in range(partners):
            part = slice(partner * clusters, (partner + 1) * clusters)
            cross = slice(count + partner * clusters, count + (partner + 1) * clusters)
            a, b = gathered[part, lanes], gathered[cross, lanes]
            real += a * factors[part, lanes] - b * factors[part, other]
            imag += a * factors[part, other] + b * factors[part, lanes]
        for device in range(devices):
            rows = slice(device * groups, (device + 1) * groups)
            out[device, step * size : (step + 1) * size, :] = jnp.concatenate([real[rows], imag[rows]], axis=0)


def unpacked_fields(arrived_ref, size, columns):
    fields = []
    for start in range(0, arrived_ref.shape[1], size):
        fields += unpacked_pieces([arrived_ref[device, start : start + size, :] for device in range(arrived_ref.shape[0])], columns)
    return fields


def coarse_columns(fields, cos_ref, sin_ref, wide_ref):
    blocks = wide_ref.shape[0]
    rows, size = len(fields), fields[0].shape[0]
    groups = size // 2
    crossed = [jnp.concatenate([field[groups:], -field[:groups]], axis=0) for field in fields]
    mains, rims = [], []
    for block in range(blocks):
        part = slice(block * PAIR, (block + 1) * PAIR)
        lowered = []
        for octant in range(OCTANTS):
            for row in range(rows):
                turn = slice(row * OCTANTS + octant, row * OCTANTS + octant + 1)
                lowered.append(fields[row][:, part] * cos_ref[turn, part] + crossed[row][:, part] * sin_ref[turn, part])
        high, low = split_two(jnp.concatenate(lowered, axis=0))
        left = jnp.concatenate([high, low, high], axis=1)
        right = jnp.concatenate([wide_ref[block, :PAIR], wide_ref[block, :PAIR], wide_ref[block, PAIR:]], axis=1)
        both = product(left, right, 1, 1)
        mains.append(both[:, :TILE])
        rims.append(both[:, TILE:])
    lane = iota((OCTANTS * rows * size, TILE), 1)
    return jnp.concatenate(
        [
            mains[block] + jnp.where(lane < HALF, rims[(block - 1) % blocks], rims[(block + 1) % blocks])
            for block in range(blocks)
        ],
        axis=1,
    )


def anterpolated(coarse, polar_ref, octant, place, rows, size, wide):
    total = None
    for row in range(rows):
        start = (octant * rows + row) * size
        term = coarse[start : start + size] * polar_splat(polar_ref, row * wide + place, coarse.shape[1])
        total = term if total is None else total + term
    return total


def lower_kernel(groups, own, arrived_ref, cos_ref, sin_ref, wide_ref, polar_ref, parent_out, partial_ref, parent_ref, sem):
    devices = arrived_ref.shape[0]
    azimuth = cos_ref.shape[1]
    size = 2 * groups
    fields = unpacked_fields(arrived_ref, size, azimuth // devices)
    rows = len(fields)
    wide = polar_ref.shape[0] // rows
    tiles = azimuth // TILE
    for row, field in enumerate(fields):
        for tile in range(tiles):
            for part in range(2):
                start = (row * tiles + tile) * 2 + part
                parent_ref[pl.ds(start, groups, stride=rows * tiles * 2), :] = field[
                    part * groups : (part + 1) * groups, tile * TILE : (tile + 1) * TILE
                ]
    copy = pltpu.make_async_copy(parent_ref, parent_out, sem)
    copy.start()
    coarse = coarse_columns(fields, cos_ref, sin_ref, wide_ref)
    for octant in range(OCTANTS):
        for row in range(own):
            start = (octant * own + row) * size
            partial_ref[start : start + size, :] = anterpolated(coarse, polar_ref, octant, row, rows, size, wide)
    copy.wait()


def finish_kernel(groups, sources, own, *refs):
    arrived = refs[: sources - 1]
    turned_refs = refs[sources - 1 : 3 * (sources - 1)]
    wide_ref, polar_ref, partial_ref, out = refs[3 * (sources - 1) :]
    blocks = wide_ref.shape[0]
    azimuth = turned_refs[0].shape[1]
    size = 2 * groups
    coarse = []
    for place, field in enumerate(arrived):
        fields = unpacked_fields(field, size, azimuth // field.shape[0])
        coarse.append(coarse_columns(fields, turned_refs[2 * place], turned_refs[2 * place + 1], wide_ref))
    rows = len(fields)
    wide = sources * own
    row_stride = 2 * blocks
    for octant in range(OCTANTS):
        for row in range(own):
            start = (octant * own + row) * size
            value = partial_ref[start : start + size, :]
            for place in range(sources - 1):
                value += anterpolated(coarse[place], polar_ref, octant, (place + 1) * own + row, rows, size, wide)
            for block in range(blocks):
                for part in range(2):
                    first = (octant * own + row) * row_stride + 2 * block + part
                    out[pl.ds(first, groups, stride=OCTANTS * own * row_stride), :] = value[
                        part * groups : (part + 1) * groups, block * TILE : (block + 1) * TILE
                    ]


def call(kernel, outs, args, flops, name, remote=(), after=(), far=(), scratch=(), into=0):
    held = sum(4 * leaf.size for leaf in outs) + sum(4 * arg.size for arg in (*remote, *args))
    remote = [pltpu.with_memory_space_constraint(arg, pltpu.HBM) for arg in remote]
    scratch = [*scratch, *(pltpu.VMEM(arg.shape, arg.dtype) for arg in remote[: len(remote) - into])]
    if remote:
        scratch.append(pltpu.SemaphoreType.DMA((len(remote),)))
    near, away, free = (pl.BlockSpec(memory_space=space) for space in (pltpu.VMEM, pltpu.HBM, pl.ANY))
    return pl.pallas_call(
        kernel,
        out_shape=outs,
        in_specs=[away] * len(remote) + [near] * len(args) + [free] * len(after),
        out_specs=[free if place in far else near for place in range(len(outs))],
        scratch_shapes=scratch,
        compiler_params=pltpu.CompilerParams(vmem_limit_bytes=max(VMEM_BYTES, 8 * max(arg.size for arg in (*remote, *args)))),
        cost_estimate=pl.CostEstimate(flops=flops, bytes_accessed=held, transcendentals=0),
        name=name,
    )(*remote, *args, *after)


def bind(kernel, *settings):
    return lambda *refs: kernel(*settings, *refs)


def exchange(blocks):
    return lax.all_to_all(blocks, "clus", split_axis=0, concat_axis=0, tiled=True)


def per_device(child_patterns, theta_weights, phi_stencil, phi_weights, shift_phase, translation_table, far_list, far_vector):
    devices, halves = lax.axis_size("clus"), lax.axis_size("samp")
    children, _, own, columns = child_patterns.shape
    groups = children // OCTANTS
    rows, azimuth = theta_weights.shape[0], phi_stencil.shape[0]
    clusters, partners = far_list.shape
    vectors, width = translation_table.shape[0], 2 * translation_table.shape[3]
    blocks, rows_all = columns // TILE, groups * rows
    long = children * own
    sources = 2 if halves == 2 else 3
    struct = jax.ShapeDtypeStruct
    forward = [(i, (i + 1) % halves) for i in range(halves)]
    backward = [((i + 1) % halves, i) for i in range(halves)]

    field = child_patterns.reshape(children, 2, own, blocks, TILE).transpose(0, 2, 3, 1, 4).reshape(long * blocks * 2, TILE)
    neighbours = [lax.ppermute(field, "samp", forward)]
    if sources == 3:
        neighbours.append(lax.ppermute(field, "samp", backward))
    phase = shift_phase.transpose(1, 0, 2).reshape(rows * OCTANTS, azimuth)
    ways = [backward] if sources == 2 else [backward, forward]
    phases = [lax.ppermute(phase, "samp", way) for way in ways]
    table = translation_table.transpose(0, 2, 1, 3).reshape(vectors * rows * 2, width // 2)
    turn = struct((rows * OCTANTS, azimuth), F32)

    cosine, sine, wide, polar, held = call(
        bind(prepare_kernel, sources, own),
        [
            turn,
            turn,
            struct((blocks, 2 * PAIR, PAIR), BF16),
            struct((rows * sources * own, TILE), F32),
            struct(field.shape, F32),
        ],
        [],
        400_000_000,
        "prepare",
        [theta_weights, phase, phi_stencil.T, phi_weights.T, field],
        into=1,
    )
    (outgoing,) = call(
        bind(aggregate_kernel, groups, sources, own, devices),
        [struct((devices, rows_all, width), F32)],
        [held, *neighbours, cosine, sine, wide, polar],
        1_500_000_000,
        "aggregate",
        after=phases,
        scratch=[pltpu.VMEM((2 * groups * OCTANTS * rows, columns), BF16)] * 2,
    )
    arrived = exchange(outgoing)
    hot, chosen, factors, *turned_parts = call(
        bind(tables_kernel, groups, sources, rows),
        [
            struct((2 * partners * clusters, 4 * clusters), BF16),
            struct((partners * clusters, 3 * vectors), BF16),
            struct((3 * vectors, rows * width), BF16),
        ]
        + [turn] * (2 * sources - 2),
        phases,
        600_000_000,
        "tables",
        [far_list.T, far_vector.T, table],
        [outgoing],
    )
    (translated,) = call(
        bind(translate_kernel, groups),
        [struct((devices, rows_all, width), F32)],
        [hot, chosen, factors, arrived],
        600_000_000,
        "translate",
    )
    returned = exchange(translated)
    size = rows_all * 2 * azimuth // TILE
    parent, partial = call(
        bind(lower_kernel, groups, own),
        [struct((size, TILE), F32), struct((2 * long, columns), F32)],
        [returned, cosine, sine, wide, polar],
        1_500_000_000,
        "lower",
        far=(0,),
        scratch=[pltpu.VMEM((size, TILE), F32), pltpu.SemaphoreType.DMA],
    )
    returned_parts = [lax.ppermute(returned, "samp", way) for way in ways]
    (total,) = call(
        bind(finish_kernel, groups, sources, own),
        [struct((long * blocks * 2, TILE), F32)],
        [*returned_parts, *turned_parts, wide, polar, partial],
        1_500_000_000,
        "finish",
    )
    child_incoming = total.reshape(children, own, blocks, 2, TILE).transpose(0, 3, 1, 2, 4).reshape(children, 2, own, columns)
    parent_incoming = (
        parent.reshape(groups, rows, azimuth // TILE, 2, TILE).transpose(0, 3, 1, 2, 4).reshape(groups, 2, rows, azimuth)
    )
    return (parent_incoming, child_incoming)


def solution(mesh):
    placed = (
        P("clus", None, "samp", None),
        P(),
        P(),
        P(),
        P(None, "samp", None),
        P(None, None, "samp", "clus"),
        P(),
        P(),
    )
    return jax.shard_map(
        per_device,
        mesh=mesh,
        in_specs=placed,
        out_specs=(P("clus", None, "samp", None), P("clus", None, "samp", None)),
        check_vma=False,
    )
```

```python
import jax
import jax.numpy as jnp
from jax import lax
from jax.experimental import pallas as pl
from jax.experimental.pallas import tpu as pltpu
from jax.sharding import PartitionSpec as P

P_SIZE = 6
OCTANTS = 8
TILE = 128
PAIR = 2 * TILE
HALF = TILE // 2
VMEM_BYTES = 8 * 1024 * 1024
F32 = jnp.float32
BF16 = jnp.bfloat16

SIN_TERMS = (-1 / 6, 1 / 120, -1 / 5040, 1 / 362880, -1 / 39916800, 1 / 6227020800)
COS_TERMS = (-1 / 2, 1 / 24, -1 / 720, 1 / 40320, -1 / 3628800, 1 / 479001600, -1 / 87178291200)


def split_two(value):
    high = value.astype(BF16)
    return high, (value - high.astype(F32)).astype(BF16)


def split_three(value):
    high = value.astype(BF16)
    rest = value - high.astype(F32)
    middle = rest.astype(BF16)
    return high, middle, (rest - middle.astype(F32)).astype(BF16)


def product(left, right, left_dim=1, right_dim=0):
    return lax.dot_general(left, right, (((left_dim,), (right_dim,)), ((), ())), preferred_element_type=F32)


def series(square, terms):
    total = jnp.full_like(square, terms[-1])
    for term in terms[-2::-1]:
        total = total * square + term
    return total


def iota(shape, dim):
    return lax.broadcasted_iota(jnp.int32, shape, dim)


def one_hot(flags):
    return flags.astype(F32).astype(BF16)


def turned(block):
    return jnp.roll(block, HALF, axis=1)


def folded(theta, sources, own):
    below, middle, above = theta[:, :own], theta[:, own : 2 * own], theta[:, 2 * own :]
    return jnp.concatenate((middle, below + above) if sources == 2 else (middle, below, above), axis=1)


def turns(phase):
    half = 0.5 * phase
    square = half * half
    sine = half + half * square * series(square, SIN_TERMS)
    cosine = 1.0 + square * series(square, COS_TERMS)
    return 1.0 - 2.0 * sine * sine, 2.0 * sine * cosine


def started(remote, local, sems):
    copies = [pltpu.make_async_copy(source, target, sems.at[place]) for place, (source, target) in enumerate(zip(remote, local))]
    for copy in copies:
        copy.start()
    return copies


def prepare_kernel(sources, own, *refs):
    count = 5
    remote, outs, rest = refs[:count], refs[count : count + 5], refs[count + 5 :]
    cos_ref, sin_ref, wide_ref, polar_ref, field_out = outs
    theta_ref, phase_ref, stencil_ref, weight_ref, sems = rest
    copies = started(remote, [theta_ref, phase_ref, stencil_ref, weight_ref, field_out], sems)
    rows = theta_ref.shape[0]
    blocks = wide_ref.shape[0]

    wide = sources * own
    at_row = one_hot(iota((rows * wide, rows), 0) // wide == iota((rows * wide, rows), 1))
    keep = iota((rows * wide, wide), 0) % wide == iota((rows * wide, wide), 1)
    ones = jnp.ones((wide, TILE), BF16)
    copies[0].wait()
    parts = [
        product(jnp.where(keep, product(at_row, part), 0.0).astype(BF16), ones)
        for part in split_three(folded(theta_ref[...], sources, own))
    ]
    polar_ref[...] = parts[0] + (parts[1] + parts[2])

    copies[1].wait()
    cos_ref[...], sin_ref[...] = turns(phase_ref[...])

    copies[2].wait()
    copies[3].wait()
    for block in range(blocks):
        columns = slice(block * PAIR, (block + 1) * PAIR)
        after, before = (block + 1) % blocks, (block - 1) % blocks
        pieces = (
            (0, TILE, block * TILE),
            (TILE, 16, after * TILE),
            (PAIR - 16, 16, before * TILE + TILE - 16),
        )
        for start, size, first in pieces:
            child = iota((size, PAIR), 0) + first
            total = jnp.zeros((size, PAIR), F32)
            for point in range(P_SIZE):
                hit = stencil_ref[point : point + 1, columns] == child
                total = jnp.where(hit, weight_ref[point : point + 1, columns], total)
            high, low = split_two(total)
            wide_ref[block, start : start + size, :] = high
            wide_ref[block, PAIR + start : PAIR + start + size, :] = low
        empty = jnp.zeros((TILE - 32, PAIR), BF16)
        wide_ref[block, TILE + 16 : PAIR - 16, :] = empty
        wide_ref[block, PAIR + TILE + 16 : 2 * PAIR - 16, :] = empty
    copies[4].wait()


def polar_splat(polar_ref, row, width):
    return jnp.concatenate([polar_ref[row : row + 1, :]] * (width // TILE), axis=1)


def aggregate_kernel(groups, sources, own, devices, *refs):
    fields = refs[:sources]
    cos_ref, sin_ref, wide_ref, polar_ref = refs[sources : sources + 4]
    out, high_s, low_s = refs[-3:]
    blocks = wide_ref.shape[0]
    rows = cos_ref.shape[0] // OCTANTS
    columns = cos_ref.shape[1] // devices
    size = 2 * groups
    wide = sources * own
    row_stride = 2 * blocks
    child_stride = OCTANTS * own * row_stride

    for octant in range(OCTANTS):
        given = []
        for field in fields:
            for row in range(own):
                start = (octant * own + row) * row_stride
                given.append(
                    jnp.concatenate(
                        [
                            jnp.concatenate(
                                [field[pl.ds(start + 2 * block + part, groups, stride=child_stride), :] for part in range(2)],
                                axis=0,
                            )
                            for block in range(blocks)
                        ],
                        axis=1,
                    )
                )
        for first in range(0, rows, 2):
            pair = []
            for row in (first, first + 1):
                total = given[0] * polar_splat(polar_ref, row * wide, blocks * TILE)
                for place in range(1, wide):
                    total += given[place] * polar_splat(polar_ref, row * wide + place, blocks * TILE)
                pair.append(total)
            high, low = split_two(jnp.concatenate(pair, axis=0))
            target = slice((octant * rows + first) * size, (octant * rows + first + 2) * size)
            high_s[target, :] = high
            low_s[target, :] = low

    lane = iota((OCTANTS * rows * size, TILE), 1)

    def windows(value, block):
        main = value[:, block * TILE : (block + 1) * TILE]
        after, before = (block + 1) % blocks, (block - 1) % blocks
        rim = jnp.where(lane < HALF, value[:, after * TILE : (after + 1) * TILE], value[:, before * TILE : (before + 1) * TILE])
        return [main, rim]

    for block in range(blocks):
        one, two = windows(high_s, block), windows(low_s, block)
        left = jnp.concatenate(one + two + one, axis=1)
        right = jnp.concatenate([wide_ref[block, :PAIR], wide_ref[block, :PAIR], wide_ref[block, PAIR:]], axis=0)
        spread = product(left, right)
        part = slice(block * PAIR, (block + 1) * PAIR)
        summed = []
        for row in range(rows):
            direct = jnp.zeros((size, PAIR), F32)
            crossed = jnp.zeros((size, PAIR), F32)
            for octant in range(OCTANTS):
                start = (octant * rows + row) * size
                turn = slice(row * OCTANTS + octant, row * OCTANTS + octant + 1)
                direct += spread[start : start + size] * cos_ref[turn, part]
                crossed += spread[start : start + size] * sin_ref[turn, part]
            summed.append(direct + jnp.concatenate([-crossed[groups:], crossed[:groups]], axis=0))
        for first in range(0, rows, 2):
            target = slice(first // 2 * size, (first // 2 + 1) * size)
            for place, piece in enumerate(packed_pieces(summed[first], summed[first + 1], columns)):
                out[block * PAIR // columns + place, target, :] = piece


def packed_pieces(one, two, columns):
    found = []
    if columns == HALF:
        lane = iota((one.shape[0], TILE), 1)
        for start in range(0, one.shape[1], TILE):
            a, b = one[:, start : start + TILE], two[:, start : start + TILE]
            found.append(jnp.where(lane < HALF, a, turned(b)))
            found.append(jnp.where(lane < HALF, turned(a), b))
        return found
    for start in range(0, one.shape[1], columns):
        found.append(jnp.concatenate([one[:, start : start + columns], two[:, start : start + columns]], axis=1))
    return found


def unpacked_pieces(blocks, columns):
    if columns == HALF:
        one, two = [], []
        for a, b in zip(blocks[::2], blocks[1::2]):
            lane = iota(a.shape, 1)
            one.append(jnp.where(lane < HALF, a, turned(b)))
            two.append(jnp.where(lane < HALF, turned(a), b))
        return [jnp.concatenate(one, axis=1), jnp.concatenate(two, axis=1)]
    return [
        jnp.concatenate([block[:, :columns] for block in blocks], axis=1),
        jnp.concatenate([block[:, columns:] for block in blocks], axis=1),
    ]


def tables_kernel(sources, rows, *refs):
    count = 3
    remote, phases = refs[:count], refs[count : count + sources - 1]
    outs = refs[count + sources : -count - 1]
    local, sems = refs[-count - 1 : -1], refs[-1]
    listed_ref, vector_ref, table_ref = local
    hot_ref, chosen_ref, table_out, *turned_refs = outs
    copies = started(remote, local, sems)
    for place, phase in enumerate(phases):
        turned_refs[2 * place][...], turned_refs[2 * place + 1][...] = turns(phase[...])

    copies[2].wait()
    raw = table_ref[...]
    many, width = raw.shape
    vectors = many // (2 * rows)
    at, place = iota((many, many), 1), iota((many, many), 0)
    order = one_hot(at == place % vectors * (2 * rows) + place // (2 * vectors) * 2 + place // vectors % 2)
    twice = one_hot(iota((width, 2 * width), 1) % width == iota((width, 2 * width), 0))
    lane = iota((vectors, 2 * width), 1)
    for piece, part in enumerate(split_three(raw)):
        double = product(product(order, part).astype(BF16), twice)
        target = slice(piece * vectors, (piece + 1) * vectors)
        for kind in range(2):
            for first in range(0, rows, 2):
                one, two = (double[(2 * row + kind) * vectors : (2 * row + kind + 1) * vectors] for row in (first, first + 1))
                start = (kind * rows + first) * width
                table_out[target, start : start + 2 * width] = jnp.where(lane < width, one, two).astype(BF16)

    copies[0].wait()
    copies[1].wait()
    partners, clusters = listed_ref.shape
    unit = one_hot(iota((clusters, clusters), 0) == iota((clusters, clusters), 1))
    listed = sum(product(unit, half, 1, 1) for half in split_two(listed_ref[...].astype(F32)))
    chosen = sum(product(unit, half, 1, 1) for half in split_two(vector_ref[...].astype(F32)))
    cluster = (iota((clusters, 2 * clusters), 1) % clusters).astype(F32)
    vector = (iota((clusters, 3 * vectors), 1) % vectors).astype(F32)
    for partner in range(partners):
        part = slice(partner * clusters, (partner + 1) * clusters)
        hot_ref[part, :] = one_hot(cluster == listed[:, partner : partner + 1])
        chosen_ref[part, :] = one_hot(vector == chosen[:, partner : partner + 1])


def translate_kernel(groups, hot_ref, chosen_ref, table_ref, arrived_ref, out):
    devices, tall, width = arrived_ref.shape
    clusters = devices * groups
    partners = chosen_ref.shape[0] // clusters
    size = 2 * groups
    steps = tall // size
    starts = [step * size + part * groups for part in range(2) for step in range(steps)]
    source = jnp.concatenate(
        [arrived_ref[:, start : start + groups, :].reshape(clusters, width) for start in starts], axis=1
    )
    gathered = product(hot_ref[...], jnp.concatenate(split_two(source), axis=0))
    factors = product(chosen_ref[...], table_ref[...])
    for step in range(steps):
        lanes = slice(step * width, (step + 1) * width)
        other = slice((steps + step) * width, (steps + step + 1) * width)
        real = jnp.zeros((clusters, width), F32)
        imag = jnp.zeros((clusters, width), F32)
        for partner in range(partners):
            part = slice(partner * clusters, (partner + 1) * clusters)
            a, b = gathered[part, lanes], gathered[part, other]
            real += a * factors[part, lanes] - b * factors[part, other]
            imag += a * factors[part, other] + b * factors[part, lanes]
        for device in range(devices):
            rows = slice(device * groups, (device + 1) * groups)
            out[device, step * size : (step + 1) * size, :] = jnp.concatenate([real[rows], imag[rows]], axis=0)


def unpacked_fields(arrived_ref, size, columns):
    fields = []
    for start in range(0, arrived_ref.shape[1], size):
        fields += unpacked_pieces([arrived_ref[device, start : start + size, :] for device in range(arrived_ref.shape[0])], columns)
    return fields


def coarse_columns(fields, cos_ref, sin_ref, wide_ref):
    blocks = wide_ref.shape[0]
    rows, size = len(fields), fields[0].shape[0]
    groups = size // 2
    crossed = [jnp.concatenate([field[groups:], -field[:groups]], axis=0) for field in fields]
    mains, rims = [], []
    for block in range(blocks):
        part = slice(block * PAIR, (block + 1) * PAIR)
        lowered = []
        for octant in range(OCTANTS):
            for row in range(rows):
                turn = slice(row * OCTANTS + octant, row * OCTANTS + octant + 1)
                lowered.append(fields[row][:, part] * cos_ref[turn, part] + crossed[row][:, part] * sin_ref[turn, part])
        high, low = split_two(jnp.concatenate(lowered, axis=0))
        left = jnp.concatenate([high, low, high], axis=1)
        right = jnp.concatenate([wide_ref[block, :PAIR], wide_ref[block, :PAIR], wide_ref[block, PAIR:]], axis=1)
        both = product(left, right, 1, 1)
        mains.append(both[:, :TILE])
        rims.append(both[:, TILE:])
    lane = iota((OCTANTS * rows * size, TILE), 1)
    return jnp.concatenate(
        [
            mains[block] + jnp.where(lane < HALF, rims[(block - 1) % blocks], rims[(block + 1) % blocks])
            for block in range(blocks)
        ],
        axis=1,
    )


def anterpolated(coarse, polar_ref, octant, place, rows, size, wide):
    total = None
    for row in range(rows):
        start = (octant * rows + row) * size
        term = coarse[start : start + size] * polar_splat(polar_ref, row * wide + place, coarse.shape[1])
        total = term if total is None else total + term
    return total


def lower_kernel(groups, own, arrived_ref, cos_ref, sin_ref, wide_ref, polar_ref, parent_out, partial_ref, parent_ref, sem):
    devices = arrived_ref.shape[0]
    azimuth = cos_ref.shape[1]
    size = 2 * groups
    fields = unpacked_fields(arrived_ref, size, azimuth // devices)
    rows = len(fields)
    wide = polar_ref.shape[0] // rows
    tiles = azimuth // TILE
    for row, field in enumerate(fields):
        for tile in range(tiles):
            for part in range(2):
                start = (row * tiles + tile) * 2 + part
                parent_ref[pl.ds(start, groups, stride=rows * tiles * 2), :] = field[
                    part * groups : (part + 1) * groups, tile * TILE : (tile + 1) * TILE
                ]
    copy = pltpu.make_async_copy(parent_ref, parent_out, sem)
    copy.start()
    coarse = coarse_columns(fields, cos_ref, sin_ref, wide_ref)
    for octant in range(OCTANTS):
        for row in range(own):
            start = (octant * own + row) * size
            partial_ref[start : start + size, :] = anterpolated(coarse, polar_ref, octant, row, rows, size, wide)
    copy.wait()


def finish_kernel(groups, sources, own, *refs):
    arrived = refs[: sources - 1]
    turned_refs = refs[sources - 1 : 3 * (sources - 1)]
    wide_ref, polar_ref, partial_ref, out = refs[3 * (sources - 1) :]
    blocks = wide_ref.shape[0]
    azimuth = turned_refs[0].shape[1]
    size = 2 * groups
    coarse = []
    for place, field in enumerate(arrived):
        fields = unpacked_fields(field, size, azimuth // field.shape[0])
        coarse.append(coarse_columns(fields, turned_refs[2 * place], turned_refs[2 * place + 1], wide_ref))
    rows = len(fields)
    wide = sources * own
    row_stride = 2 * blocks
    for octant in range(OCTANTS):
        for row in range(own):
            start = (octant * own + row) * size
            value = partial_ref[start : start + size, :]
            for place in range(sources - 1):
                value += anterpolated(coarse[place], polar_ref, octant, (place + 1) * own + row, rows, size, wide)
            for block in range(blocks):
                for part in range(2):
                    first = (octant * own + row) * row_stride + 2 * block + part
                    out[pl.ds(first, groups, stride=OCTANTS * own * row_stride), :] = value[
                        part * groups : (part + 1) * groups, block * TILE : (block + 1) * TILE
                    ]


def call(kernel, outs, args, flops, name, remote=(), after=(), far=(), scratch=(), into=0):
    held = sum(4 * leaf.size for leaf in outs) + sum(4 * arg.size for arg in (*remote, *args))
    remote = [pltpu.with_memory_space_constraint(arg, pltpu.HBM) for arg in remote]
    scratch = [*scratch, *(pltpu.VMEM(arg.shape, arg.dtype) for arg in remote[: len(remote) - into])]
    if remote:
        scratch.append(pltpu.SemaphoreType.DMA((len(remote),)))
    near, away, free = (pl.BlockSpec(memory_space=space) for space in (pltpu.VMEM, pltpu.HBM, pl.ANY))
    return pl.pallas_call(
        kernel,
        out_shape=outs,
        in_specs=[away] * len(remote) + [near] * len(args) + [free] * len(after),
        out_specs=[free if place in far else near for place in range(len(outs))],
        scratch_shapes=scratch,
        compiler_params=pltpu.CompilerParams(vmem_limit_bytes=max(VMEM_BYTES, 8 * max(arg.size for arg in (*remote, *args)))),
        cost_estimate=pl.CostEstimate(flops=flops, bytes_accessed=held, transcendentals=0),
        name=name,
    )(*remote, *args, *after)


def bind(kernel, *settings):
    return lambda *refs: kernel(*settings, *refs)


def exchange(blocks):
    return lax.all_to_all(blocks, "clus", split_axis=0, concat_axis=0, tiled=True)


def per_device(child_patterns, theta_weights, phi_stencil, phi_weights, shift_phase, translation_table, far_list, far_vector):
    devices, halves = lax.axis_size("clus"), lax.axis_size("samp")
    children, _, own, columns = child_patterns.shape
    groups = children // OCTANTS
    rows, azimuth = theta_weights.shape[0], phi_stencil.shape[0]
    clusters, partners = far_list.shape
    vectors, width = translation_table.shape[0], 2 * translation_table.shape[3]
    blocks, rows_all = columns // TILE, groups * rows
    long = children * own
    sources = 2 if halves == 2 else 3
    struct = jax.ShapeDtypeStruct
    forward = [(i, (i + 1) % halves) for i in range(halves)]
    backward = [((i + 1) % halves, i) for i in range(halves)]

    field = child_patterns.reshape(children, 2, own, blocks, TILE).transpose(0, 2, 3, 1, 4).reshape(long * blocks * 2, TILE)
    neighbours = [lax.ppermute(field, "samp", forward)]
    if sources == 3:
        neighbours.append(lax.ppermute(field, "samp", backward))
    phase = shift_phase.transpose(1, 0, 2).reshape(rows * OCTANTS, azimuth)
    ways = [backward] if sources == 2 else [backward, forward]
    phases = [lax.ppermute(phase, "samp", way) for way in ways]
    table = translation_table.transpose(0, 2, 1, 3).reshape(vectors * rows * 2, width // 2)
    turn = struct((rows * OCTANTS, azimuth), F32)

    cosine, sine, wide, polar, held = call(
        bind(prepare_kernel, sources, own),
        [
            turn,
            turn,
            struct((blocks, 2 * PAIR, PAIR), BF16),
            struct((rows * sources * own, TILE), F32),
            struct(field.shape, F32),
        ],
        [],
        400_000_000,
        "prepare",
        [theta_weights, phase, phi_stencil.T, phi_weights.T, field],
        into=1,
    )
    (outgoing,) = call(
        bind(aggregate_kernel, groups, sources, own, devices),
        [struct((devices, rows_all, width), F32)],
        [held, *neighbours, cosine, sine, wide, polar],
        1_500_000_000,
        "aggregate",
        scratch=[pltpu.VMEM((2 * groups * OCTANTS * rows, columns), BF16)] * 2,
    )
    arrived = exchange(outgoing)
    hot, chosen, factors, *turned_parts = call(
        bind(tables_kernel, sources, rows),
        [
            struct((partners * clusters, 2 * clusters), BF16),
            struct((partners * clusters, 3 * vectors), BF16),
            struct((3 * vectors, rows * width), BF16),
        ]
        + [turn] * (2 * sources - 2),
        phases,
        600_000_000,
        "tables",
        [far_list.T, far_vector.T, table],
        [outgoing],
    )
    (translated,) = call(
        bind(translate_kernel, groups),
        [struct((devices, rows_all, width), F32)],
        [hot, chosen, factors, arrived],
        600_000_000,
        "translate",
    )
    returned = exchange(translated)
    size = rows_all * 2 * azimuth // TILE
    parent, partial = call(
        bind(lower_kernel, groups, own),
        [struct((size, TILE), F32), struct((2 * long, columns), F32)],
        [returned, cosine, sine, wide, polar],
        1_500_000_000,
        "lower",
        far=(0,),
        scratch=[pltpu.VMEM((size, TILE), F32), pltpu.SemaphoreType.DMA],
    )
    returned_parts = [lax.ppermute(returned, "samp", way) for way in ways]
    (total,) = call(
        bind(finish_kernel, groups, sources, own),
        [struct((long * blocks * 2, TILE), F32)],
        [*returned_parts, *turned_parts, wide, polar, partial],
        1_500_000_000,
        "finish",
    )
    child_incoming = total.reshape(children, own, blocks, 2, TILE).transpose(0, 3, 1, 2, 4).reshape(children, 2, own, columns)
    parent_incoming = (
        parent.reshape(groups, rows, azimuth // TILE, 2, TILE).transpose(0, 3, 1, 2, 4).reshape(groups, 2, rows, azimuth)
    )
    return (parent_incoming, child_incoming)


def solution(mesh):
    placed = (
        P("clus", None, "samp", None),
        P(),
        P(),
        P(),
        P(None, "samp", None),
        P(None, None, "samp", "clus"),
        P(),
        P(),
    )
    return jax.shard_map(
        per_device,
        mesh=mesh,
        in_specs=placed,
        out_specs=(P("clus", None, "samp", None), P("clus", None, "samp", None)),
        check_vma=False,
    )
```

```python
import jax
import jax.numpy as jnp
from jax import lax
from jax.experimental import pallas as pl
from jax.experimental.pallas import tpu as pltpu
from jax.sharding import PartitionSpec as P

P_SIZE = 6
OCTANTS = 8
SUBLANES = 8
TILE = 128
PAIR = 2 * TILE
HALF = TILE // 2
VMEM_BYTES = 8 * 1024 * 1024
F32 = jnp.float32
BF16 = jnp.bfloat16

SIN_TERMS = (-1 / 6, 1 / 120, -1 / 5040, 1 / 362880, -1 / 39916800, 1 / 6227020800)
COS_TERMS = (-1 / 2, 1 / 24, -1 / 720, 1 / 40320, -1 / 3628800, 1 / 479001600, -1 / 87178291200)


def split_two(value):
    high = value.astype(BF16)
    return high, (value - high.astype(F32)).astype(BF16)


def split_three(value):
    high = value.astype(BF16)
    rest = value - high.astype(F32)
    middle = rest.astype(BF16)
    return high, middle, (rest - middle.astype(F32)).astype(BF16)


def product(left, right, left_dim=1, right_dim=0):
    return lax.dot_general(left, right, (((left_dim,), (right_dim,)), ((), ())), preferred_element_type=F32)


def series(square, terms):
    total = jnp.full_like(square, terms[-1])
    for term in terms[-2::-1]:
        total = total * square + term
    return total


def iota(shape, dim):
    return lax.broadcasted_iota(jnp.int32, shape, dim)


def one_hot(flags):
    return flags.astype(F32).astype(BF16)


def turned(block):
    return jnp.roll(block, HALF, axis=1)


def folded(theta, sources, own):
    below, middle, above = theta[:, :own], theta[:, own : 2 * own], theta[:, 2 * own :]
    return jnp.concatenate((middle, below + above) if sources == 2 else (middle, below, above), axis=1)


def turns(phase):
    half = 0.5 * phase
    square = half * half
    sine = half + half * square * series(square, SIN_TERMS)
    cosine = 1.0 + square * series(square, COS_TERMS)
    return 1.0 - 2.0 * sine * sine, 2.0 * sine * cosine


def started(remote, local, sems):
    copies = [pltpu.make_async_copy(source, target, sems.at[place]) for place, (source, target) in enumerate(zip(remote, local))]
    for copy in copies:
        copy.start()
    return copies


def prepare_kernel(sources, own, *refs):
    count = 5
    remote, outs, rest = refs[:count], refs[count : count + 5], refs[count + 5 :]
    cos_ref, sin_ref, wide_ref, polar_ref, field_out = outs
    theta_ref, phase_ref, stencil_ref, weight_ref, sems = rest
    copies = started(remote, [theta_ref, phase_ref, stencil_ref, weight_ref, field_out], sems)
    rows = theta_ref.shape[0]
    blocks = wide_ref.shape[0]

    wide = sources * own
    tall = rows * wide * SUBLANES
    at_row = one_hot(iota((tall, rows), 0) // (wide * SUBLANES) == iota((tall, rows), 1))
    keep = iota((tall, wide), 0) // SUBLANES % wide == iota((tall, wide), 1)
    ones = jnp.ones((wide, TILE), BF16)
    copies[0].wait()
    parts = [
        product(jnp.where(keep, product(at_row, part), 0.0).astype(BF16), ones)
        for part in split_three(folded(theta_ref[...], sources, own))
    ]
    polar_ref[...] = parts[0] + (parts[1] + parts[2])

    copies[1].wait()
    keep_turns(phase_ref[...], cos_ref, sin_ref)

    copies[2].wait()
    copies[3].wait()
    for block in range(blocks):
        columns = slice(block * PAIR, (block + 1) * PAIR)
        after, before = (block + 1) % blocks, (block - 1) % blocks
        pieces = (
            (0, TILE, block * TILE),
            (TILE, 16, after * TILE),
            (PAIR - 16, 16, before * TILE + TILE - 16),
        )
        for start, size, first in pieces:
            child = iota((size, PAIR), 0) + first
            total = jnp.zeros((size, PAIR), F32)
            for point in range(P_SIZE):
                hit = stencil_ref[point : point + 1, columns] == child
                total = jnp.where(hit, weight_ref[point : point + 1, columns], total)
            high, low = split_two(total)
            wide_ref[block, start : start + size, :] = high
            wide_ref[block, PAIR + start : PAIR + start + size, :] = low
        empty = jnp.zeros((TILE - 32, PAIR), BF16)
        wide_ref[block, TILE + 16 : PAIR - 16, :] = empty
        wide_ref[block, PAIR + TILE + 16 : 2 * PAIR - 16, :] = empty
    copies[4].wait()


def polar_splat(polar_ref, row, width):
    return jnp.concatenate([polar_ref[row * SUBLANES : (row + 1) * SUBLANES, :]] * (width // TILE), axis=1)


def turn_splat(turn_ref, row, block, size):
    return jnp.concatenate([turn_ref[2 * block + half, pl.ds(row, size, stride=0), :] for half in range(2)], axis=1)


def keep_turns(phase, cos_ref, sin_ref):
    count = phase.shape[0]
    for value, target in zip(turns(phase), (cos_ref, sin_ref)):
        for tile in range(target.shape[0]):
            target[tile, :count, :] = value[:, tile * TILE : (tile + 1) * TILE]
            target[tile, count:, :] = jnp.zeros((target.shape[1] - count, TILE), F32)


def aggregate_kernel(groups, sources, own, devices, *refs):
    fields = refs[:sources]
    cos_ref, sin_ref, wide_ref, polar_ref = refs[sources : sources + 4]
    out, high_s, low_s = refs[-3:]
    blocks = wide_ref.shape[0]
    rows = cos_ref.shape[1] // OCTANTS - 1
    columns = cos_ref.shape[0] * TILE // devices
    size = 2 * groups
    wide = sources * own
    row_stride = 2 * blocks
    child_stride = OCTANTS * own * row_stride

    for octant in range(OCTANTS):
        given = []
        for field in fields:
            for row in range(own):
                start = (octant * own + row) * row_stride
                given.append(
                    jnp.concatenate(
                        [
                            jnp.concatenate(
                                [field[pl.ds(start + 2 * block + part, groups, stride=child_stride), :] for part in range(2)],
                                axis=0,
                            )
                            for block in range(blocks)
                        ],
                        axis=1,
                    )
                )
        for first in range(0, rows, 2):
            pair = []
            for row in (first, first + 1):
                total = given[0] * polar_splat(polar_ref, row * wide, blocks * TILE)
                for place in range(1, wide):
                    total += given[place] * polar_splat(polar_ref, row * wide + place, blocks * TILE)
                pair.append(total)
            high, low = split_two(jnp.concatenate(pair, axis=0))
            target = slice((octant * rows + first) * size, (octant * rows + first + 2) * size)
            high_s[target, :] = high
            low_s[target, :] = low

    lane = iota((OCTANTS * rows * size, TILE), 1)

    def windows(value, block):
        main = value[:, block * TILE : (block + 1) * TILE]
        after, before = (block + 1) % blocks, (block - 1) % blocks
        rim = jnp.where(lane < HALF, value[:, after * TILE : (after + 1) * TILE], value[:, before * TILE : (before + 1) * TILE])
        return [main, rim]

    for block in range(blocks):
        one, two = windows(high_s, block), windows(low_s, block)
        left = jnp.concatenate(one + two + one, axis=1)
        right = jnp.concatenate([wide_ref[block, :PAIR], wide_ref[block, :PAIR], wide_ref[block, PAIR:]], axis=0)
        spread = product(left, right)
        summed = []
        for row in range(rows):
            direct = jnp.zeros((size, PAIR), F32)
            crossed = jnp.zeros((size, PAIR), F32)
            for octant in range(OCTANTS):
                start = (octant * rows + row) * size
                turn = row * OCTANTS + octant
                direct += spread[start : start + size] * turn_splat(cos_ref, turn, block, size)
                crossed += spread[start : start + size] * turn_splat(sin_ref, turn, block, size)
            summed.append(direct + jnp.concatenate([-crossed[groups:], crossed[:groups]], axis=0))
        for first in range(0, rows, 2):
            target = slice(first // 2 * size, (first // 2 + 1) * size)
            for place, piece in enumerate(packed_pieces(summed[first], summed[first + 1], columns)):
                out[block * PAIR // columns + place, target, :] = piece


def packed_pieces(one, two, columns):
    found = []
    if columns == HALF:
        lane = iota((one.shape[0], TILE), 1)
        for start in range(0, one.shape[1], TILE):
            a, b = one[:, start : start + TILE], two[:, start : start + TILE]
            found.append(jnp.where(lane < HALF, a, turned(b)))
            found.append(jnp.where(lane < HALF, turned(a), b))
        return found
    for start in range(0, one.shape[1], columns):
        found.append(jnp.concatenate([one[:, start : start + columns], two[:, start : start + columns]], axis=1))
    return found


def unpacked_pieces(blocks, columns):
    if columns == HALF:
        one, two = [], []
        for a, b in zip(blocks[::2], blocks[1::2]):
            lane = iota(a.shape, 1)
            one.append(jnp.where(lane < HALF, a, turned(b)))
            two.append(jnp.where(lane < HALF, turned(a), b))
        return [jnp.concatenate(one, axis=1), jnp.concatenate(two, axis=1)]
    return [
        jnp.concatenate([block[:, :columns] for block in blocks], axis=1),
        jnp.concatenate([block[:, columns:] for block in blocks], axis=1),
    ]


def tables_kernel(sources, rows, *refs):
    count = 3
    remote, phases = refs[:count], refs[count : count + sources - 1]
    outs = refs[count + sources : -count - 1]
    local, sems = refs[-count - 1 : -1], refs[-1]
    listed_ref, vector_ref, table_ref = local
    hot_ref, chosen_ref, table_out, *turned_refs = outs
    copies = started(remote, local, sems)
    for place, phase in enumerate(phases):
        keep_turns(phase[...], turned_refs[2 * place], turned_refs[2 * place + 1])

    copies[2].wait()
    raw = table_ref[...]
    many, width = raw.shape
    vectors = many // (2 * rows)
    at, place = iota((many, many), 1), iota((many, many), 0)
    order = one_hot(at == place % vectors * (2 * rows) + place // (2 * vectors) * 2 + place // vectors % 2)
    twice = one_hot(iota((width, 2 * width), 1) % width == iota((width, 2 * width), 0))
    lane = iota((vectors, 2 * width), 1)
    for piece, part in enumerate(split_three(raw)):
        double = product(product(order, part).astype(BF16), twice)
        target = slice(piece * vectors, (piece + 1) * vectors)
        for kind in range(2):
            for first in range(0, rows, 2):
                one, two = (double[(2 * row + kind) * vectors : (2 * row + kind + 1) * vectors] for row in (first, first + 1))
                start = (kind * rows + first) * width
                table_out[target, start : start + 2 * width] = jnp.where(lane < width, one, two).astype(BF16)

    copies[0].wait()
    copies[1].wait()
    partners, clusters = listed_ref.shape
    unit = one_hot(iota((clusters, clusters), 0) == iota((clusters, clusters), 1))
    listed = sum(product(unit, half, 1, 1) for half in split_two(listed_ref[...].astype(F32)))
    chosen = sum(product(unit, half, 1, 1) for half in split_two(vector_ref[...].astype(F32)))
    cluster = (iota((clusters, 2 * clusters), 1) % clusters).astype(F32)
    vector = (iota((clusters, 3 * vectors), 1) % vectors).astype(F32)
    for partner in range(partners):
        part = slice(partner * clusters, (partner + 1) * clusters)
        hot_ref[part, :] = one_hot(cluster == listed[:, partner : partner + 1])
        chosen_ref[part, :] = one_hot(vector == chosen[:, partner : partner + 1])


def translate_kernel(groups, hot_ref, chosen_ref, table_ref, arrived_ref, out):
    devices, tall, width = arrived_ref.shape
    clusters = devices * groups
    partners = chosen_ref.shape[0] // clusters
    size = 2 * groups
    steps = tall // size
    starts = [step * size + part * groups for part in range(2) for step in range(steps)]
    source = jnp.concatenate(
        [arrived_ref[:, start : start + groups, :].reshape(clusters, width) for start in starts], axis=1
    )
    gathered = product(hot_ref[...], jnp.concatenate(split_two(source), axis=0))
    factors = product(chosen_ref[...], table_ref[...])
    for step in range(steps):
        lanes = slice(step * width, (step + 1) * width)
        other = slice((steps + step) * width, (steps + step + 1) * width)
        real = jnp.zeros((clusters, width), F32)
        imag = jnp.zeros((clusters, width), F32)
        for partner in range(partners):
            part = slice(partner * clusters, (partner + 1) * clusters)
            a, b = gathered[part, lanes], gathered[part, other]
            real += a * factors[part, lanes] - b * factors[part, other]
            imag += a * factors[part, other] + b * factors[part, lanes]
        for device in range(devices):
            rows = slice(device * groups, (device + 1) * groups)
            out[device, step * size : (step + 1) * size, :] = jnp.concatenate([real[rows], imag[rows]], axis=0)


def unpacked_fields(arrived_ref, size, columns):
    fields = []
    for start in range(0, arrived_ref.shape[1], size):
        fields += unpacked_pieces([arrived_ref[device, start : start + size, :] for device in range(arrived_ref.shape[0])], columns)
    return fields


def coarse_columns(fields, cos_ref, sin_ref, wide_ref):
    blocks = wide_ref.shape[0]
    rows, size = len(fields), fields[0].shape[0]
    groups = size // 2
    crossed = [jnp.concatenate([field[groups:], -field[:groups]], axis=0) for field in fields]
    mains, rims = [], []
    for block in range(blocks):
        part = slice(block * PAIR, (block + 1) * PAIR)
        lowered = []
        for octant in range(OCTANTS):
            for row in range(rows):
                turn = row * OCTANTS + octant
                lowered.append(
                    fields[row][:, part] * turn_splat(cos_ref, turn, block, size)
                    + crossed[row][:, part] * turn_splat(sin_ref, turn, block, size)
                )
        high, low = split_two(jnp.concatenate(lowered, axis=0))
        left = jnp.concatenate([high, low, high], axis=1)
        right = jnp.concatenate([wide_ref[block, :PAIR], wide_ref[block, :PAIR], wide_ref[block, PAIR:]], axis=1)
        both = product(left, right, 1, 1)
        mains.append(both[:, :TILE])
        rims.append(both[:, TILE:])
    lane = iota((OCTANTS * rows * size, TILE), 1)
    return jnp.concatenate(
        [
            mains[block] + jnp.where(lane < HALF, rims[(block - 1) % blocks], rims[(block + 1) % blocks])
            for block in range(blocks)
        ],
        axis=1,
    )


def anterpolated(coarse, polar_ref, octant, place, rows, size, wide):
    total = None
    for row in range(rows):
        start = (octant * rows + row) * size
        term = coarse[start : start + size] * polar_splat(polar_ref, row * wide + place, coarse.shape[1])
        total = term if total is None else total + term
    return total


def lower_kernel(groups, own, arrived_ref, cos_ref, sin_ref, wide_ref, polar_ref, parent_out, partial_ref, parent_ref, sem):
    devices = arrived_ref.shape[0]
    azimuth = cos_ref.shape[0] * TILE
    size = 2 * groups
    fields = unpacked_fields(arrived_ref, size, azimuth // devices)
    rows = len(fields)
    wide = polar_ref.shape[0] // (rows * SUBLANES)
    tiles = azimuth // TILE
    for row, field in enumerate(fields):
        for tile in range(tiles):
            for part in range(2):
                start = (row * tiles + tile) * 2 + part
                parent_ref[pl.ds(start, groups, stride=rows * tiles * 2), :] = field[
                    part * groups : (part + 1) * groups, tile * TILE : (tile + 1) * TILE
                ]
    copy = pltpu.make_async_copy(parent_ref, parent_out, sem)
    copy.start()
    coarse = coarse_columns(fields, cos_ref, sin_ref, wide_ref)
    for octant in range(OCTANTS):
        for row in range(own):
            start = (octant * own + row) * size
            partial_ref[start : start + size, :] = anterpolated(coarse, polar_ref, octant, row, rows, size, wide)
    copy.wait()


def finish_kernel(groups, sources, own, *refs):
    arrived = refs[: sources - 1]
    turned_refs = refs[sources - 1 : 3 * (sources - 1)]
    wide_ref, polar_ref, partial_ref, out = refs[3 * (sources - 1) :]
    blocks = wide_ref.shape[0]
    azimuth = turned_refs[0].shape[0] * TILE
    size = 2 * groups
    coarse = []
    for place, field in enumerate(arrived):
        fields = unpacked_fields(field, size, azimuth // field.shape[0])
        coarse.append(coarse_columns(fields, turned_refs[2 * place], turned_refs[2 * place + 1], wide_ref))
    rows = len(fields)
    wide = sources * own
    row_stride = 2 * blocks
    for octant in range(OCTANTS):
        for row in range(own):
            start = (octant * own + row) * size
            value = partial_ref[start : start + size, :]
            for place in range(sources - 1):
                value += anterpolated(coarse[place], polar_ref, octant, (place + 1) * own + row, rows, size, wide)
            for block in range(blocks):
                for part in range(2):
                    first = (octant * own + row) * row_stride + 2 * block + part
                    out[pl.ds(first, groups, stride=OCTANTS * own * row_stride), :] = value[
                        part * groups : (part + 1) * groups, block * TILE : (block + 1) * TILE
                    ]


def call(kernel, outs, args, flops, name, remote=(), after=(), far=(), scratch=(), into=0):
    held = sum(4 * leaf.size for leaf in outs) + sum(4 * arg.size for arg in (*remote, *args))
    remote = [pltpu.with_memory_space_constraint(arg, pltpu.HBM) for arg in remote]
    scratch = [*scratch, *(pltpu.VMEM(arg.shape, arg.dtype) for arg in remote[: len(remote) - into])]
    if remote:
        scratch.append(pltpu.SemaphoreType.DMA((len(remote),)))
    near, away, free = (pl.BlockSpec(memory_space=space) for space in (pltpu.VMEM, pltpu.HBM, pl.ANY))
    return pl.pallas_call(
        kernel,
        out_shape=outs,
        in_specs=[away] * len(remote) + [near] * len(args) + [free] * len(after),
        out_specs=[free if place in far else near for place in range(len(outs))],
        scratch_shapes=scratch,
        compiler_params=pltpu.CompilerParams(vmem_limit_bytes=max(VMEM_BYTES, 8 * max(arg.size for arg in (*remote, *args)))),
        cost_estimate=pl.CostEstimate(flops=flops, bytes_accessed=held, transcendentals=0),
        name=name,
    )(*remote, *args, *after)


def bind(kernel, *settings):
    return lambda *refs: kernel(*settings, *refs)


def exchange(blocks):
    return lax.all_to_all(blocks, "clus", split_axis=0, concat_axis=0, tiled=True)


def per_device(child_patterns, theta_weights, phi_stencil, phi_weights, shift_phase, translation_table, far_list, far_vector):
    devices, halves = lax.axis_size("clus"), lax.axis_size("samp")
    children, _, own, columns = child_patterns.shape
    groups = children // OCTANTS
    rows, azimuth = theta_weights.shape[0], phi_stencil.shape[0]
    clusters, partners = far_list.shape
    vectors, width = translation_table.shape[0], 2 * translation_table.shape[3]
    blocks, rows_all = columns // TILE, groups * rows
    long = children * own
    sources = 2 if halves == 2 else 3
    struct = jax.ShapeDtypeStruct
    forward = [(i, (i + 1) % halves) for i in range(halves)]
    backward = [((i + 1) % halves, i) for i in range(halves)]

    field = child_patterns.reshape(children, 2, own, blocks, TILE).transpose(0, 2, 3, 1, 4).reshape(long * blocks * 2, TILE)
    neighbours = [lax.ppermute(field, "samp", forward)]
    if sources == 3:
        neighbours.append(lax.ppermute(field, "samp", backward))
    phase = shift_phase.transpose(1, 0, 2).reshape(rows * OCTANTS, azimuth)
    ways = [backward] if sources == 2 else [backward, forward]
    phases = [lax.ppermute(phase, "samp", way) for way in ways]
    table = translation_table.transpose(0, 2, 1, 3).reshape(vectors * rows * 2, width // 2)
    turn = struct((azimuth // TILE, rows * OCTANTS + OCTANTS, TILE), F32)

    cosine, sine, wide, polar, held = call(
        bind(prepare_kernel, sources, own),
        [
            turn,
            turn,
            struct((blocks, 2 * PAIR, PAIR), BF16),
            struct((rows * sources * own * SUBLANES, TILE), F32),
            struct(field.shape, F32),
        ],
        [],
        400_000_000,
        "prepare",
        [theta_weights, phase, phi_stencil.T, phi_weights.T, field],
        into=1,
    )
    (outgoing,) = call(
        bind(aggregate_kernel, groups, sources, own, devices),
        [struct((devices, rows_all, width), F32)],
        [held, *neighbours, cosine, sine, wide, polar],
        1_500_000_000,
        "aggregate",
        scratch=[pltpu.VMEM((2 * groups * OCTANTS * rows, columns), BF16)] * 2,
    )
    arrived = exchange(outgoing)
    hot, chosen, factors, *turned_parts = call(
        bind(tables_kernel, sources, rows),
        [
            struct((partners * clusters, 2 * clusters), BF16),
            struct((partners * clusters, 3 * vectors), BF16),
            struct((3 * vectors, rows * width), BF16),
        ]
        + [turn] * (2 * sources - 2),
        phases,
        600_000_000,
        "tables",
        [far_list.T, far_vector.T, table],
        [outgoing],
    )
    (translated,) = call(
        bind(translate_kernel, groups),
        [struct((devices, rows_all, width), F32)],
        [hot, chosen, factors, arrived],
        600_000_000,
        "translate",
    )
    returned = exchange(translated)
    size = rows_all * 2 * azimuth // TILE
    parent, partial = call(
        bind(lower_kernel, groups, own),
        [struct((size, TILE), F32), struct((2 * long, columns), F32)],
        [returned, cosine, sine, wide, polar],
        1_500_000_000,
        "lower",
        far=(0,),
        scratch=[pltpu.VMEM((size, TILE), F32), pltpu.SemaphoreType.DMA],
    )
    returned_parts = [lax.ppermute(returned, "samp", way) for way in ways]
    (total,) = call(
        bind(finish_kernel, groups, sources, own),
        [struct((long * blocks * 2, TILE), F32)],
        [*returned_parts, *turned_parts, wide, polar, partial],
        1_500_000_000,
        "finish",
    )
    child_incoming = total.reshape(children, own, blocks, 2, TILE).transpose(0, 3, 1, 2, 4).reshape(children, 2, own, columns)
    parent_incoming = (
        parent.reshape(groups, rows, azimuth // TILE, 2, TILE).transpose(0, 3, 1, 2, 4).reshape(groups, 2, rows, azimuth)
    )
    return (parent_incoming, child_incoming)


def solution(mesh):
    placed = (
        P("clus", None, "samp", None),
        P(),
        P(),
        P(),
        P(None, "samp", None),
        P(None, None, "samp", "clus"),
        P(),
        P(),
    )
    return jax.shard_map(
        per_device,
        mesh=mesh,
        in_specs=placed,
        out_specs=(P("clus", None, "samp", None), P("clus", None, "samp", None)),
        check_vma=False,
    )
```

```python
import jax
import jax.numpy as jnp
from jax import lax
from jax.experimental import pallas as pl
from jax.experimental.pallas import tpu as pltpu
from jax.sharding import PartitionSpec as P

P_SIZE = 6
OCTANTS = 8
TILE = 128
PAIR = 2 * TILE
HALF = TILE // 2
VMEM_BYTES = 8 * 1024 * 1024
F32 = jnp.float32
BF16 = jnp.bfloat16

SIN_TERMS = (-1 / 6, 1 / 120, -1 / 5040, 1 / 362880, -1 / 39916800, 1 / 6227020800)
COS_TERMS = (-1 / 2, 1 / 24, -1 / 720, 1 / 40320, -1 / 3628800, 1 / 479001600, -1 / 87178291200)


def split_two(value):
    high = value.astype(BF16)
    return high, (value - high.astype(F32)).astype(BF16)


def split_three(value):
    high = value.astype(BF16)
    rest = value - high.astype(F32)
    middle = rest.astype(BF16)
    return high, middle, (rest - middle.astype(F32)).astype(BF16)


def product(left, right, left_dim=1, right_dim=0):
    return lax.dot_general(left, right, (((left_dim,), (right_dim,)), ((), ())), preferred_element_type=F32)


def series(square, terms):
    total = jnp.full_like(square, terms[-1])
    for term in terms[-2::-1]:
        total = total * square + term
    return total


def iota(shape, dim):
    return lax.broadcasted_iota(jnp.int32, shape, dim)


def one_hot(flags):
    return flags.astype(F32).astype(BF16)


def turned(block):
    return jnp.roll(block, HALF, axis=1)


def folded(theta, sources, own):
    below, middle, above = theta[:, :own], theta[:, own : 2 * own], theta[:, 2 * own :]
    return jnp.concatenate((middle, below + above) if sources == 2 else (middle, below, above), axis=1)


def turns(phase):
    half = 0.5 * phase
    square = half * half
    sine = half + half * square * series(square, SIN_TERMS)
    cosine = 1.0 + square * series(square, COS_TERMS)
    return 1.0 - 2.0 * sine * sine, 2.0 * sine * cosine


def started(remote, local, sems):
    copies = [pltpu.make_async_copy(source, target, sems.at[place]) for place, (source, target) in enumerate(zip(remote, local))]
    for copy in copies:
        copy.start()
    return copies


def prepare_kernel(sources, own, *refs):
    count = 5
    remote, outs, rest = refs[:count], refs[count : count + 5], refs[count + 5 :]
    cos_ref, sin_ref, wide_ref, polar_ref, field_out = outs
    theta_ref, phase_ref, stencil_ref, weight_ref, sems = rest
    copies = started(remote, [theta_ref, phase_ref, stencil_ref, weight_ref, field_out], sems)
    rows = theta_ref.shape[0]
    blocks = wide_ref.shape[0]

    wide = sources * own
    at_row = one_hot(iota((rows * wide, rows), 0) // wide == iota((rows * wide, rows), 1))
    keep = iota((rows * wide, wide), 0) % wide == iota((rows * wide, wide), 1)
    ones = jnp.ones((wide, TILE), BF16)
    copies[0].wait()
    parts = [
        product(jnp.where(keep, product(at_row, part), 0.0).astype(BF16), ones)
        for part in split_three(folded(theta_ref[...], sources, own))
    ]
    polar_ref[...] = parts[0] + (parts[1] + parts[2])

    copies[1].wait()
    cos_ref[...], sin_ref[...] = turns(phase_ref[...])

    copies[2].wait()
    copies[3].wait()
    for block in range(blocks):
        columns = slice(block * PAIR, (block + 1) * PAIR)
        after, before = (block + 1) % blocks, (block - 1) % blocks
        pieces = (
            (0, TILE, block * TILE),
            (TILE, 16, after * TILE),
            (PAIR - 16, 16, before * TILE + TILE - 16),
        )
        for start, size, first in pieces:
            child = iota((size, PAIR), 0) + first
            total = jnp.zeros((size, PAIR), F32)
            for point in range(P_SIZE):
                hit = stencil_ref[point : point + 1, columns] == child
                total = jnp.where(hit, weight_ref[point : point + 1, columns], total)
            high, low = split_two(total)
            wide_ref[block, start : start + size, :] = high
            wide_ref[block, PAIR + start : PAIR + start + size, :] = low
        empty = jnp.zeros((TILE - 32, PAIR), BF16)
        wide_ref[block, TILE + 16 : PAIR - 16, :] = empty
        wide_ref[block, PAIR + TILE + 16 : 2 * PAIR - 16, :] = empty
    copies[4].wait()


def polar_splat(polar_ref, row, width):
    return jnp.concatenate([polar_ref[row : row + 1, :]] * (width // TILE), axis=1)


def aggregate_kernel(groups, sources, own, devices, *refs):
    fields = refs[:sources]
    cos_ref, sin_ref, wide_ref, polar_ref = refs[sources : sources + 4]
    out, high_s, low_s = refs[-3:]
    blocks = wide_ref.shape[0]
    rows = cos_ref.shape[0] // OCTANTS
    columns = cos_ref.shape[1] // devices
    size = 2 * groups
    wide = sources * own
    row_stride = 2 * blocks
    child_stride = OCTANTS * own * row_stride

    for octant in range(OCTANTS):
        given = []
        for field in fields:
            for row in range(own):
                start = (octant * own + row) * row_stride
                given.append(
                    jnp.concatenate(
                        [
                            jnp.concatenate(
                                [field[pl.ds(start + 2 * block + part, groups, stride=child_stride), :] for part in range(2)],
                                axis=0,
                            )
                            for block in range(blocks)
                        ],
                        axis=1,
                    )
                )
        for first in range(0, rows, 2):
            pair = []
            for row in (first, first + 1):
                total = given[0] * polar_splat(polar_ref, row * wide, blocks * TILE)
                for place in range(1, wide):
                    total += given[place] * polar_splat(polar_ref, row * wide + place, blocks * TILE)
                pair.append(total)
            high, low = split_two(jnp.concatenate(pair, axis=0))
            target = slice((octant * rows + first) * size, (octant * rows + first + 2) * size)
            high_s[target, :] = high
            low_s[target, :] = low

    lane = iota((OCTANTS * rows * size, TILE), 1)

    def windows(value, block):
        main = value[:, block * TILE : (block + 1) * TILE]
        after, before = (block + 1) % blocks, (block - 1) % blocks
        rim = jnp.where(lane < HALF, value[:, after * TILE : (after + 1) * TILE], value[:, before * TILE : (before + 1) * TILE])
        return [main, rim]

    for block in range(blocks):
        one, two = windows(high_s, block), windows(low_s, block)
        left = jnp.concatenate(one + two + one, axis=1)
        right = jnp.concatenate([wide_ref[block, :PAIR], wide_ref[block, :PAIR], wide_ref[block, PAIR:]], axis=0)
        spread = product(left, right)
        part = slice(block * PAIR, (block + 1) * PAIR)
        summed = []
        for row in range(rows):
            direct = jnp.zeros((size, PAIR), F32)
            crossed = jnp.zeros((size, PAIR), F32)
            for octant in range(OCTANTS):
                start = (octant * rows + row) * size
                turn = slice(row * OCTANTS + octant, row * OCTANTS + octant + 1)
                direct += spread[start : start + size] * cos_ref[turn, part]
                crossed += spread[start : start + size] * sin_ref[turn, part]
            summed.append(direct + jnp.concatenate([-crossed[groups:], crossed[:groups]], axis=0))
        for first in range(0, rows, 2):
            target = slice(first // 2 * size, (first // 2 + 1) * size)
            for place, piece in enumerate(packed_pieces(summed[first], summed[first + 1], columns)):
                out[block * PAIR // columns + place, target, :] = piece


def packed_pieces(one, two, columns):
    found = []
    if columns == HALF:
        lane = iota((one.shape[0], TILE), 1)
        for start in range(0, one.shape[1], TILE):
            a, b = one[:, start : start + TILE], two[:, start : start + TILE]
            found.append(jnp.where(lane < HALF, a, turned(b)))
            found.append(jnp.where(lane < HALF, turned(a), b))
        return found
    for start in range(0, one.shape[1], columns):
        found.append(jnp.concatenate([one[:, start : start + columns], two[:, start : start + columns]], axis=1))
    return found


def unpacked_pieces(blocks, columns):
    if columns == HALF:
        one, two = [], []
        for a, b in zip(blocks[::2], blocks[1::2]):
            lane = iota(a.shape, 1)
            one.append(jnp.where(lane < HALF, a, turned(b)))
            two.append(jnp.where(lane < HALF, turned(a), b))
        return [jnp.concatenate(one, axis=1), jnp.concatenate(two, axis=1)]
    return [
        jnp.concatenate([block[:, :columns] for block in blocks], axis=1),
        jnp.concatenate([block[:, columns:] for block in blocks], axis=1),
    ]


def tables_kernel(sources, rows, *refs):
    count = 3
    remote, phases = refs[:count], refs[count : count + sources - 1]
    outs = refs[count + sources : -count - 1]
    local, sems = refs[-count - 1 : -1], refs[-1]
    listed_ref, vector_ref, table_ref = local
    hot_ref, chosen_ref, table_out, *turned_refs = outs
    copies = started(remote, local, sems)
    for place, phase in enumerate(phases):
        turned_refs[2 * place][...], turned_refs[2 * place + 1][...] = turns(phase[...])

    copies[2].wait()
    raw = table_ref[...]
    many, width = raw.shape
    vectors = many // (2 * rows)
    at, place = iota((many, many), 1), iota((many, many), 0)
    order = one_hot(at == place % vectors * (2 * rows) + place // (2 * vectors) * 2 + place // vectors % 2)
    twice = one_hot(iota((width, 2 * width), 1) % width == iota((width, 2 * width), 0))
    lane = iota((vectors, 2 * width), 1)
    for piece, part in enumerate(split_three(raw)):
        double = product(product(order, part).astype(BF16), twice)
        target = slice(piece * vectors, (piece + 1) * vectors)
        for kind in range(2):
            for first in range(0, rows, 2):
                one, two = (double[(2 * row + kind) * vectors : (2 * row + kind + 1) * vectors] for row in (first, first + 1))
                start = (kind * rows + first) * width
                table_out[target, start : start + 2 * width] = jnp.where(lane < width, one, two).astype(BF16)

    copies[0].wait()
    copies[1].wait()
    partners, clusters = listed_ref.shape
    unit = one_hot(iota((clusters, clusters), 0) == iota((clusters, clusters), 1))
    listed = sum(product(unit, half, 1, 1) for half in split_two(listed_ref[...].astype(F32)))
    chosen = sum(product(unit, half, 1, 1) for half in split_two(vector_ref[...].astype(F32)))
    cluster = (iota((clusters, 2 * clusters), 1) % clusters).astype(F32)
    vector = (iota((clusters, 3 * vectors), 1) % vectors).astype(F32)
    for partner in range(partners):
        part = slice(partner * clusters, (partner + 1) * clusters)
        hot_ref[part, :] = one_hot(cluster == listed[:, partner : partner + 1])
        chosen_ref[part, :] = one_hot(vector == chosen[:, partner : partner + 1])


def translate_kernel(groups, hot_ref, chosen_ref, table_ref, arrived_ref, out):
    devices, tall, width = arrived_ref.shape
    clusters = devices * groups
    partners = chosen_ref.shape[0] // clusters
    size = 2 * groups
    steps = tall // size
    starts = [step * size + part * groups for part in range(2) for step in range(steps)]
    source = jnp.concatenate(
        [arrived_ref[:, start : start + groups, :].reshape(clusters, width) for start in starts], axis=1
    )
    gathered = product(hot_ref[...], jnp.concatenate(split_two(source), axis=0))
    factors = product(chosen_ref[...], table_ref[...])
    for step in range(steps):
        lanes = slice(step * width, (step + 1) * width)
        other = slice((steps + step) * width, (steps + step + 1) * width)
        real = jnp.zeros((clusters, width), F32)
        imag = jnp.zeros((clusters, width), F32)
        for partner in range(partners):
            part = slice(partner * clusters, (partner + 1) * clusters)
            a, b = gathered[part, lanes], gathered[part, other]
            real += a * factors[part, lanes] - b * factors[part, other]
            imag += a * factors[part, other] + b * factors[part, lanes]
        for device in range(devices):
            rows = slice(device * groups, (device + 1) * groups)
            out[device, step * size : (step + 1) * size, :] = jnp.concatenate([real[rows], imag[rows]], axis=0)


def unpacked_fields(arrived_ref, size, columns):
    fields = []
    for start in range(0, arrived_ref.shape[1], size):
        fields += unpacked_pieces([arrived_ref[device, start : start + size, :] for device in range(arrived_ref.shape[0])], columns)
    return fields


def coarse_columns(fields, cos_ref, sin_ref, wide_ref, polar_ref, first, own):
    blocks = wide_ref.shape[0]
    rows, size = len(fields), fields[0].shape[0]
    groups = size // 2
    wide = polar_ref.shape[0] // rows
    crossed = [jnp.concatenate([field[groups:], -field[:groups]], axis=0) for field in fields]
    mains, rims = [], []
    for block in range(blocks):
        part = slice(block * PAIR, (block + 1) * PAIR)
        kept = []
        for octant in range(OCTANTS):
            lowered = []
            for row in range(rows):
                turn = slice(row * OCTANTS + octant, row * OCTANTS + octant + 1)
                lowered.append(fields[row][:, part] * cos_ref[turn, part] + crossed[row][:, part] * sin_ref[turn, part])
            for place in range(first, first + own):
                total = lowered[0] * polar_splat(polar_ref, place, PAIR)
                for row in range(1, rows):
                    total += lowered[row] * polar_splat(polar_ref, row * wide + place, PAIR)
                kept.append(total)
        high, low = split_two(jnp.concatenate(kept, axis=0))
        left = jnp.concatenate([high, low, high], axis=1)
        right = jnp.concatenate([wide_ref[block, :PAIR], wide_ref[block, :PAIR], wide_ref[block, PAIR:]], axis=1)
        both = product(left, right, 1, 1)
        mains.append(both[:, :TILE])
        rims.append(both[:, TILE:])
    lane = iota((OCTANTS * own * size, TILE), 1)
    return jnp.concatenate(
        [
            mains[block] + jnp.where(lane < HALF, rims[(block - 1) % blocks], rims[(block + 1) % blocks])
            for block in range(blocks)
        ],
        axis=1,
    )


def lower_kernel(groups, own, arrived_ref, cos_ref, sin_ref, wide_ref, polar_ref, parent_out, partial_ref, parent_ref, sem):
    devices = arrived_ref.shape[0]
    azimuth = cos_ref.shape[1]
    size = 2 * groups
    fields = unpacked_fields(arrived_ref, size, azimuth // devices)
    rows = len(fields)
    tiles = azimuth // TILE
    for row, field in enumerate(fields):
        for tile in range(tiles):
            for part in range(2):
                start = (row * tiles + tile) * 2 + part
                parent_ref[pl.ds(start, groups, stride=rows * tiles * 2), :] = field[
                    part * groups : (part + 1) * groups, tile * TILE : (tile + 1) * TILE
                ]
    copy = pltpu.make_async_copy(parent_ref, parent_out, sem)
    copy.start()
    partial_ref[...] = coarse_columns(fields, cos_ref, sin_ref, wide_ref, polar_ref, 0, own)
    copy.wait()


def finish_kernel(groups, sources, own, *refs):
    arrived = refs[: sources - 1]
    turned_refs = refs[sources - 1 : 3 * (sources - 1)]
    wide_ref, polar_ref, partial_ref, out = refs[3 * (sources - 1) :]
    blocks = wide_ref.shape[0]
    azimuth = turned_refs[0].shape[1]
    size = 2 * groups
    total = partial_ref[...]
    for place, field in enumerate(arrived):
        fields = unpacked_fields(field, size, azimuth // field.shape[0])
        turn_refs = turned_refs[2 * place : 2 * place + 2]
        total += coarse_columns(fields, *turn_refs, wide_ref, polar_ref, (place + 1) * own, own)
    row_stride = 2 * blocks
    for octant in range(OCTANTS):
        for row in range(own):
            value = total[(octant * own + row) * size : (octant * own + row + 1) * size]
            for block in range(blocks):
                for part in range(2):
                    first = (octant * own + row) * row_stride + 2 * block + part
                    out[pl.ds(first, groups, stride=OCTANTS * own * row_stride), :] = value[
                        part * groups : (part + 1) * groups, block * TILE : (block + 1) * TILE
                    ]


def call(kernel, outs, args, flops, name, remote=(), after=(), far=(), scratch=(), into=0):
    held = sum(4 * leaf.size for leaf in outs) + sum(4 * arg.size for arg in (*remote, *args))
    remote = [pltpu.with_memory_space_constraint(arg, pltpu.HBM) for arg in remote]
    scratch = [*scratch, *(pltpu.VMEM(arg.shape, arg.dtype) for arg in remote[: len(remote) - into])]
    if remote:
        scratch.append(pltpu.SemaphoreType.DMA((len(remote),)))
    near, away, free = (pl.BlockSpec(memory_space=space) for space in (pltpu.VMEM, pltpu.HBM, pl.ANY))
    return pl.pallas_call(
        kernel,
        out_shape=outs,
        in_specs=[away] * len(remote) + [near] * len(args) + [free] * len(after),
        out_specs=[free if place in far else near for place in range(len(outs))],
        scratch_shapes=scratch,
        compiler_params=pltpu.CompilerParams(vmem_limit_bytes=max(VMEM_BYTES, 8 * max(arg.size for arg in (*remote, *args)))),
        cost_estimate=pl.CostEstimate(flops=flops, bytes_accessed=held, transcendentals=0),
        name=name,
    )(*remote, *args, *after)


def bind(kernel, *settings):
    return lambda *refs: kernel(*settings, *refs)


def exchange(blocks):
    return lax.all_to_all(blocks, "clus", split_axis=0, concat_axis=0, tiled=True)


def per_device(child_patterns, theta_weights, phi_stencil, phi_weights, shift_phase, translation_table, far_list, far_vector):
    devices, halves = lax.axis_size("clus"), lax.axis_size("samp")
    children, _, own, columns = child_patterns.shape
    groups = children // OCTANTS
    rows, azimuth = theta_weights.shape[0], phi_stencil.shape[0]
    clusters, partners = far_list.shape
    vectors, width = translation_table.shape[0], 2 * translation_table.shape[3]
    blocks, rows_all = columns // TILE, groups * rows
    long = children * own
    sources = 2 if halves == 2 else 3
    struct = jax.ShapeDtypeStruct
    forward = [(i, (i + 1) % halves) for i in range(halves)]
    backward = [((i + 1) % halves, i) for i in range(halves)]

    field = child_patterns.reshape(children, 2, own, blocks, TILE).transpose(0, 2, 3, 1, 4).reshape(long * blocks * 2, TILE)
    neighbours = [lax.ppermute(field, "samp", forward)]
    if sources == 3:
        neighbours.append(lax.ppermute(field, "samp", backward))
    phase = shift_phase.transpose(1, 0, 2).reshape(rows * OCTANTS, azimuth)
    ways = [backward] if sources == 2 else [backward, forward]
    phases = [lax.ppermute(phase, "samp", way) for way in ways]
    table = translation_table.transpose(0, 2, 1, 3).reshape(vectors * rows * 2, width // 2)
    turn = struct((rows * OCTANTS, azimuth), F32)

    cosine, sine, wide, polar, held = call(
        bind(prepare_kernel, sources, own),
        [
            turn,
            turn,
            struct((blocks, 2 * PAIR, PAIR), BF16),
            struct((rows * sources * own, TILE), F32),
            struct(field.shape, F32),
        ],
        [],
        400_000_000,
        "prepare",
        [theta_weights, phase, phi_stencil.T, phi_weights.T, field],
        into=1,
    )
    (outgoing,) = call(
        bind(aggregate_kernel, groups, sources, own, devices),
        [struct((devices, rows_all, width), F32)],
        [held, *neighbours, cosine, sine, wide, polar],
        1_500_000_000,
        "aggregate",
        scratch=[pltpu.VMEM((2 * groups * OCTANTS * rows, columns), BF16)] * 2,
    )
    arrived = exchange(outgoing)
    hot, chosen, factors, *turned_parts = call(
        bind(tables_kernel, sources, rows),
        [
            struct((partners * clusters, 2 * clusters), BF16),
            struct((partners * clusters, 3 * vectors), BF16),
            struct((3 * vectors, rows * width), BF16),
        ]
        + [turn] * (2 * sources - 2),
        phases,
        600_000_000,
        "tables",
        [far_list.T, far_vector.T, table],
        [outgoing],
    )
    (translated,) = call(
        bind(translate_kernel, groups),
        [struct((devices, rows_all, width), F32)],
        [hot, chosen, factors, arrived],
        600_000_000,
        "translate",
    )
    returned = exchange(translated)
    size = rows_all * 2 * azimuth // TILE
    parent, partial = call(
        bind(lower_kernel, groups, own),
        [struct((size, TILE), F32), struct((2 * long, columns), F32)],
        [returned, cosine, sine, wide, polar],
        1_500_000_000,
        "lower",
        far=(0,),
        scratch=[pltpu.VMEM((size, TILE), F32), pltpu.SemaphoreType.DMA],
    )
    returned_parts = [lax.ppermute(returned, "samp", way) for way in ways]
    (total,) = call(
        bind(finish_kernel, groups, sources, own),
        [struct((long * blocks * 2, TILE), F32)],
        [*returned_parts, *turned_parts, wide, polar, partial],
        1_500_000_000,
        "finish",
    )
    child_incoming = total.reshape(children, own, blocks, 2, TILE).transpose(0, 3, 1, 2, 4).reshape(children, 2, own, columns)
    parent_incoming = (
        parent.reshape(groups, rows, azimuth // TILE, 2, TILE).transpose(0, 3, 1, 2, 4).reshape(groups, 2, rows, azimuth)
    )
    return (parent_incoming, child_incoming)


def solution(mesh):
    placed = (
        P("clus", None, "samp", None),
        P(),
        P(),
        P(),
        P(None, "samp", None),
        P(None, None, "samp", "clus"),
        P(),
        P(),
    )
    return jax.shard_map(
        per_device,
        mesh=mesh,
        in_specs=placed,
        out_specs=(P("clus", None, "samp", None), P("clus", None, "samp", None)),
        check_vma=False,
    )
```

```python
import jax
import jax.numpy as jnp
from jax import lax
from jax.experimental import pallas as pl
from jax.experimental.pallas import tpu as pltpu
from jax.sharding import PartitionSpec as P

P_SIZE = 6
OCTANTS = 8
TILE = 128
PAIR = 2 * TILE
HALF = TILE // 2
VMEM_BYTES = 8 * 1024 * 1024
F32 = jnp.float32
BF16 = jnp.bfloat16

SIN_TERMS = (-1 / 6, 1 / 120, -1 / 5040, 1 / 362880, -1 / 39916800, 1 / 6227020800)
COS_TERMS = (-1 / 2, 1 / 24, -1 / 720, 1 / 40320, -1 / 3628800, 1 / 479001600, -1 / 87178291200)


def split_two(value):
    high = value.astype(BF16)
    return high, (value - high.astype(F32)).astype(BF16)


def split_three(value):
    high = value.astype(BF16)
    rest = value - high.astype(F32)
    middle = rest.astype(BF16)
    return high, middle, (rest - middle.astype(F32)).astype(BF16)


def product(left, right, left_dim=1, right_dim=0):
    return lax.dot_general(left, right, (((left_dim,), (right_dim,)), ((), ())), preferred_element_type=F32)


def series(square, terms):
    total = jnp.full_like(square, terms[-1])
    for term in terms[-2::-1]:
        total = total * square + term
    return total


def iota(shape, dim):
    return lax.broadcasted_iota(jnp.int32, shape, dim)


def one_hot(flags):
    return flags.astype(F32).astype(BF16)


def turned(block):
    return jnp.roll(block, HALF, axis=1)


def folded(theta, sources, own):
    below, middle, above = theta[:, :own], theta[:, own : 2 * own], theta[:, 2 * own :]
    return jnp.concatenate((middle, below + above) if sources == 2 else (middle, below, above), axis=1)


def turns(phase):
    half = 0.5 * phase
    square = half * half
    sine = half + half * square * series(square, SIN_TERMS)
    cosine = 1.0 + square * series(square, COS_TERMS)
    return 1.0 - 2.0 * sine * sine, 2.0 * sine * cosine


def started(remote, local, sems):
    copies = [pltpu.make_async_copy(source, target, sems.at[place]) for place, (source, target) in enumerate(zip(remote, local))]
    for copy in copies:
        copy.start()
    return copies


def prepare_kernel(sources, own, *refs):
    count = 5
    remote, outs, rest = refs[:count], refs[count : count + 5], refs[count + 5 :]
    cos_ref, sin_ref, wide_ref, polar_ref, field_out = outs
    theta_ref, phase_ref, stencil_ref, weight_ref, sems = rest
    copies = started(remote, [theta_ref, phase_ref, stencil_ref, weight_ref, field_out], sems)
    rows = theta_ref.shape[0]
    blocks = wide_ref.shape[0]

    wide = sources * own
    at_row = one_hot(iota((rows * wide, rows), 0) // wide == iota((rows * wide, rows), 1))
    keep = iota((rows * wide, wide), 0) % wide == iota((rows * wide, wide), 1)
    ones = jnp.ones((wide, TILE), BF16)
    copies[0].wait()
    parts = [
        product(jnp.where(keep, product(at_row, part), 0.0).astype(BF16), ones)
        for part in split_three(folded(theta_ref[...], sources, own))
    ]
    polar_ref[...] = parts[0] + (parts[1] + parts[2])

    copies[1].wait()
    cos_ref[...], sin_ref[...] = turns(phase_ref[...])

    copies[2].wait()
    copies[3].wait()
    for block in range(blocks):
        columns = slice(block * PAIR, (block + 1) * PAIR)
        after, before = (block + 1) % blocks, (block - 1) % blocks
        pieces = (
            (0, TILE, block * TILE),
            (TILE, 16, after * TILE),
            (PAIR - 16, 16, before * TILE + TILE - 16),
        )
        for start, size, first in pieces:
            child = iota((size, PAIR), 0) + first
            total = jnp.zeros((size, PAIR), F32)
            for point in range(P_SIZE):
                hit = stencil_ref[point : point + 1, columns] == child
                total = jnp.where(hit, weight_ref[point : point + 1, columns], total)
            high, low = split_two(total)
            wide_ref[block, start : start + size, :] = high
            wide_ref[block, PAIR + start : PAIR + start + size, :] = low
        empty = jnp.zeros((TILE - 32, PAIR), BF16)
        wide_ref[block, TILE + 16 : PAIR - 16, :] = empty
        wide_ref[block, PAIR + TILE + 16 : 2 * PAIR - 16, :] = empty
    copies[4].wait()


def polar_splat(polar_ref, row, width):
    return jnp.concatenate([polar_ref[row : row + 1, :]] * (width // TILE), axis=1)


def aggregate_kernel(groups, sources, own, devices, *refs):
    fields = refs[:sources]
    cos_ref, sin_ref, wide_ref, polar_ref = refs[sources : sources + 4]
    out, high_s, low_s = refs[-3:]
    blocks = wide_ref.shape[0]
    rows = cos_ref.shape[0] // OCTANTS
    columns = cos_ref.shape[1] // devices
    size = 2 * groups
    wide = sources * own
    row_stride = 2 * blocks
    child_stride = OCTANTS * own * row_stride

    for octant in range(OCTANTS):
        given = []
        for field in fields:
            for row in range(own):
                start = (octant * own + row) * row_stride
                given.append(
                    jnp.concatenate(
                        [
                            jnp.concatenate(
                                [field[pl.ds(start + 2 * block + part, groups, stride=child_stride), :] for part in range(2)],
                                axis=0,
                            )
                            for block in range(blocks)
                        ],
                        axis=1,
                    )
                )
        for first in range(0, rows, 2):
            pair = []
            for row in (first, first + 1):
                total = given[0] * polar_splat(polar_ref, row * wide, blocks * TILE)
                for place in range(1, wide):
                    total += given[place] * polar_splat(polar_ref, row * wide + place, blocks * TILE)
                pair.append(total)
            high, low = split_two(jnp.concatenate(pair, axis=0))
            target = slice((octant * rows + first) * size, (octant * rows + first + 2) * size)
            high_s[target, :] = high
            low_s[target, :] = low

    lane = iota((OCTANTS * rows * size, TILE), 1)

    def windows(value, block):
        main = value[:, block * TILE : (block + 1) * TILE]
        after, before = (block + 1) % blocks, (block - 1) % blocks
        rim = jnp.where(lane < HALF, value[:, after * TILE : (after + 1) * TILE], value[:, before * TILE : (before + 1) * TILE])
        return [main, rim]

    for block in range(blocks):
        one, two = windows(high_s, block), windows(low_s, block)
        left = jnp.concatenate(one + two + one, axis=1)
        right = jnp.concatenate([wide_ref[block, :PAIR], wide_ref[block, :PAIR], wide_ref[block, PAIR:]], axis=0)
        spread = product(left, right)
        part = slice(block * PAIR, (block + 1) * PAIR)
        summed = []
        for row in range(rows):
            direct = jnp.zeros((size, PAIR), F32)
            crossed = jnp.zeros((size, PAIR), F32)
            for octant in range(OCTANTS):
                start = (octant * rows + row) * size
                turn = slice(row * OCTANTS + octant, row * OCTANTS + octant + 1)
                direct += spread[start : start + size] * cos_ref[turn, part]
                crossed += spread[start : start + size] * sin_ref[turn, part]
            summed.append(direct + jnp.concatenate([-crossed[groups:], crossed[:groups]], axis=0))
        for first in range(0, rows, 2):
            target = slice(first // 2 * size, (first // 2 + 1) * size)
            for place, piece in enumerate(packed_pieces(summed[first], summed[first + 1], columns)):
                out[block * PAIR // columns + place, target, :] = piece


def packed_pieces(one, two, columns):
    found = []
    if columns == HALF:
        lane = iota((one.shape[0], TILE), 1)
        for start in range(0, one.shape[1], TILE):
            a, b = one[:, start : start + TILE], two[:, start : start + TILE]
            found.append(jnp.where(lane < HALF, a, turned(b)))
            found.append(jnp.where(lane < HALF, turned(a), b))
        return found
    for start in range(0, one.shape[1], columns):
        found.append(jnp.concatenate([one[:, start : start + columns], two[:, start : start + columns]], axis=1))
    return found


def unpacked_pieces(blocks, columns):
    if columns == HALF:
        one, two = [], []
        for a, b in zip(blocks[::2], blocks[1::2]):
            lane = iota(a.shape, 1)
            one.append(jnp.where(lane < HALF, a, turned(b)))
            two.append(jnp.where(lane < HALF, turned(a), b))
        return [jnp.concatenate(one, axis=1), jnp.concatenate(two, axis=1)]
    return [
        jnp.concatenate([block[:, :columns] for block in blocks], axis=1),
        jnp.concatenate([block[:, columns:] for block in blocks], axis=1),
    ]


def tables_kernel(devices, sources, rows, *refs):
    count = 3
    remote, phases = refs[:count], refs[count : count + sources - 1]
    outs = refs[count + sources : -count - 1]
    local, sems = refs[-count - 1 : -1], refs[-1]
    listed_ref, vector_ref, table_ref = local
    hot_ref, chosen_ref, table_out, *turned_refs = outs
    copies = started(remote, local, sems)
    for place, phase in enumerate(phases):
        turned_refs[2 * place][...], turned_refs[2 * place + 1][...] = turns(phase[...])

    copies[2].wait()
    raw = table_ref[...]
    many, width = raw.shape
    vectors = many // (2 * rows)
    at, place = iota((many, many), 1), iota((many, many), 0)
    order = one_hot(at == place % vectors * (2 * rows) + place // (2 * vectors) * 2 + place // vectors % 2)
    twice = one_hot(iota((width, 2 * width), 1) % width == iota((width, 2 * width), 0))
    lane = iota((vectors, 2 * width), 1)
    for piece, part in enumerate(split_three(raw)):
        double = product(product(order, part).astype(BF16), twice)
        target = slice(piece * vectors, (piece + 1) * vectors)
        for kind in range(2):
            for first in range(0, rows, 2):
                one, two = (double[(2 * row + kind) * vectors : (2 * row + kind + 1) * vectors] for row in (first, first + 1))
                start = (kind * rows + first) * width
                table_out[target, start : start + 2 * width] = jnp.where(lane < width, one, two).astype(BF16)

    copies[0].wait()
    copies[1].wait()
    partners, clusters = listed_ref.shape
    unit = one_hot(iota((clusters, clusters), 0) == iota((clusters, clusters), 1))
    groups = clusters // devices
    listed = place_of(listed_ref[...] // groups, devices) * groups + listed_ref[...] % groups
    listed = sum(product(unit, half, 1, 1) for half in split_two(listed.astype(F32)))
    chosen = sum(product(unit, half, 1, 1) for half in split_two(vector_ref[...].astype(F32)))
    cluster = (iota((clusters, 2 * clusters), 1) % clusters).astype(F32)
    vector = (iota((clusters, 3 * vectors), 1) % vectors).astype(F32)
    for partner in range(partners):
        part = slice(partner * clusters, (partner + 1) * clusters)
        hot_ref[part, :] = one_hot(cluster == listed[:, partner : partner + 1])
        chosen_ref[part, :] = one_hot(vector == chosen[:, partner : partner + 1])


def translate_kernel(groups, hot_ref, chosen_ref, table_ref, arrived_ref, out):
    devices, tall, width = arrived_ref.shape
    clusters = devices * groups
    partners = chosen_ref.shape[0] // clusters
    size = 2 * groups
    steps = tall // size
    starts = [step * size + part * groups for part in range(2) for step in range(steps)]
    source = jnp.concatenate(
        [arrived_ref[:, start : start + groups, :].reshape(clusters, width) for start in starts], axis=1
    )
    gathered = product(hot_ref[...], jnp.concatenate(split_two(source), axis=0))
    factors = product(chosen_ref[...], table_ref[...])
    for step in range(steps):
        lanes = slice(step * width, (step + 1) * width)
        other = slice((steps + step) * width, (steps + step + 1) * width)
        real = jnp.zeros((clusters, width), F32)
        imag = jnp.zeros((clusters, width), F32)
        for partner in range(partners):
            part = slice(partner * clusters, (partner + 1) * clusters)
            a, b = gathered[part, lanes], gathered[part, other]
            real += a * factors[part, lanes] - b * factors[part, other]
            imag += a * factors[part, other] + b * factors[part, lanes]
        for device in range(devices):
            rows = slice(device * groups, (device + 1) * groups)
            out[device, step * size : (step + 1) * size, :] = jnp.concatenate([real[rows], imag[rows]], axis=0)


def unpacked_fields(arrived_ref, size, columns):
    fields = []
    for start in range(0, arrived_ref.shape[1], size):
        devices = arrived_ref.shape[0]
        blocks = [arrived_ref[place_of(device, devices), start : start + size, :] for device in range(devices)]
        fields += unpacked_pieces(blocks, columns)
    return fields


def coarse_columns(fields, cos_ref, sin_ref, wide_ref):
    blocks = wide_ref.shape[0]
    rows, size = len(fields), fields[0].shape[0]
    groups = size // 2
    crossed = [jnp.concatenate([field[groups:], -field[:groups]], axis=0) for field in fields]
    mains, rims = [], []
    for block in range(blocks):
        part = slice(block * PAIR, (block + 1) * PAIR)
        lowered = []
        for octant in range(OCTANTS):
            for row in range(rows):
                turn = slice(row * OCTANTS + octant, row * OCTANTS + octant + 1)
                lowered.append(fields[row][:, part] * cos_ref[turn, part] + crossed[row][:, part] * sin_ref[turn, part])
        high, low = split_two(jnp.concatenate(lowered, axis=0))
        left = jnp.concatenate([high, low, high], axis=1)
        right = jnp.concatenate([wide_ref[block, :PAIR], wide_ref[block, :PAIR], wide_ref[block, PAIR:]], axis=1)
        both = product(left, right, 1, 1)
        mains.append(both[:, :TILE])
        rims.append(both[:, TILE:])
    lane = iota((OCTANTS * rows * size, TILE), 1)
    return jnp.concatenate(
        [
            mains[block] + jnp.where(lane < HALF, rims[(block - 1) % blocks], rims[(block + 1) % blocks])
            for block in range(blocks)
        ],
        axis=1,
    )


def anterpolated(coarse, polar_ref, octant, place, rows, size, wide):
    total = None
    for row in range(rows):
        start = (octant * rows + row) * size
        term = coarse[start : start + size] * polar_splat(polar_ref, row * wide + place, coarse.shape[1])
        total = term if total is None else total + term
    return total


def lower_kernel(groups, own, arrived_ref, cos_ref, sin_ref, wide_ref, polar_ref, parent_out, partial_ref, parent_ref, sem):
    devices = arrived_ref.shape[0]
    azimuth = cos_ref.shape[1]
    size = 2 * groups
    fields = unpacked_fields(arrived_ref, size, azimuth // devices)
    rows = len(fields)
    wide = polar_ref.shape[0] // rows
    tiles = azimuth // TILE
    for row, field in enumerate(fields):
        for tile in range(tiles):
            for part in range(2):
                start = (row * tiles + tile) * 2 + part
                parent_ref[pl.ds(start, groups, stride=rows * tiles * 2), :] = field[
                    part * groups : (part + 1) * groups, tile * TILE : (tile + 1) * TILE
                ]
    copy = pltpu.make_async_copy(parent_ref, parent_out, sem)
    copy.start()
    coarse = coarse_columns(fields, cos_ref, sin_ref, wide_ref)
    for octant in range(OCTANTS):
        for row in range(own):
            start = (octant * own + row) * size
            partial_ref[start : start + size, :] = anterpolated(coarse, polar_ref, octant, row, rows, size, wide)
    copy.wait()


def finish_kernel(groups, sources, own, *refs):
    arrived = refs[: sources - 1]
    turned_refs = refs[sources - 1 : 3 * (sources - 1)]
    wide_ref, polar_ref, partial_ref, out = refs[3 * (sources - 1) :]
    blocks = wide_ref.shape[0]
    azimuth = turned_refs[0].shape[1]
    size = 2 * groups
    coarse = []
    for place, field in enumerate(arrived):
        fields = unpacked_fields(field, size, azimuth // field.shape[0])
        coarse.append(coarse_columns(fields, turned_refs[2 * place], turned_refs[2 * place + 1], wide_ref))
    rows = len(fields)
    wide = sources * own
    row_stride = 2 * blocks
    for octant in range(OCTANTS):
        for row in range(own):
            start = (octant * own + row) * size
            value = partial_ref[start : start + size, :]
            for place in range(sources - 1):
                value += anterpolated(coarse[place], polar_ref, octant, (place + 1) * own + row, rows, size, wide)
            for block in range(blocks):
                for part in range(2):
                    first = (octant * own + row) * row_stride + 2 * block + part
                    out[pl.ds(first, groups, stride=OCTANTS * own * row_stride), :] = value[
                        part * groups : (part + 1) * groups, block * TILE : (block + 1) * TILE
                    ]


def call(kernel, outs, args, flops, name, remote=(), after=(), far=(), scratch=(), into=0):
    held = sum(4 * leaf.size for leaf in outs) + sum(4 * arg.size for arg in (*remote, *args))
    remote = [pltpu.with_memory_space_constraint(arg, pltpu.HBM) for arg in remote]
    scratch = [*scratch, *(pltpu.VMEM(arg.shape, arg.dtype) for arg in remote[: len(remote) - into])]
    if remote:
        scratch.append(pltpu.SemaphoreType.DMA((len(remote),)))
    near, away, free = (pl.BlockSpec(memory_space=space) for space in (pltpu.VMEM, pltpu.HBM, pl.ANY))
    return pl.pallas_call(
        kernel,
        out_shape=outs,
        in_specs=[away] * len(remote) + [near] * len(args) + [free] * len(after),
        out_specs=[free if place in far else near for place in range(len(outs))],
        scratch_shapes=scratch,
        compiler_params=pltpu.CompilerParams(vmem_limit_bytes=max(VMEM_BYTES, 8 * max(arg.size for arg in (*remote, *args)))),
        cost_estimate=pl.CostEstimate(flops=flops, bytes_accessed=held, transcendentals=0),
        name=name,
    )(*remote, *args, *after)


def bind(kernel, *settings):
    return lambda *refs: kernel(*settings, *refs)


def factors_of(devices):
    near = 1
    while near * near < devices:
        near *= 2
    return (devices // near, near) if devices % near == 0 else (1, devices)


def place_of(device, devices):
    far, near = factors_of(devices)
    return device % near * far + device // near


def exchange(blocks, devices):
    far, near = factors_of(devices)
    along_far = [[z * near + r for z in range(far)] for r in range(near)]
    along_near = [[z * near + r for r in range(near)] for z in range(far)]
    moved = lax.all_to_all(blocks, "clus", split_axis=0, concat_axis=0, tiled=True, axis_index_groups=along_far)
    moved = moved.reshape(far, near, *blocks.shape[1:]).swapaxes(0, 1).reshape(blocks.shape)
    return lax.all_to_all(moved, "clus", split_axis=0, concat_axis=0, tiled=True, axis_index_groups=along_near)


def per_device(child_patterns, theta_weights, phi_stencil, phi_weights, shift_phase, translation_table, far_list, far_vector):
    devices, halves = lax.axis_size("clus"), lax.axis_size("samp")
    children, _, own, columns = child_patterns.shape
    groups = children // OCTANTS
    rows, azimuth = theta_weights.shape[0], phi_stencil.shape[0]
    clusters, partners = far_list.shape
    vectors, width = translation_table.shape[0], 2 * translation_table.shape[3]
    blocks, rows_all = columns // TILE, groups * rows
    long = children * own
    sources = 2 if halves == 2 else 3
    struct = jax.ShapeDtypeStruct
    forward = [(i, (i + 1) % halves) for i in range(halves)]
    backward = [((i + 1) % halves, i) for i in range(halves)]

    field = child_patterns.reshape(children, 2, own, blocks, TILE).transpose(0, 2, 3, 1, 4).reshape(long * blocks * 2, TILE)
    neighbours = [lax.ppermute(field, "samp", forward)]
    if sources == 3:
        neighbours.append(lax.ppermute(field, "samp", backward))
    phase = shift_phase.transpose(1, 0, 2).reshape(rows * OCTANTS, azimuth)
    ways = [backward] if sources == 2 else [backward, forward]
    phases = [lax.ppermute(phase, "samp", way) for way in ways]
    table = translation_table.transpose(0, 2, 1, 3).reshape(vectors * rows * 2, width // 2)
    turn = struct((rows * OCTANTS, azimuth), F32)

    cosine, sine, wide, polar, held = call(
        bind(prepare_kernel, sources, own),
        [
            turn,
            turn,
            struct((blocks, 2 * PAIR, PAIR), BF16),
            struct((rows * sources * own, TILE), F32),
            struct(field.shape, F32),
        ],
        [],
        400_000_000,
        "prepare",
        [theta_weights, phase, phi_stencil.T, phi_weights.T, field],
        into=1,
    )
    (outgoing,) = call(
        bind(aggregate_kernel, groups, sources, own, devices),
        [struct((devices, rows_all, width), F32)],
        [held, *neighbours, cosine, sine, wide, polar],
        1_500_000_000,
        "aggregate",
        scratch=[pltpu.VMEM((2 * groups * OCTANTS * rows, columns), BF16)] * 2,
    )
    arrived = exchange(outgoing, devices)
    hot, chosen, factors, *turned_parts = call(
        bind(tables_kernel, devices, sources, rows),
        [
            struct((partners * clusters, 2 * clusters), BF16),
            struct((partners * clusters, 3 * vectors), BF16),
            struct((3 * vectors, rows * width), BF16),
        ]
        + [turn] * (2 * sources - 2),
        phases,
        600_000_000,
        "tables",
        [far_list.T, far_vector.T, table],
        [outgoing],
    )
    (translated,) = call(
        bind(translate_kernel, groups),
        [struct((devices, rows_all, width), F32)],
        [hot, chosen, factors, arrived],
        600_000_000,
        "translate",
    )
    returned = exchange(translated, devices)
    size = rows_all * 2 * azimuth // TILE
    parent, partial = call(
        bind(lower_kernel, groups, own),
        [struct((size, TILE), F32), struct((2 * long, columns), F32)],
        [returned, cosine, sine, wide, polar],
        1_500_000_000,
        "lower",
        far=(0,),
        scratch=[pltpu.VMEM((size, TILE), F32), pltpu.SemaphoreType.DMA],
    )
    returned_parts = [lax.ppermute(returned, "samp", way) for way in ways]
    (total,) = call(
        bind(finish_kernel, groups, sources, own),
        [struct((long * blocks * 2, TILE), F32)],
        [*returned_parts, *turned_parts, wide, polar, partial],
        1_500_000_000,
        "finish",
    )
    child_incoming = total.reshape(children, own, blocks, 2, TILE).transpose(0, 3, 1, 2, 4).reshape(children, 2, own, columns)
    parent_incoming = (
        parent.reshape(groups, rows, azimuth // TILE, 2, TILE).transpose(0, 3, 1, 2, 4).reshape(groups, 2, rows, azimuth)
    )
    return (parent_incoming, child_incoming)


def solution(mesh):
    placed = (
        P("clus", None, "samp", None),
        P(),
        P(),
        P(),
        P(None, "samp", None),
        P(None, None, "samp", "clus"),
        P(),
        P(),
    )
    return jax.shard_map(
        per_device,
        mesh=mesh,
        in_specs=placed,
        out_specs=(P("clus", None, "samp", None), P("clus", None, "samp", None)),
        check_vma=False,
    )
```

```python
import jax
import jax.numpy as jnp
from jax import lax
from jax.experimental import pallas as pl
from jax.experimental.pallas import tpu as pltpu
from jax.sharding import PartitionSpec as P

P_SIZE = 6
OCTANTS = 8
TILE = 128
PAIR = 2 * TILE
HALF = TILE // 2
VMEM_BYTES = 8 * 1024 * 1024
F32 = jnp.float32
BF16 = jnp.bfloat16

RIM = 16
KEPT = TILE + 2 * RIM

SIN_TERMS = (-1 / 6, 1 / 120, -1 / 5040, 1 / 362880, -1 / 39916800, 1 / 6227020800)
COS_TERMS = (-1 / 2, 1 / 24, -1 / 720, 1 / 40320, -1 / 3628800, 1 / 479001600, -1 / 87178291200)


def split_two(value):
    high = value.astype(BF16)
    return high, (value - high.astype(F32)).astype(BF16)


def split_three(value):
    high = value.astype(BF16)
    rest = value - high.astype(F32)
    middle = rest.astype(BF16)
    return high, middle, (rest - middle.astype(F32)).astype(BF16)


def product(left, right, left_dim=1, right_dim=0):
    return lax.dot_general(left, right, (((left_dim,), (right_dim,)), ((), ())), preferred_element_type=F32)


def series(square, terms):
    total = jnp.full_like(square, terms[-1])
    for term in terms[-2::-1]:
        total = total * square + term
    return total


def iota(shape, dim):
    return lax.broadcasted_iota(jnp.int32, shape, dim)


def one_hot(flags):
    return flags.astype(F32).astype(BF16)


def turned(block):
    return jnp.roll(block, HALF, axis=1)


def folded(theta, sources, own):
    below, middle, above = theta[:, :own], theta[:, own : 2 * own], theta[:, 2 * own :]
    return jnp.concatenate((middle, below + above) if sources == 2 else (middle, below, above), axis=1)


def turns(phase):
    half = 0.5 * phase
    square = half * half
    sine = half + half * square * series(square, SIN_TERMS)
    cosine = 1.0 + square * series(square, COS_TERMS)
    return 1.0 - 2.0 * sine * sine, 2.0 * sine * cosine


def started(remote, local, sems):
    copies = [pltpu.make_async_copy(source, target, sems.at[place]) for place, (source, target) in enumerate(zip(remote, local))]
    for copy in copies:
        copy.start()
    return copies


def prepare_kernel(sources, own, *refs):
    count = 5
    remote, outs, rest = refs[:count], refs[count : count + 5], refs[count + 5 :]
    cos_ref, sin_ref, wide_ref, polar_ref, field_out = outs
    theta_ref, phase_ref, stencil_ref, weight_ref, sems = rest
    copies = started(remote, [theta_ref, phase_ref, stencil_ref, weight_ref, field_out], sems)
    rows = theta_ref.shape[0]
    blocks = wide_ref.shape[0]

    wide = sources * own
    at_row = one_hot(iota((rows * wide, rows), 0) // wide == iota((rows * wide, rows), 1))
    keep = iota((rows * wide, wide), 0) % wide == iota((rows * wide, wide), 1)
    ones = jnp.ones((wide, TILE), BF16)
    copies[0].wait()
    parts = [
        product(jnp.where(keep, product(at_row, part), 0.0).astype(BF16), ones)
        for part in split_three(folded(theta_ref[...], sources, own))
    ]
    polar_ref[...] = parts[0] + (parts[1] + parts[2])

    copies[1].wait()
    cos_ref[...], sin_ref[...] = turns(phase_ref[...])

    copies[2].wait()
    copies[3].wait()
    for block in range(blocks):
        columns = slice(block * PAIR, (block + 1) * PAIR)
        after, before = (block + 1) % blocks, (block - 1) % blocks
        pieces = (
            (0, TILE, block * TILE),
            (TILE, RIM, after * TILE),
            (TILE + RIM, RIM, before * TILE + TILE - RIM),
        )
        for start, size, first in pieces:
            child = iota((size, PAIR), 0) + first
            total = jnp.zeros((size, PAIR), F32)
            for point in range(P_SIZE):
                hit = stencil_ref[point : point + 1, columns] == child
                total = jnp.where(hit, weight_ref[point : point + 1, columns], total)
            high, low = split_two(total)
            wide_ref[block, start : start + size, :] = high
            wide_ref[block, KEPT + start : KEPT + start + size, :] = low
    copies[4].wait()


def azimuthal(wide_ref, block, axis):
    empty = jnp.zeros((TILE - 2 * RIM, PAIR), BF16)
    halves = []
    for start in (0, KEPT):
        kept = (wide_ref[block, start : start + TILE + RIM], empty, wide_ref[block, start + TILE + RIM : start + KEPT])
        halves.append(jnp.concatenate(kept, axis=0))
    return jnp.concatenate([halves[0], halves[0], halves[1]], axis=axis)


def polar_splat(polar_ref, row, width):
    return jnp.concatenate([polar_ref[row : row + 1, :]] * (width // TILE), axis=1)


def aggregate_kernel(groups, sources, own, devices, *refs):
    fields = refs[:sources]
    cos_ref, sin_ref, wide_ref, polar_ref = refs[sources : sources + 4]
    out, high_s, low_s = refs[-3:]
    blocks = wide_ref.shape[0]
    rows = cos_ref.shape[0] // OCTANTS
    columns = cos_ref.shape[1] // devices
    size = 2 * groups
    wide = sources * own
    row_stride = 2 * blocks
    child_stride = OCTANTS * own * row_stride

    for octant in range(OCTANTS):
        given = []
        for field in fields:
            for row in range(own):
                start = (octant * own + row) * row_stride
                given.append(
                    jnp.concatenate(
                        [
                            jnp.concatenate(
                                [field[pl.ds(start + 2 * block + part, groups, stride=child_stride), :] for part in range(2)],
                                axis=0,
                            )
                            for block in range(blocks)
                        ],
                        axis=1,
                    )
                )
        for first in range(0, rows, 2):
            pair = []
            for row in (first, first + 1):
                total = given[0] * polar_splat(polar_ref, row * wide, blocks * TILE)
                for place in range(1, wide):
                    total += given[place] * polar_splat(polar_ref, row * wide + place, blocks * TILE)
                pair.append(total)
            high, low = split_two(jnp.concatenate(pair, axis=0))
            target = slice((octant * rows + first) * size, (octant * rows + first + 2) * size)
            high_s[target, :] = high
            low_s[target, :] = low

    lane = iota((OCTANTS * rows * size, TILE), 1)

    def windows(value, block):
        main = value[:, block * TILE : (block + 1) * TILE]
        after, before = (block + 1) % blocks, (block - 1) % blocks
        rim = jnp.where(lane < HALF, value[:, after * TILE : (after + 1) * TILE], value[:, before * TILE : (before + 1) * TILE])
        return [main, rim]

    for block in range(blocks):
        one, two = windows(high_s, block), windows(low_s, block)
        left = jnp.concatenate(one + two + one, axis=1)
        spread = product(left, azimuthal(wide_ref, block, 0))
        part = slice(block * PAIR, (block + 1) * PAIR)
        summed = []
        for row in range(rows):
            direct = jnp.zeros((size, PAIR), F32)
            crossed = jnp.zeros((size, PAIR), F32)
            for octant in range(OCTANTS):
                start = (octant * rows + row) * size
                turn = slice(row * OCTANTS + octant, row * OCTANTS + octant + 1)
                direct += spread[start : start + size] * cos_ref[turn, part]
                crossed += spread[start : start + size] * sin_ref[turn, part]
            summed.append(direct + jnp.concatenate([-crossed[groups:], crossed[:groups]], axis=0))
        for first in range(0, rows, 2):
            target = slice(first // 2 * size, (first // 2 + 1) * size)
            for place, piece in enumerate(packed_pieces(summed[first], summed[first + 1], columns)):
                out[block * PAIR // columns + place, target, :] = piece


def packed_pieces(one, two, columns):
    found = []
    if columns == HALF:
        lane = iota((one.shape[0], TILE), 1)
        for start in range(0, one.shape[1], TILE):
            a, b = one[:, start : start + TILE], two[:, start : start + TILE]
            found.append(jnp.where(lane < HALF, a, turned(b)))
            found.append(jnp.where(lane < HALF, turned(a), b))
        return found
    for start in range(0, one.shape[1], columns):
        found.append(jnp.concatenate([one[:, start : start + columns], two[:, start : start + columns]], axis=1))
    return found


def unpacked_pieces(blocks, columns):
    if columns == HALF:
        one, two = [], []
        for a, b in zip(blocks[::2], blocks[1::2]):
            lane = iota(a.shape, 1)
            one.append(jnp.where(lane < HALF, a, turned(b)))
            two.append(jnp.where(lane < HALF, turned(a), b))
        return [jnp.concatenate(one, axis=1), jnp.concatenate(two, axis=1)]
    return [
        jnp.concatenate([block[:, :columns] for block in blocks], axis=1),
        jnp.concatenate([block[:, columns:] for block in blocks], axis=1),
    ]


def tables_kernel(sources, rows, *refs):
    count = 3
    remote, phases = refs[:count], refs[count : count + sources - 1]
    outs = refs[count + sources : -count - 1]
    local, sems = refs[-count - 1 : -1], refs[-1]
    listed_ref, vector_ref, table_ref = local
    hot_ref, factors_ref, *turned_refs = outs
    copies = started(remote, local, sems)
    for place, phase in enumerate(phases):
        turned_refs[2 * place][...], turned_refs[2 * place + 1][...] = turns(phase[...])

    copies[2].wait()
    raw = table_ref[...]
    many, width = raw.shape
    vectors = many // (2 * rows)
    at, place = iota((many, many), 1), iota((many, many), 0)
    order = one_hot(at == place % vectors * (2 * rows) + place // (2 * vectors) * 2 + place // vectors % 2)
    twice = one_hot(iota((width, 2 * width), 1) % width == iota((width, 2 * width), 0))
    lane = iota((vectors, 2 * width), 1)
    pieces = []
    for part in split_three(raw):
        double = product(product(order, part).astype(BF16), twice)
        pairs = []
        for kind in range(2):
            for first in range(0, rows, 2):
                one, two = (double[(2 * row + kind) * vectors : (2 * row + kind + 1) * vectors] for row in (first, first + 1))
                pairs.append(jnp.where(lane < width, one, two).astype(BF16))
        pieces.append(jnp.concatenate(pairs, axis=1))
    spread = jnp.concatenate(pieces, axis=0)

    copies[0].wait()
    copies[1].wait()
    partners, clusters = listed_ref.shape
    unit = one_hot(iota((clusters, clusters), 0) == iota((clusters, clusters), 1))
    listed = sum(product(unit, half, 1, 1) for half in split_two(listed_ref[...].astype(F32)))
    chosen = sum(product(unit, half, 1, 1) for half in split_two(vector_ref[...].astype(F32)))
    cluster = (iota((clusters, 2 * clusters), 1) % clusters).astype(F32)
    vector = (iota((clusters, 3 * vectors), 1) % vectors).astype(F32)
    picked = []
    for partner in range(partners):
        part = slice(partner * clusters, (partner + 1) * clusters)
        hot_ref[part, :] = one_hot(cluster == listed[:, partner : partner + 1])
        picked.append(one_hot(vector == chosen[:, partner : partner + 1]))
    factors_ref[...] = product(jnp.concatenate(picked, axis=0), spread)


def translate_kernel(groups, hot_ref, factors_ref, arrived_ref, out):
    devices, tall, width = arrived_ref.shape
    clusters = devices * groups
    partners = hot_ref.shape[0] // clusters
    size = 2 * groups
    steps = tall // size
    starts = [step * size + part * groups for part in range(2) for step in range(steps)]
    source = jnp.concatenate(
        [arrived_ref[:, start : start + groups, :].reshape(clusters, width) for start in starts], axis=1
    )
    gathered = product(hot_ref[...], jnp.concatenate(split_two(source), axis=0))
    for step in range(steps):
        lanes = slice(step * width, (step + 1) * width)
        other = slice((steps + step) * width, (steps + step + 1) * width)
        real = jnp.zeros((clusters, width), F32)
        imag = jnp.zeros((clusters, width), F32)
        for partner in range(partners):
            part = slice(partner * clusters, (partner + 1) * clusters)
            a, b = gathered[part, lanes], gathered[part, other]
            c, d = factors_ref[part, lanes], factors_ref[part, other]
            real += a * c - b * d
            imag += a * d + b * c
        for device in range(devices):
            rows = slice(device * groups, (device + 1) * groups)
            out[device, step * size : (step + 1) * size, :] = jnp.concatenate([real[rows], imag[rows]], axis=0)


def unpacked_fields(arrived_ref, size, columns):
    fields = []
    for start in range(0, arrived_ref.shape[1], size):
        fields += unpacked_pieces([arrived_ref[device, start : start + size, :] for device in range(arrived_ref.shape[0])], columns)
    return fields


def coarse_columns(fields, cos_ref, sin_ref, wide_ref):
    blocks = wide_ref.shape[0]
    rows, size = len(fields), fields[0].shape[0]
    groups = size // 2
    crossed = [jnp.concatenate([field[groups:], -field[:groups]], axis=0) for field in fields]
    mains, rims = [], []
    for block in range(blocks):
        part = slice(block * PAIR, (block + 1) * PAIR)
        lowered = []
        for octant in range(OCTANTS):
            for row in range(rows):
                turn = slice(row * OCTANTS + octant, row * OCTANTS + octant + 1)
                lowered.append(fields[row][:, part] * cos_ref[turn, part] + crossed[row][:, part] * sin_ref[turn, part])
        high, low = split_two(jnp.concatenate(lowered, axis=0))
        left = jnp.concatenate([high, low, high], axis=1)
        both = product(left, azimuthal(wide_ref, block, 1), 1, 1)
        mains.append(both[:, :TILE])
        rims.append(both[:, TILE:])
    lane = iota((OCTANTS * rows * size, TILE), 1)
    return jnp.concatenate(
        [
            mains[block] + jnp.where(lane < HALF, rims[(block - 1) % blocks], rims[(block + 1) % blocks])
            for block in range(blocks)
        ],
        axis=1,
    )


def anterpolated(coarse, polar_ref, octant, place, rows, size, wide):
    total = None
    for row in range(rows):
        start = (octant * rows + row) * size
        term = coarse[start : start + size] * polar_splat(polar_ref, row * wide + place, coarse.shape[1])
        total = term if total is None else total + term
    return total


def lower_kernel(groups, own, arrived_ref, cos_ref, sin_ref, wide_ref, polar_ref, parent_out, partial_ref, parent_ref, sem):
    devices = arrived_ref.shape[0]
    azimuth = cos_ref.shape[1]
    size = 2 * groups
    fields = unpacked_fields(arrived_ref, size, azimuth // devices)
    rows = len(fields)
    wide = polar_ref.shape[0] // rows
    tiles = azimuth // TILE
    for row, field in enumerate(fields):
        for tile in range(tiles):
            for part in range(2):
                start = (row * tiles + tile) * 2 + part
                parent_ref[pl.ds(start, groups, stride=rows * tiles * 2), :] = field[
                    part * groups : (part + 1) * groups, tile * TILE : (tile + 1) * TILE
                ]
    copy = pltpu.make_async_copy(parent_ref, parent_out, sem)
    copy.start()
    coarse = coarse_columns(fields, cos_ref, sin_ref, wide_ref)
    for octant in range(OCTANTS):
        for row in range(own):
            start = (octant * own + row) * size
            partial_ref[start : start + size, :] = anterpolated(coarse, polar_ref, octant, row, rows, size, wide)
    copy.wait()


def finish_kernel(groups, sources, own, *refs):
    arrived = refs[: sources - 1]
    turned_refs = refs[sources - 1 : 3 * (sources - 1)]
    wide_ref, polar_ref, partial_ref, out = refs[3 * (sources - 1) :]
    blocks = wide_ref.shape[0]
    azimuth = turned_refs[0].shape[1]
    size = 2 * groups
    coarse = []
    for place, field in enumerate(arrived):
        fields = unpacked_fields(field, size, azimuth // field.shape[0])
        coarse.append(coarse_columns(fields, turned_refs[2 * place], turned_refs[2 * place + 1], wide_ref))
    rows = len(fields)
    wide = sources * own
    row_stride = 2 * blocks
    for octant in range(OCTANTS):
        for row in range(own):
            start = (octant * own + row) * size
            value = partial_ref[start : start + size, :]
            for place in range(sources - 1):
                value += anterpolated(coarse[place], polar_ref, octant, (place + 1) * own + row, rows, size, wide)
            for block in range(blocks):
                for part in range(2):
                    first = (octant * own + row) * row_stride + 2 * block + part
                    out[pl.ds(first, groups, stride=OCTANTS * own * row_stride), :] = value[
                        part * groups : (part + 1) * groups, block * TILE : (block + 1) * TILE
                    ]


def call(kernel, outs, args, flops, name, remote=(), after=(), far=(), scratch=(), into=0):
    held = sum(4 * leaf.size for leaf in outs) + sum(4 * arg.size for arg in (*remote, *args))
    remote = [pltpu.with_memory_space_constraint(arg, pltpu.HBM) for arg in remote]
    scratch = [*scratch, *(pltpu.VMEM(arg.shape, arg.dtype) for arg in remote[: len(remote) - into])]
    if remote:
        scratch.append(pltpu.SemaphoreType.DMA((len(remote),)))
    near, away, free = (pl.BlockSpec(memory_space=space) for space in (pltpu.VMEM, pltpu.HBM, pl.ANY))
    return pl.pallas_call(
        kernel,
        out_shape=outs,
        in_specs=[away] * len(remote) + [near] * len(args) + [free] * len(after),
        out_specs=[free if place in far else near for place in range(len(outs))],
        scratch_shapes=scratch,
        compiler_params=pltpu.CompilerParams(vmem_limit_bytes=max(VMEM_BYTES, 8 * max(arg.size for arg in (*remote, *args)))),
        cost_estimate=pl.CostEstimate(flops=flops, bytes_accessed=held, transcendentals=0),
        name=name,
    )(*remote, *args, *after)


def bind(kernel, *settings):
    return lambda *refs: kernel(*settings, *refs)


def exchange(blocks):
    return lax.all_to_all(blocks, "clus", split_axis=0, concat_axis=0, tiled=True)


def per_device(child_patterns, theta_weights, phi_stencil, phi_weights, shift_phase, translation_table, far_list, far_vector):
    devices, halves = lax.axis_size("clus"), lax.axis_size("samp")
    children, _, own, columns = child_patterns.shape
    groups = children // OCTANTS
    rows, azimuth = theta_weights.shape[0], phi_stencil.shape[0]
    clusters, partners = far_list.shape
    vectors, width = translation_table.shape[0], 2 * translation_table.shape[3]
    blocks, rows_all = columns // TILE, groups * rows
    long = children * own
    sources = 2 if halves == 2 else 3
    struct = jax.ShapeDtypeStruct
    forward = [(i, (i + 1) % halves) for i in range(halves)]
    backward = [((i + 1) % halves, i) for i in range(halves)]

    field = child_patterns.reshape(children, 2, own, blocks, TILE).transpose(0, 2, 3, 1, 4).reshape(long * blocks * 2, TILE)
    neighbours = [lax.ppermute(field, "samp", forward)]
    if sources == 3:
        neighbours.append(lax.ppermute(field, "samp", backward))
    phase = shift_phase.transpose(1, 0, 2).reshape(rows * OCTANTS, azimuth)
    ways = [backward] if sources == 2 else [backward, forward]
    phases = [lax.ppermute(phase, "samp", way) for way in ways]
    table = translation_table.transpose(0, 2, 1, 3).reshape(vectors * rows * 2, width // 2)
    turn = struct((rows * OCTANTS, azimuth), F32)

    cosine, sine, wide, polar, held = call(
        bind(prepare_kernel, sources, own),
        [
            turn,
            turn,
            struct((blocks, 2 * KEPT, PAIR), BF16),
            struct((rows * sources * own, TILE), F32),
            struct(field.shape, F32),
        ],
        [],
        400_000_000,
        "prepare",
        [theta_weights, phase, phi_stencil.T, phi_weights.T, field],
        into=1,
    )
    (outgoing,) = call(
        bind(aggregate_kernel, groups, sources, own, devices),
        [struct((devices, rows_all, width), F32)],
        [held, *neighbours, cosine, sine, wide, polar],
        1_500_000_000,
        "aggregate",
        scratch=[pltpu.VMEM((2 * groups * OCTANTS * rows, columns), BF16)] * 2,
    )
    arrived = exchange(outgoing)
    hot, factors, *turned_parts = call(
        bind(tables_kernel, sources, rows),
        [
            struct((partners * clusters, 2 * clusters), BF16),
            struct((partners * clusters, rows * width), F32),
        ]
        + [turn] * (2 * sources - 2),
        phases,
        600_000_000,
        "tables",
        [far_list.T, far_vector.T, table],
        [outgoing],
    )
    (translated,) = call(
        bind(translate_kernel, groups),
        [struct((devices, rows_all, width), F32)],
        [hot, factors, arrived],
        600_000_000,
        "translate",
    )
    returned = exchange(translated)
    size = rows_all * 2 * azimuth // TILE
    parent, partial = call(
        bind(lower_kernel, groups, own),
        [struct((size, TILE), F32), struct((2 * long, columns), F32)],
        [returned, cosine, sine, wide, polar],
        1_500_000_000,
        "lower",
        far=(0,),
        scratch=[pltpu.VMEM((size, TILE), F32), pltpu.SemaphoreType.DMA],
    )
    returned_parts = [lax.ppermute(returned, "samp", way) for way in ways]
    (total,) = call(
        bind(finish_kernel, groups, sources, own),
        [struct((long * blocks * 2, TILE), F32)],
        [*returned_parts, *turned_parts, wide, polar, partial],
        1_500_000_000,
        "finish",
    )
    child_incoming = total.reshape(children, own, blocks, 2, TILE).transpose(0, 3, 1, 2, 4).reshape(children, 2, own, columns)
    parent_incoming = (
        parent.reshape(groups, rows, azimuth // TILE, 2, TILE).transpose(0, 3, 1, 2, 4).reshape(groups, 2, rows, azimuth)
    )
    return (parent_incoming, child_incoming)


def solution(mesh):
    placed = (
        P("clus", None, "samp", None),
        P(),
        P(),
        P(),
        P(None, "samp", None),
        P(None, None, "samp", "clus"),
        P(),
        P(),
    )
    return jax.shard_map(
        per_device,
        mesh=mesh,
        in_specs=placed,
        out_specs=(P("clus", None, "samp", None), P("clus", None, "samp", None)),
        check_vma=False,
    )
```

```python
import jax
import jax.numpy as jnp
from jax import lax
from jax.experimental import pallas as pl
from jax.experimental.pallas import tpu as pltpu
from jax.sharding import PartitionSpec as P

P_SIZE = 6
OCTANTS = 8
TILE = 128
PAIR = 2 * TILE
HALF = TILE // 2
VMEM_BYTES = 4 * 1024 * 1024
F32 = jnp.float32
BF16 = jnp.bfloat16

RIM = 16
KEPT = TILE + 2 * RIM

SIN_TERMS = (-1 / 6, 1 / 120, -1 / 5040, 1 / 362880, -1 / 39916800, 1 / 6227020800)
COS_TERMS = (-1 / 2, 1 / 24, -1 / 720, 1 / 40320, -1 / 3628800, 1 / 479001600, -1 / 87178291200)


def split_two(value):
    high = value.astype(BF16)
    return high, (value - high.astype(F32)).astype(BF16)


def split_three(value):
    high = value.astype(BF16)
    rest = value - high.astype(F32)
    middle = rest.astype(BF16)
    return high, middle, (rest - middle.astype(F32)).astype(BF16)


def product(left, right, left_dim=1, right_dim=0):
    return lax.dot_general(left, right, (((left_dim,), (right_dim,)), ((), ())), preferred_element_type=F32)


def series(square, terms):
    total = jnp.full_like(square, terms[-1])
    for term in terms[-2::-1]:
        total = total * square + term
    return total


def iota(shape, dim):
    return lax.broadcasted_iota(jnp.int32, shape, dim)


def one_hot(flags):
    return flags.astype(F32).astype(BF16)


def turned(block):
    return jnp.roll(block, HALF, axis=1)


def folded(theta, sources, own):
    below, middle, above = theta[:, :own], theta[:, own : 2 * own], theta[:, 2 * own :]
    return jnp.concatenate((middle, below + above) if sources == 2 else (middle, below, above), axis=1)


def turns(phase):
    half = 0.5 * phase
    square = half * half
    sine = half + half * square * series(square, SIN_TERMS)
    cosine = 1.0 + square * series(square, COS_TERMS)
    return 1.0 - 2.0 * sine * sine, 2.0 * sine * cosine


def started(remote, local, sems):
    copies = [pltpu.make_async_copy(source, target, sems.at[place]) for place, (source, target) in enumerate(zip(remote, local))]
    for copy in copies:
        copy.start()
    return copies


def prepare_kernel(sources, own, *refs):
    count = 5
    remote, outs, rest = refs[:count], refs[count : count + 5], refs[count + 5 :]
    cos_ref, sin_ref, wide_ref, polar_ref, field_out = outs
    theta_ref, phase_ref, stencil_ref, weight_ref, sems = rest
    copies = started(remote, [theta_ref, phase_ref, stencil_ref, weight_ref, field_out], sems)
    rows = theta_ref.shape[0]
    blocks = wide_ref.shape[0]

    wide = sources * own
    at_row = one_hot(iota((rows * wide, rows), 0) // wide == iota((rows * wide, rows), 1))
    keep = iota((rows * wide, wide), 0) % wide == iota((rows * wide, wide), 1)
    ones = jnp.ones((wide, TILE), BF16)
    copies[0].wait()
    parts = [
        product(jnp.where(keep, product(at_row, part), 0.0).astype(BF16), ones)
        for part in split_three(folded(theta_ref[...], sources, own))
    ]
    polar_ref[...] = parts[0] + (parts[1] + parts[2])

    copies[1].wait()
    cos_ref[...], sin_ref[...] = turns(phase_ref[...])

    copies[2].wait()
    copies[3].wait()
    for block in range(blocks):
        columns = slice(block * PAIR, (block + 1) * PAIR)
        after, before = (block + 1) % blocks, (block - 1) % blocks
        pieces = (
            (0, TILE, block * TILE),
            (TILE, RIM, after * TILE),
            (TILE + RIM, RIM, before * TILE + TILE - RIM),
        )
        for start, size, first in pieces:
            child = iota((size, PAIR), 0) + first
            total = jnp.zeros((size, PAIR), F32)
            for point in range(P_SIZE):
                hit = stencil_ref[point : point + 1, columns] == child
                total = jnp.where(hit, weight_ref[point : point + 1, columns], total)
            high, low = split_two(total)
            wide_ref[block, start : start + size, :] = high
            wide_ref[block, KEPT + start : KEPT + start + size, :] = low
    copies[4].wait()


def azimuthal(wide_ref, block, axis):
    empty = jnp.zeros((TILE - 2 * RIM, PAIR), BF16)
    halves = []
    for start in (0, KEPT):
        kept = (wide_ref[block, start : start + TILE + RIM], empty, wide_ref[block, start + TILE + RIM : start + KEPT])
        halves.append(jnp.concatenate(kept, axis=0))
    return jnp.concatenate([halves[0], halves[0], halves[1]], axis=axis)


def polar_splat(polar_ref, row, width):
    return jnp.concatenate([polar_ref[row : row + 1, :]] * (width // TILE), axis=1)


def aggregate_kernel(groups, sources, own, devices, *refs):
    fields = refs[:sources]
    cos_ref, sin_ref, wide_ref, polar_ref = refs[sources : sources + 4]
    out, high_s, low_s = refs[-3:]
    blocks = wide_ref.shape[0]
    rows = cos_ref.shape[0] // OCTANTS
    columns = cos_ref.shape[1] // devices
    size = 2 * groups
    wide = sources * own
    row_stride = 2 * blocks
    child_stride = OCTANTS * own * row_stride

    for octant in range(OCTANTS):
        given = []
        for field in fields:
            for row in range(own):
                start = (octant * own + row) * row_stride
                given.append(
                    jnp.concatenate(
                        [
                            jnp.concatenate(
                                [field[pl.ds(start + 2 * block + part, groups, stride=child_stride), :] for part in range(2)],
                                axis=0,
                            )
                            for block in range(blocks)
                        ],
                        axis=1,
                    )
                )
        for first in range(0, rows, 2):
            pair = []
            for row in (first, first + 1):
                total = given[0] * polar_splat(polar_ref, row * wide, blocks * TILE)
                for place in range(1, wide):
                    total += given[place] * polar_splat(polar_ref, row * wide + place, blocks * TILE)
                pair.append(total)
            high, low = split_two(jnp.concatenate(pair, axis=0))
            target = slice((octant * rows + first) * size, (octant * rows + first + 2) * size)
            high_s[target, :] = high
            low_s[target, :] = low

    lane = iota((OCTANTS * rows * size, TILE), 1)

    def windows(value, block):
        main = value[:, block * TILE : (block + 1) * TILE]
        after, before = (block + 1) % blocks, (block - 1) % blocks
        rim = jnp.where(lane < HALF, value[:, after * TILE : (after + 1) * TILE], value[:, before * TILE : (before + 1) * TILE])
        return [main, rim]

    for block in range(blocks):
        one, two = windows(high_s, block), windows(low_s, block)
        left = jnp.concatenate(one + two + one, axis=1)
        spread = product(left, azimuthal(wide_ref, block, 0))
        part = slice(block * PAIR, (block + 1) * PAIR)
        summed = []
        for row in range(rows):
            direct = jnp.zeros((size, PAIR), F32)
            crossed = jnp.zeros((size, PAIR), F32)
            for octant in range(OCTANTS):
                start = (octant * rows + row) * size
                turn = slice(row * OCTANTS + octant, row * OCTANTS + octant + 1)
                direct += spread[start : start + size] * cos_ref[turn, part]
                crossed += spread[start : start + size] * sin_ref[turn, part]
            summed.append(direct + jnp.concatenate([-crossed[groups:], crossed[:groups]], axis=0))
        for first in range(0, rows, 2):
            target = slice(first // 2 * size, (first // 2 + 1) * size)
            for place, piece in enumerate(packed_pieces(summed[first], summed[first + 1], columns)):
                out[block * PAIR // columns + place, target, :] = piece


def packed_pieces(one, two, columns):
    found = []
    if columns == HALF:
        lane = iota((one.shape[0], TILE), 1)
        for start in range(0, one.shape[1], TILE):
            a, b = one[:, start : start + TILE], two[:, start : start + TILE]
            found.append(jnp.where(lane < HALF, a, turned(b)))
            found.append(jnp.where(lane < HALF, turned(a), b))
        return found
    for start in range(0, one.shape[1], columns):
        found.append(jnp.concatenate([one[:, start : start + columns], two[:, start : start + columns]], axis=1))
    return found


def unpacked_pieces(blocks, columns):
    if columns == HALF:
        one, two = [], []
        for a, b in zip(blocks[::2], blocks[1::2]):
            lane = iota(a.shape, 1)
            one.append(jnp.where(lane < HALF, a, turned(b)))
            two.append(jnp.where(lane < HALF, turned(a), b))
        return [jnp.concatenate(one, axis=1), jnp.concatenate(two, axis=1)]
    return [
        jnp.concatenate([block[:, :columns] for block in blocks], axis=1),
        jnp.concatenate([block[:, columns:] for block in blocks], axis=1),
    ]


def tables_kernel(sources, rows, *refs):
    count = 3
    remote, phases = refs[:count], refs[count : count + sources - 1]
    outs = refs[count + sources : -count - 1]
    local, sems = refs[-count - 1 : -1], refs[-1]
    listed_ref, vector_ref, table_ref = local
    hot_ref, factors_ref, *turned_refs = outs
    copies = started(remote, local, sems)
    for place, phase in enumerate(phases):
        turned_refs[2 * place][...], turned_refs[2 * place + 1][...] = turns(phase[...])

    copies[2].wait()
    raw = table_ref[...]
    many, width = raw.shape
    vectors = many // (2 * rows)
    at, place = iota((many, many), 1), iota((many, many), 0)
    order = one_hot(at == place % vectors * (2 * rows) + place // (2 * vectors) * 2 + place // vectors % 2)
    twice = one_hot(iota((width, 2 * width), 1) % width == iota((width, 2 * width), 0))
    lane = iota((vectors, 2 * width), 1)
    pieces = []
    for part in split_three(raw):
        double = product(product(order, part).astype(BF16), twice)
        pairs = []
        for kind in range(2):
            for first in range(0, rows, 2):
                one, two = (double[(2 * row + kind) * vectors : (2 * row + kind + 1) * vectors] for row in (first, first + 1))
                pairs.append(jnp.where(lane < width, one, two).astype(BF16))
        pieces.append(jnp.concatenate(pairs, axis=1))
    spread = jnp.concatenate(pieces, axis=0)

    copies[0].wait()
    copies[1].wait()
    partners, clusters = listed_ref.shape
    unit = one_hot(iota((clusters, clusters), 0) == iota((clusters, clusters), 1))
    listed = sum(product(unit, half, 1, 1) for half in split_two(listed_ref[...].astype(F32)))
    chosen = sum(product(unit, half, 1, 1) for half in split_two(vector_ref[...].astype(F32)))
    cluster = (iota((clusters, 2 * clusters), 1) % clusters).astype(F32)
    vector = (iota((clusters, 3 * vectors), 1) % vectors).astype(F32)
    picked = []
    for partner in range(partners):
        part = slice(partner * clusters, (partner + 1) * clusters)
        hot_ref[part, :] = one_hot(cluster == listed[:, partner : partner + 1])
        picked.append(one_hot(vector == chosen[:, partner : partner + 1]))
    factors_ref[...] = product(jnp.concatenate(picked, axis=0), spread)


def translate_kernel(groups, hot_ref, factors_ref, arrived_ref, out):
    devices, tall, width = arrived_ref.shape
    clusters = devices * groups
    partners = hot_ref.shape[0] // clusters
    size = 2 * groups
    steps = tall // size
    starts = [step * size + part * groups for part in range(2) for step in range(steps)]
    source = jnp.concatenate(
        [arrived_ref[:, start : start + groups, :].reshape(clusters, width) for start in starts], axis=1
    )
    gathered = product(hot_ref[...], jnp.concatenate(split_two(source), axis=0))
    for step in range(steps):
        lanes = slice(step * width, (step + 1) * width)
        other = slice((steps + step) * width, (steps + step + 1) * width)
        real = jnp.zeros((clusters, width), F32)
        imag = jnp.zeros((clusters, width), F32)
        for partner in range(partners):
            part = slice(partner * clusters, (partner + 1) * clusters)
            a, b = gathered[part, lanes], gathered[part, other]
            c, d = factors_ref[part, lanes], factors_ref[part, other]
            real += a * c - b * d
            imag += a * d + b * c
        for device in range(devices):
            rows = slice(device * groups, (device + 1) * groups)
            out[device, step * size : (step + 1) * size, :] = jnp.concatenate([real[rows], imag[rows]], axis=0)


def unpacked_fields(arrived_ref, size, columns):
    fields = []
    for start in range(0, arrived_ref.shape[1], size):
        fields += unpacked_pieces([arrived_ref[device, start : start + size, :] for device in range(arrived_ref.shape[0])], columns)
    return fields


def coarse_columns(fields, cos_ref, sin_ref, wide_ref):
    blocks = wide_ref.shape[0]
    rows, size = len(fields), fields[0].shape[0]
    groups = size // 2
    crossed = [jnp.concatenate([field[groups:], -field[:groups]], axis=0) for field in fields]
    mains, rims = [], []
    for block in range(blocks):
        part = slice(block * PAIR, (block + 1) * PAIR)
        lowered = []
        for octant in range(OCTANTS):
            for row in range(rows):
                turn = slice(row * OCTANTS + octant, row * OCTANTS + octant + 1)
                lowered.append(fields[row][:, part] * cos_ref[turn, part] + crossed[row][:, part] * sin_ref[turn, part])
        high, low = split_two(jnp.concatenate(lowered, axis=0))
        left = jnp.concatenate([high, low, high], axis=1)
        both = product(left, azimuthal(wide_ref, block, 1), 1, 1)
        mains.append(both[:, :TILE])
        rims.append(both[:, TILE:])
    lane = iota((OCTANTS * rows * size, TILE), 1)
    return jnp.concatenate(
        [
            mains[block] + jnp.where(lane < HALF, rims[(block - 1) % blocks], rims[(block + 1) % blocks])
            for block in range(blocks)
        ],
        axis=1,
    )


def anterpolated(coarse, polar_ref, octant, place, rows, size, wide):
    total = None
    for row in range(rows):
        start = (octant * rows + row) * size
        term = coarse[start : start + size] * polar_splat(polar_ref, row * wide + place, coarse.shape[1])
        total = term if total is None else total + term
    return total


def lower_kernel(groups, own, arrived_ref, cos_ref, sin_ref, wide_ref, polar_ref, parent_out, partial_ref, parent_ref, sem):
    devices = arrived_ref.shape[0]
    azimuth = cos_ref.shape[1]
    size = 2 * groups
    fields = unpacked_fields(arrived_ref, size, azimuth // devices)
    rows = len(fields)
    wide = polar_ref.shape[0] // rows
    tiles = azimuth // TILE
    for row, field in enumerate(fields):
        for tile in range(tiles):
            for part in range(2):
                start = (row * tiles + tile) * 2 + part
                parent_ref[pl.ds(start, groups, stride=rows * tiles * 2), :] = field[
                    part * groups : (part + 1) * groups, tile * TILE : (tile + 1) * TILE
                ]
    copy = pltpu.make_async_copy(parent_ref, parent_out, sem)
    copy.start()
    coarse = coarse_columns(fields, cos_ref, sin_ref, wide_ref)
    for octant in range(OCTANTS):
        for row in range(own):
            start = (octant * own + row) * size
            partial_ref[start : start + size, :] = anterpolated(coarse, polar_ref, octant, row, rows, size, wide)
    copy.wait()


def finish_kernel(groups, sources, own, *refs):
    arrived = refs[: sources - 1]
    turned_refs = refs[sources - 1 : 3 * (sources - 1)]
    wide_ref, polar_ref, partial_ref, out = refs[3 * (sources - 1) :]
    blocks = wide_ref.shape[0]
    azimuth = turned_refs[0].shape[1]
    size = 2 * groups
    coarse = []
    for place, field in enumerate(arrived):
        fields = unpacked_fields(field, size, azimuth // field.shape[0])
        coarse.append(coarse_columns(fields, turned_refs[2 * place], turned_refs[2 * place + 1], wide_ref))
    rows = len(fields)
    wide = sources * own
    row_stride = 2 * blocks
    for octant in range(OCTANTS):
        for row in range(own):
            start = (octant * own + row) * size
            value = partial_ref[start : start + size, :]
            for place in range(sources - 1):
                value += anterpolated(coarse[place], polar_ref, octant, (place + 1) * own + row, rows, size, wide)
            for block in range(blocks):
                for part in range(2):
                    first = (octant * own + row) * row_stride + 2 * block + part
                    out[pl.ds(first, groups, stride=OCTANTS * own * row_stride), :] = value[
                        part * groups : (part + 1) * groups, block * TILE : (block + 1) * TILE
                    ]


def call(kernel, outs, args, flops, name, remote=(), after=(), far=(), scratch=(), into=0):
    held = sum(4 * leaf.size for leaf in outs) + sum(4 * arg.size for arg in (*remote, *args))
    remote = [pltpu.with_memory_space_constraint(arg, pltpu.HBM) for arg in remote]
    scratch = [*scratch, *(pltpu.VMEM(arg.shape, arg.dtype) for arg in remote[: len(remote) - into])]
    if remote:
        scratch.append(pltpu.SemaphoreType.DMA((len(remote),)))
    near, away, free = (pl.BlockSpec(memory_space=space) for space in (pltpu.VMEM, pltpu.HBM, pl.ANY))
    return pl.pallas_call(
        kernel,
        out_shape=outs,
        in_specs=[away] * len(remote) + [near] * len(args) + [free] * len(after),
        out_specs=[free if place in far else near for place in range(len(outs))],
        scratch_shapes=scratch,
        compiler_params=pltpu.CompilerParams(vmem_limit_bytes=max(VMEM_BYTES, 6 * max(arg.size for arg in (*remote, *args)))),
        cost_estimate=pl.CostEstimate(flops=flops, bytes_accessed=held, transcendentals=0),
        name=name,
    )(*remote, *args, *after)


def bind(kernel, *settings):
    return lambda *refs: kernel(*settings, *refs)


def exchange(blocks):
    return lax.all_to_all(blocks, "clus", split_axis=0, concat_axis=0, tiled=True)


def per_device(child_patterns, theta_weights, phi_stencil, phi_weights, shift_phase, translation_table, far_list, far_vector):
    devices, halves = lax.axis_size("clus"), lax.axis_size("samp")
    children, _, own, columns = child_patterns.shape
    groups = children // OCTANTS
    rows, azimuth = theta_weights.shape[0], phi_stencil.shape[0]
    clusters, partners = far_list.shape
    vectors, width = translation_table.shape[0], 2 * translation_table.shape[3]
    blocks, rows_all = columns // TILE, groups * rows
    long = children * own
    sources = 2 if halves == 2 else 3
    struct = jax.ShapeDtypeStruct
    forward = [(i, (i + 1) % halves) for i in range(halves)]
    backward = [((i + 1) % halves, i) for i in range(halves)]

    field = child_patterns.reshape(children, 2, own, blocks, TILE).transpose(0, 2, 3, 1, 4).reshape(long * blocks * 2, TILE)
    neighbours = [lax.ppermute(field, "samp", forward)]
    if sources == 3:
        neighbours.append(lax.ppermute(field, "samp", backward))
    phase = shift_phase.transpose(1, 0, 2).reshape(rows * OCTANTS, azimuth)
    ways = [backward] if sources == 2 else [backward, forward]
    phases = [lax.ppermute(phase, "samp", way) for way in ways]
    table = translation_table.transpose(0, 2, 1, 3).reshape(vectors * rows * 2, width // 2)
    turn = struct((rows * OCTANTS, azimuth), F32)

    cosine, sine, wide, polar, held = call(
        bind(prepare_kernel, sources, own),
        [
            turn,
            turn,
            struct((blocks, 2 * KEPT, PAIR), BF16),
            struct((rows * sources * own, TILE), F32),
            struct(field.shape, F32),
        ],
        [],
        400_000_000,
        "prepare",
        [theta_weights, phase, phi_stencil.T, phi_weights.T, field],
        into=1,
    )
    (outgoing,) = call(
        bind(aggregate_kernel, groups, sources, own, devices),
        [struct((devices, rows_all, width), F32)],
        [held, *neighbours, cosine, sine, wide, polar],
        1_500_000_000,
        "aggregate",
        scratch=[pltpu.VMEM((2 * groups * OCTANTS * rows, columns), BF16)] * 2,
    )
    arrived = exchange(outgoing)
    hot, factors, *turned_parts = call(
        bind(tables_kernel, sources, rows),
        [
            struct((partners * clusters, 2 * clusters), BF16),
            struct((partners * clusters, rows * width), F32),
        ]
        + [turn] * (2 * sources - 2),
        phases,
        600_000_000,
        "tables",
        [far_list.T, far_vector.T, table],
        [outgoing],
    )
    (translated,) = call(
        bind(translate_kernel, groups),
        [struct((devices, rows_all, width), F32)],
        [hot, factors, arrived],
        600_000_000,
        "translate",
    )
    returned = exchange(translated)
    size = rows_all * 2 * azimuth // TILE
    parent, partial = call(
        bind(lower_kernel, groups, own),
        [struct((size, TILE), F32), struct((2 * long, columns), F32)],
        [returned, cosine, sine, wide, polar],
        1_500_000_000,
        "lower",
        far=(0,),
        scratch=[pltpu.VMEM((size, TILE), F32), pltpu.SemaphoreType.DMA],
    )
    returned_parts = [lax.ppermute(returned, "samp", way) for way in ways]
    (total,) = call(
        bind(finish_kernel, groups, sources, own),
        [struct((long * blocks * 2, TILE), F32)],
        [*returned_parts, *turned_parts, wide, polar, partial],
        1_500_000_000,
        "finish",
    )
    child_incoming = total.reshape(children, own, blocks, 2, TILE).transpose(0, 3, 1, 2, 4).reshape(children, 2, own, columns)
    parent_incoming = (
        parent.reshape(groups, rows, azimuth // TILE, 2, TILE).transpose(0, 3, 1, 2, 4).reshape(groups, 2, rows, azimuth)
    )
    return (parent_incoming, child_incoming)


def solution(mesh):
    placed = (
        P("clus", None, "samp", None),
        P(),
        P(),
        P(),
        P(None, "samp", None),
        P(None, None, "samp", "clus"),
        P(),
        P(),
    )
    return jax.shard_map(
        per_device,
        mesh=mesh,
        in_specs=placed,
        out_specs=(P("clus", None, "samp", None), P("clus", None, "samp", None)),
        check_vma=False,
    )
```
